128 devices in a mesh: batch: 2 (over x_hi), blk: 16 (over x_lo, z, core), ulysses: 4 (over y).
Axes of the slice: x: 4 (x_hi: 2, x_lo: 2; x = x_hi * 2 + x_lo), y: 4, z: 4, core: 2. Of those that a mesh axis runs over, the one named last changes fastest.
Arguments:
- tokens: bfloat16 [16384, 768], P(('batch', 'blk', 'ulysses')), may hold values from -6 to 6
- stretch_order: int32 [2, 32], P('batch'), may hold values from 0 to 31, each once within a row
- ln_gain: bfloat16 [1, 1536], P(None, ('batch', 'blk', 'ulysses')), may hold values from 0.5 to 1.5
- ln_bias: bfloat16 [1, 1536], P(None, ('batch', 'blk', 'ulysses')), may hold values from -3 to 3
- w_qkv: bfloat16 [1, 768, 2304], P(None, ('batch', 'blk', 'ulysses')), may hold values from -0.21875 to 0.21875
- qv_bias: bfloat16 [1, 1536], P(None, ('batch', 'blk', 'ulysses')), may hold values from -4 to 4
- w_out: bfloat16 [1, 768, 768], P(None, ('batch', 'blk', 'ulysses')), may hold values from -0.875 to 0.875
- out_bias: bfloat16 [1, 768], P(None, ('batch', 'blk', 'ulysses')), may hold values from -3 to 3
- w_up: bfloat16 [1, 768, 3072], P(None, ('batch', 'blk', 'ulysses')), may hold values from -0.21875 to 0.21875
- up_bias: bfloat16 [1, 3072], P(None, ('batch', 'blk', 'ulysses')), may hold values from -4 to 4
- w_down: bfloat16 [1, 3072, 768], P(None, ('batch', 'blk', 'ulysses')), may hold values from -0.21875 to 0.21875
- down_bias: bfloat16 [1, 768], P(None, ('batch', 'blk', 'ulysses')), may hold values from -3 to 3
- cotangent: float32 [16384, 768], P(('batch', 'blk', 'ulysses')), may hold values from -6 to 6
Outputs:
- result: float32 [16384, 768], P(('batch', 'blk', 'ulysses'))
- d_tokens: float32 [16384, 768], P(('batch', 'blk', 'ulysses'))
- g_ln_gain: float32 [1, 1536], P(None, ('batch', 'blk', 'ulysses'))
- g_ln_bias: float32 [1, 1536], P(None, ('batch', 'blk', 'ulysses'))
- g_w_qkv: float32 [1, 768, 2304], P(None, ('batch', 'blk', 'ulysses'))
- g_qv_bias: float32 [1, 1536], P(None, ('batch', 'blk', 'ulysses'))
- g_w_out: float32 [1, 768, 768], P(None, ('batch', 'blk', 'ulysses'))
- g_out_bias: float32 [1, 768], P(None, ('batch', 'blk', 'ulysses'))
- g_w_up: float32 [1, 768, 3072], P(None, ('batch', 'blk', 'ulysses'))
- g_up_bias: float32 [1, 3072], P(None, ('batch', 'blk', 'ulysses'))
- g_w_down: float32 [1, 3072, 768], P(None, ('batch', 'blk', 'ulysses'))
- g_down_bias: float32 [1, 768], P(None, ('batch', 'blk', 'ulysses'))
The draws below stay inside these ranges and needn't reach their ends.
Inputs may be any that keep to these rules, and one draw needn't show every extreme that they name: Each row of stretch_order is a permutation of the 32 stretches of 256 positions; stored rows 2 j * 256 to 2 (j + 1) * 256 - 1 of a sequence hold the stretches named at entries 2 j and 2 j + 1, in that order.
All inputs are finite; a program needn't handle non-finite values.
Results may differ from the reference program's by a relative error of at most 0.038.
Values may be sent and summed in bfloat16 or wider, within the bound.
No kernel may reach another device: no remote copies, remote signals or barrier semaphores. Data moves between devices by JAX's collectives and lax.ppermute only.
A program may use at most 256 MiB of HBM per device.

```python
import math
import jax
import jax.numpy as jnp
from jax import lax

D = 768
HEADS = 12
FF = 3072
HEAD_DIM = 64
LAYERS = 1
GROUP = 512
STRETCH = 256
STRETCHES = 32
SEQ_LEN = 8192
SEQS = 2
TOKENS = 16384


def level_of(key, dims, cuts, low, top_value):
    gain = 1.0
    for dim, shards_of in cuts:
        heights = jax.random.uniform(jax.random.fold_in(jax.random.fold_in(key, 6), dim), (shards_of,), jnp.float32, low / len(cuts), top_value / len(cuts))
        gain = gain * jnp.repeat(jnp.exp(heights), dims[dim] // shards_of).reshape((-1,) + (1,) * (len(dims) - 1 - dim))
    return gain


def normal_values(own_key, shape, width, most, cuts=(), held_as=jnp.bfloat16):
    entries = jax.random.normal(own_key, shape, jnp.float32) * width
    if len(cuts) > 0:
        entries = level_of(own_key, shape, cuts, -0.22, 0.18) * entries
    return jnp.clip(entries, min=-most, max=most).astype(held_as)


def setup_inputs(seed: int = 0) -> dict:
    arg_keys = jax.random.split(jax.random.key(seed), 14)
    tokens = normal_values(arg_keys[0], (TOKENS, D), 1.0, 6.0, ((0, 128),))
    stretch_order = jax.vmap(lambda own: jax.random.permutation(own, STRETCHES))(jax.random.split(arg_keys[1], SEQS)).reshape((SEQS, STRETCHES)).astype(jnp.int32)
    ln_gain = jnp.clip(1.0 + 0.1 * jax.random.normal(arg_keys[2], (LAYERS, 2 * D), jnp.float32), 0.5, 1.5).astype(jnp.bfloat16)
    ln_bias = normal_values(arg_keys[3], (LAYERS, 2 * D), 0.3, 3.0, ((1, 128),))
    w_qkv = normal_values(arg_keys[4], (LAYERS, D, 3 * D), D ** -0.5, 0.21875, ((1, 128),))
    qv_bias = normal_values(arg_keys[5], (LAYERS, 2 * D), 0.5, 4.0, ((1, 128),))
    w_out = normal_values(arg_keys[6], (LAYERS, D, D), (D // 16) ** -0.5, 0.875, ((1, 128),))
    out_bias = normal_values(arg_keys[7], (LAYERS, D), 0.3, 3.0, ((1, 128),))
    w_up = normal_values(arg_keys[8], (LAYERS, D, FF), D ** -0.5, 0.21875, ((1, 128),))
    up_bias = normal_values(arg_keys[9], (LAYERS, FF), 0.5, 4.0, ((1, 128),))
    w_down = normal_values(arg_keys[10], (LAYERS, FF, D), (FF // 4) ** -0.5, 0.21875, ((1, 128),))
    down_bias = normal_values(arg_keys[11], (LAYERS, D), 0.3, 3.0, ((1, 128),))
    cotangent = normal_values(arg_keys[12], (TOKENS, D), 1.0, 6.0, ((0, 128),), jnp.float32)
    return dict(tokens=tokens, stretch_order=stretch_order, ln_gain=ln_gain, ln_bias=ln_bias, w_qkv=w_qkv, qv_bias=qv_bias, w_out=w_out, out_bias=out_bias, w_up=w_up, up_bias=up_bias, w_down=w_down, down_bias=down_bias, cotangent=cotangent)


NORM_EPS = 1e-05
MASKED_SCORE = -1e+30
HIGHEST = lax.Precision.HIGHEST

@jax.custom_vjp
def low(v):
    return lax.optimization_barrier(v.astype(jnp.bfloat16)).astype(jnp.float32)

@jax.custom_vjp
def low_back(v):
    return v

def low_keep(v):
    return (low(v), None)

def low_pass(kept, grad):
    return (grad,)

def back_keep(v):
    return (v, None)

def back_low(kept, grad):
    return (low(grad),)
low.defvjp(low_keep, low_pass)
low_back.defvjp(back_keep, back_low)

def norm_rows(values, norm_gain, norm_shift):
    row_mean = lax.optimization_barrier(jnp.mean(values, axis=-1, keepdims=True))
    centered = values - row_mean
    spread = lax.optimization_barrier(jnp.mean(centered * centered, axis=-1, keepdims=True))
    return centered * lax.rsqrt(spread + NORM_EPS) * norm_gain + norm_shift

def product(left, right):
    return jnp.dot(left, right, precision=HIGHEST)

def attend_block(queries, query_pos, keys_all, values_all, key_pos):
    score_scale = 1.0 / math.sqrt(HEAD_DIM)
    logits = low_back(jnp.einsum('qhd,khd->hqk', queries, keys_all, precision=HIGHEST) * score_scale)
    allowed = key_pos[None, None, :] <= query_pos[None, :, None]
    masked = jnp.where(allowed, logits, MASKED_SCORE)
    row_max = lax.optimization_barrier(jnp.max(masked, axis=-1, keepdims=True))
    weights = jnp.where(allowed, jnp.exp(masked - row_max), 0.0)
    attn_probs = weights / lax.optimization_barrier(jnp.sum(weights, axis=-1, keepdims=True))
    return jnp.einsum('hqk,khd->qhd', low(attn_probs), values_all, precision=HIGHEST)

def attend_sequence(seq_pack):
    queries, keys_all, values_all, positions = seq_pack
    block_count = SEQ_LEN // GROUP
    step_fn = jax.checkpoint(attend_block)
    blocks = lax.map(lambda block_pair: step_fn(block_pair[0], block_pair[1], keys_all, values_all, positions), (queries.reshape(block_count, GROUP, HEADS, HEAD_DIM), positions.reshape(block_count, GROUP)))
    return blocks.reshape(SEQ_LEN, HEADS * HEAD_DIM)

def layer_forward(residual, layer_params, positions):
    norm_gain, norm_shift, w_qkv, qv_bias, w_out, out_bias, w_up, up_bias, w_down, down_bias = layer_params
    normed = low(norm_rows(residual, norm_gain[:D], norm_shift[:D]))
    projected = product(normed, w_qkv)
    queries = low(low_back(projected[:, :D] + qv_bias[:D]))
    keys_all = low(low_back(projected[:, D:2 * D]))
    values_all = low(low_back(projected[:, 2 * D:] + qv_bias[D:]))
    shape_heads = (SEQS, SEQ_LEN, HEADS, HEAD_DIM)
    context = lax.map(attend_sequence, (queries.reshape(shape_heads), keys_all.reshape(shape_heads), values_all.reshape(shape_heads), positions))
    context_low = low(low_back(context.reshape(TOKENS, D)))
    after_attn = residual + low_back(product(context_low, w_out) + out_bias)
    normed_two = low(norm_rows(after_attn, norm_gain[D:], norm_shift[D:]))
    up_pre = low_back(product(normed_two, w_up) + up_bias)
    activated = low(jax.nn.gelu(up_pre, approximate=True))
    return after_attn + low_back(product(activated, w_down) + down_bias)

def reference(tokens, stretch_order, ln_gain, ln_bias, w_qkv, qv_bias, w_out, out_bias, w_up, up_bias, w_down, down_bias, cotangent):
    row_index = jnp.arange(SEQ_LEN, dtype=jnp.int32)
    slot_index = (2 * (row_index // GROUP) + row_index % GROUP // STRETCH).astype(jnp.int32)
    positions = (stretch_order[:, slot_index] * STRETCH + (row_index % STRETCH)[None, :]).astype(jnp.int32)
    params = tuple((array_in.astype(jnp.float32) for array_in in (ln_gain, ln_bias, w_qkv, qv_bias, w_out, out_bias, w_up, up_bias, w_down, down_bias)))

    def forward(inputs, weights):
        residual = inputs
        for layer_index in range(LAYERS):
            residual = layer_forward(residual, tuple((array_in[layer_index] for array_in in weights)), positions)
        return residual
    result, pull = jax.vjp(forward, tokens.astype(jnp.float32), params)
    d_tokens, grads = pull(cotangent)
    g_ln_gain, g_ln_bias, g_w_qkv, g_qv_bias, g_w_out, g_out_bias, g_w_up, g_up_bias, g_w_down, g_down_bias = grads
    return (result, d_tokens, g_ln_gain, g_ln_bias, g_w_qkv, g_qv_bias, g_w_out, g_out_bias, g_w_up, g_up_bias, g_w_down, g_down_bias)
```

```python
import functools
import math

import jax
import jax.numpy as jnp
from jax import lax
from jax.experimental import pallas as pl
from jax.experimental.pallas import tpu as pltpu
from jax.sharding import PartitionSpec as P

HEADS = 12
HEAD_DIM = 64
NORM_EPS = 1e-05
FLOOR = -1e25
BELOW_FLOOR = -1e30
ALL = ("batch", "blk", "ulysses")
WIDE = ("batch", "blk")
BF16 = jnp.bfloat16
F32 = jnp.float32
NT = (((1,), (1,)), ((), ()))
VMEM_LIMIT = 40 * 1024 * 1024


def mm(a, b):
    return jnp.dot(a, b, preferred_element_type=F32)


def mm_nt(a, b):
    return lax.dot_general(a, b, NT, preferred_element_type=F32)


def mm_tn(a, b):
    return lax.dot_general(a, b, (((0,), (0,)), ((), ())), preferred_element_type=F32)


def allowed_tile(key_ranks, query_ranks, half, key_rows, query_cols):
    rows = lax.broadcasted_iota(jnp.int32, (key_rows, 1), 0)
    cols = lax.broadcasted_iota(jnp.int32, (1, query_cols), 1)

    def positions(index, ranks):
        if len(ranks) == 1:
            return ranks[0] * half + index
        return jnp.where(index < half, ranks[0] * half + index, (ranks[1] - 1) * half + index)

    return positions(rows, key_ranks) <= positions(cols, query_ranks)


def attend_kernel(
    ranks, own, qpad, kv, ctx_low, ctx, lse, v_turned, row_max, row_sum, total, *, half, heads
):
    step = pl.program_id(0)
    width = HEAD_DIM

    @pl.when(step == 0)
    def _():
        row_max[...] = jnp.full_like(row_max, FLOOR)
        row_sum[...] = jnp.zeros_like(row_sum)
        total[...] = jnp.zeros_like(total)

    key_ranks = (ranks[2 * step], ranks[2 * step + 1])
    low_rank = jnp.minimum(*key_ranks)
    high_rank = jnp.maximum(*key_ranks)
    v_turned[...] = kv[:, 128:].T

    def tile(part, masked):
        cols = slice(part * half, (part + 1) * half)
        if masked:
            allowed = allowed_tile(key_ranks, (own[part],), half, 2 * half, half)
        for h in range(heads):
            logits = mm_nt(kv[:, :256], qpad[h, cols, :])
            if masked:
                logits = jnp.where(allowed, logits, BELOW_FLOOR)
            old_max = row_max[h : h + 1, cols]
            new_max = jnp.maximum(old_max, jnp.max(logits, axis=0, keepdims=True))
            scale = jnp.exp(old_max - new_max)
            probs = jnp.exp(logits - new_max)
            row_max[h : h + 1, cols] = new_max
            row_sum[h : h + 1, cols] = row_sum[h : h + 1, cols] * scale + jnp.sum(
                probs, axis=0, keepdims=True
            )
            rows = slice(h * width, (h + 1) * width)
            values = v_turned[width * (h + 1) : width * (h + 2), :]
            total[rows, cols] = total[rows, cols] * scale + mm(values, probs.astype(BF16))

    for part in range(2):
        own_rank = own[part]

        @pl.when(high_rank < own_rank)
        def _():
            tile(part, False)

        @pl.when(jnp.logical_and(low_rank <= own_rank, own_rank <= high_rank))
        def _():
            tile(part, True)

    @pl.when(step == pl.num_programs(0) - 1)
    def _():
        for h in range(heads):
            rows = slice(h * width, (h + 1) * width)
            total[rows, :] = total[rows, :] / row_sum[h : h + 1, :]
        done = total[...].T
        ctx[...] = done
        ctx_low[...] = done.astype(BF16)
        lse[...] = row_max[...] + jnp.log(row_sum[...])


def query_grad_kernel(
    ranks, own, qpad, dpad, lse, delta, kv, d_query, k_turned, total, *, half, heads
):
    step = pl.program_id(0)
    width = HEAD_DIM

    @pl.when(step == 0)
    def _():
        total[...] = jnp.zeros_like(total)

    key_ranks = (ranks[2 * step], ranks[2 * step + 1])
    low_rank = jnp.minimum(*key_ranks)
    high_rank = jnp.maximum(*key_ranks)
    k_turned[...] = kv[:, :256].T

    def tile(part, masked):
        cols = slice(part * half, (part + 1) * half)
        if masked:
            allowed = allowed_tile(key_ranks, (own[part],), half, 2 * half, half)
        for h in range(heads):
            probs = jnp.exp(mm_nt(kv[:, :256], qpad[h, cols, :]) - lse[h : h + 1, cols])
            if masked:
                probs = jnp.where(allowed, probs, 0.0)
            d_probs = mm_nt(kv[:, 128:], dpad[h, cols, :])
            d_logits = (probs * (d_probs - delta[h : h + 1, cols])).astype(BF16)
            rows = slice(h * width, (h + 1) * width)
            total[rows, cols] += mm(k_turned[rows, :], d_logits)

    for part in range(2):
        own_rank = own[part]

        @pl.when(high_rank < own_rank)
        def _():
            tile(part, False)

        @pl.when(jnp.logical_and(low_rank <= own_rank, own_rank <= high_rank))
        def _():
            tile(part, True)

    @pl.when(step == pl.num_programs(0) - 1)
    def _():
        d_query[...] = (total[...] * (1.0 / math.sqrt(HEAD_DIM))).T.astype(BF16)


def key_grad_kernel(ranks, own, kpad, vpad, q_all, p_all, d_key, d_value, k_sum, v_sum, *, half, heads):
    step = pl.program_id(0)
    width = HEAD_DIM

    @pl.when(step == 0)
    def _():
        k_sum[...] = jnp.zeros_like(k_sum)
        v_sum[...] = jnp.zeros_like(v_sum)

    query_ranks = (ranks[2 * step], ranks[2 * step + 1])
    low_rank = jnp.minimum(*query_ranks)
    high_rank = jnp.maximum(*query_ranks)

    def tile(part, masked):
        rows = slice(part * half, (part + 1) * half)
        lane = lax.broadcasted_iota(jnp.int32, (2 * half, 256), 1)
        queries = q_all[...]
        packed = p_all[...]
        q_ext = jnp.where(lane < heads * width, queries, packed)
        if masked:
            allowed = allowed_tile((own[part],), query_ranks, half, half, 2 * half)
        k_new = jnp.zeros((half, 256), F32)
        v_new = jnp.zeros((half, 256), F32)
        zero = jnp.zeros_like(queries)
        for h in range(heads):
            here = jnp.logical_and(lane >= h * width, lane < (h + 1) * width)
            probs = jnp.exp(mm_nt(kpad[h, rows, :], q_ext))
            if masked:
                probs = jnp.where(allowed, probs, 0.0)
            d_probs = mm_nt(vpad[h, rows, :], packed)
            d_logits = (probs * d_probs).astype(BF16)
            k_new += mm(d_logits, jnp.where(here, queries, zero))
            v_new += mm(probs.astype(BF16), jnp.where(here, packed, zero))
        k_sum[rows, :] += k_new
        v_sum[rows, :] += v_new

    for part in range(2):
        own_rank = own[part]

        @pl.when(own_rank < low_rank)
        def _():
            tile(part, False)

        @pl.when(jnp.logical_and(low_rank <= own_rank, own_rank <= high_rank))
        def _():
            tile(part, True)

    @pl.when(step == pl.num_programs(0) - 1)
    def _():
        d_key[...] = k_sum[:, : heads * width].astype(BF16)
        d_value[...] = v_sum[:, : heads * width].astype(BF16)


def whole(shape):
    return pl.BlockSpec(shape, lambda i, *_: (0,) * len(shape))


def streamed(rows, cols):
    return pl.BlockSpec((rows, cols), lambda i, *_: (i, 0))


def cost(rows, keys, heads, products):
    area = rows * keys * heads
    return pl.CostEstimate(
        flops=2 * area * 256 * products, bytes_accessed=keys * 768, transcendentals=area
    )


def params():
    return pltpu.CompilerParams(
        dimension_semantics=("arbitrary",), vmem_limit_bytes=VMEM_LIMIT
    )


def attend(ranks, own, qpad, kv):
    heads, rows, _ = qpad.shape
    keys = kv.shape[0]
    width = heads * HEAD_DIM
    return pl.pallas_call(
        functools.partial(attend_kernel, half=rows // 2, heads=heads),
        out_shape=(
            jax.ShapeDtypeStruct((rows, width), BF16),
            jax.ShapeDtypeStruct((rows, width), F32),
            jax.ShapeDtypeStruct((8, rows), F32),
        ),
        grid_spec=pltpu.PrefetchScalarGridSpec(
            num_scalar_prefetch=2,
            grid=(keys // rows,),
            in_specs=[whole(qpad.shape), streamed(rows, kv.shape[1])],
            out_specs=[whole((rows, width)), whole((rows, width)), whole((8, rows))],
            scratch_shapes=[
                pltpu.VMEM((256, rows), BF16),
                pltpu.VMEM((8, rows), F32),
                pltpu.VMEM((8, rows), F32),
                pltpu.VMEM((width, rows), F32),
            ],
        ),
        compiler_params=params(),
        cost_estimate=cost(rows, keys, heads, 2),
        name="attend",
    )(ranks, own, qpad, kv)


def query_grad(ranks, own, qpad, dpad, lse, delta, kv):
    heads, rows, _ = qpad.shape
    keys = kv.shape[0]
    width = heads * HEAD_DIM
    return pl.pallas_call(
        functools.partial(query_grad_kernel, half=rows // 2, heads=heads),
        out_shape=jax.ShapeDtypeStruct((rows, width), BF16),
        grid_spec=pltpu.PrefetchScalarGridSpec(
            num_scalar_prefetch=2,
            grid=(keys // rows,),
            in_specs=[
                whole(qpad.shape),
                whole(dpad.shape),
                whole((8, rows)),
                whole((8, rows)),
                streamed(rows, kv.shape[1]),
            ],
            out_specs=whole((rows, width)),
            scratch_shapes=[pltpu.VMEM((256, rows), BF16), pltpu.VMEM((width, rows), F32)],
        ),
        compiler_params=params(),
        cost_estimate=cost(rows, keys, heads, 3),
        name="query_grad",
    )(ranks, own, qpad, dpad, lse, delta, kv)


def key_grad(ranks, own, kpad, vpad, q_all, p_all):
    heads, rows, _ = kpad.shape
    queries = q_all.shape[0]
    width = heads * HEAD_DIM
    return pl.pallas_call(
        functools.partial(key_grad_kernel, half=rows // 2, heads=heads),
        out_shape=(
            jax.ShapeDtypeStruct((rows, width), BF16),
            jax.ShapeDtypeStruct((rows, width), BF16),
        ),
        grid_spec=pltpu.PrefetchScalarGridSpec(
            num_scalar_prefetch=2,
            grid=(queries // rows,),
            in_specs=[
                whole(kpad.shape),
                whole(vpad.shape),
                streamed(rows, 256),
                streamed(rows, 256),
            ],
            out_specs=[whole((rows, width)), whole((rows, width))],
            scratch_shapes=[pltpu.VMEM((rows, 256), F32), pltpu.VMEM((rows, 256), F32)],
        ),
        compiler_params=params(),
        cost_estimate=cost(rows, queries, heads, 4),
        name="key_grad",
    )(ranks, own, kpad, vpad, q_all, p_all)


def normalized(values):
    mean = jnp.mean(values, axis=-1, keepdims=True)
    centered = values - mean
    spread = jnp.mean(centered * centered, axis=-1, keepdims=True)
    scale = lax.rsqrt(spread + NORM_EPS)
    return centered * scale, scale


def norm_back(grad, gain, normed, scale):
    e = grad * gain
    mean_e = jnp.mean(e, axis=-1, keepdims=True)
    mean_en = jnp.mean(e * normed, axis=-1, keepdims=True)
    return scale * (e - mean_e - normed * mean_en)


def gelu_tanh(values):
    return jax.nn.gelu(values, approximate=True)


def head_lanes(x, heads, first, ones_at=None):
    rows, width = x.shape
    wide = jnp.pad(x, ((0, 0), (first, 256 - width - first)))
    lane = lax.broadcasted_iota(jnp.int32, (heads, 1, 256), 2)
    head = lax.broadcasted_iota(jnp.int32, (heads, 1, 256), 0)
    start = first + head * HEAD_DIM
    here = jnp.logical_and(lane >= start, lane < start + HEAD_DIM)
    out = jnp.where(here, wide[None], jnp.zeros((), x.dtype))
    if ones_at is not None:
        at = ones_at + 3 * head
        out = jnp.where(jnp.logical_and(lane >= at, lane < at + 3), jnp.ones((), x.dtype), out)
    return out


def three_parts(x):
    high = lax.reduce_precision(x, 8, 7)
    mid = lax.reduce_precision(x - high, 8, 7)
    return jnp.stack([high, mid, x - high - mid], axis=-1).astype(BF16)


def to_all(x, axis="ulysses"):
    ways = lax.axis_size(axis)
    sent = jnp.broadcast_to(x[None], (ways,) + x.shape)
    return lax.all_to_all(sent, axis, split_axis=0, concat_axis=0, tiled=True)


def summed_at_owner(x, axis="ulysses"):
    ways = lax.axis_size(axis)
    sent = x.astype(BF16).reshape(ways, -1, x.shape[1])
    got = lax.all_to_all(sent, axis, split_axis=0, concat_axis=0, tiled=True)
    return jnp.sum(got.astype(F32), axis=0)


def on_device(
    tokens,
    stretch_order,
    ln_gain,
    ln_bias,
    w_qkv,
    qv_bias,
    w_out,
    out_bias,
    w_up,
    up_bias,
    w_down,
    down_bias,
    cotangent,
):
    own_rows, width = tokens.shape
    ways = lax.axis_size("ulysses")
    wide = lax.axis_size("batch") * lax.axis_size("blk")
    me = lax.axis_index("ulysses")
    rows = own_rows * ways
    heads = HEADS // ways
    part = width // ways
    held = w_qkv.shape[1]
    ff_held = w_down.shape[1]
    ff_part = ff_held * wide
    pair = 2 * held

    order = stretch_order[0]
    own = lax.dynamic_slice(order, (2 * lax.axis_index("blk"),), (2,))

    small = jnp.concatenate(
        [
            ln_gain,
            ln_bias,
            qv_bias,
            jnp.concatenate([out_bias, down_bias], axis=1),
            up_bias.reshape(2, pair),
        ],
        axis=0,
    )
    qkv_slices = w_qkv[0].reshape(held, 3, ways, part).transpose(2, 0, 1, 3).reshape(ways, held, 3 * part)
    first = jnp.concatenate(
        [
            qkv_slices,
            jnp.broadcast_to(small[None], (ways,) + small.shape),
            jnp.zeros((ways, held, width - 3 * part - pair), BF16),
        ],
        axis=2,
    )
    first = jnp.pad(first, ((0, 0), (0, 8 - held), (0, 0)))
    sent = jnp.concatenate([jnp.broadcast_to(tokens[None], (ways,) + tokens.shape), first], axis=1)
    got = lax.all_to_all(sent, "ulysses", split_axis=0, concat_axis=0, tiled=True)
    x = got[:, :own_rows].reshape(rows, width).astype(F32)
    piece = got[:, own_rows : own_rows + held, : 3 * part + 64].reshape(ways * held, 3 * part + 64)
    filled = lax.all_gather(piece, WIDE, axis=0, tiled=True)
    w_qkv_u = filled[:, : 3 * part]
    smalls = filled[:, 3 * part : 3 * part + pair].reshape(wide * ways, held, pair).astype(F32)
    gains = smalls[:, 0].reshape(-1)
    shifts = smalls[:, 1].reshape(-1)
    qv_all = smalls[:, 2].reshape(-1)
    out_bias_all = smalls[:, 3, :held].reshape(-1)
    down_bias_all = smalls[:, 3, held:].reshape(-1)
    up_bias_all = smalls[:, 4:].reshape(wide, ways, ff_held)
    up_bias_u = lax.dynamic_index_in_dim(up_bias_all, me, axis=1, keepdims=False).reshape(-1)
    bias_q = lax.dynamic_slice(qv_all, (me * part,), (part,))
    bias_v = lax.dynamic_slice(qv_all, (width + me * part,), (part,))

    n1, r1 = normalized(x)
    h1 = (n1 * gains[:width] + shifts[:width]).astype(BF16)
    proj_bias = jnp.concatenate([bias_q, jnp.zeros((part,), F32), bias_v])
    proj = (mm(h1, w_qkv_u) + proj_bias).astype(BF16)
    q_scaled = proj[:, :part] * jnp.asarray(1.0 / math.sqrt(HEAD_DIM), BF16)
    kv = proj[:, part:]
    kv_all = lax.all_gather(kv, "blk", axis=0, tiled=True)
    q_all = lax.all_gather(jnp.pad(q_scaled, ((0, 0), (0, 256 - part))), "blk", axis=0, tiled=True)
    qpad = head_lanes(q_scaled, heads, 0)

    up_slices = w_up[0].reshape(held, wide, ways, ff_held).transpose(2, 0, 1, 3).reshape(ways, held, ff_part)
    second = jnp.concatenate(
        [up_slices, jnp.broadcast_to(w_out[0][None], (ways, held, width))], axis=2
    )
    second = lax.all_to_all(second, "ulysses", split_axis=0, concat_axis=0, tiled=True)
    ffn = jnp.concatenate([second.reshape(ways * held, ff_part + width), w_down[0]], axis=1)
    ffn_all = lax.all_gather(ffn, WIDE, axis=0, tiled=True)
    w_up_u = ffn_all[:, :ff_part]
    w_out_all = ffn_all[:, ff_part : ff_part + width]
    w_down_u = ffn_all[:, ff_part + width :]
    w_out_u = lax.dynamic_slice(w_out_all, (me * part, 0), (part, width))

    df_own = cotangent.astype(BF16)
    df = to_all(df_own).reshape(rows, width)

    ctx_low, ctx, lse = attend(order, own, qpad, kv_all)
    ctx_all = to_all(ctx_low)
    out = mm(ctx_all[0], w_out_all[:part])
    for u in range(1, ways):
        out += mm(ctx_all[u], w_out_all[u * part : (u + 1) * part])
    x2 = x + out + out_bias_all
    n2, r2 = normalized(x2)
    gain_two = gains[width:]
    h2 = (n2 * gain_two + shifts[width:]).astype(BF16)

    up = mm(h2, w_up_u) + up_bias_u
    act = gelu_tanh(up).astype(BF16)
    down = mm(act, w_down_u)
    d_act = mm_nt(df, w_down_u)
    _, gelu_pull = jax.vjp(gelu_tanh, up)
    du = gelu_pull(d_act)[0].astype(BF16)
    dh2 = summed_at_owner(mm_nt(du, w_up_u))

    def mine(a):
        return lax.dynamic_slice(a, (me * own_rows, 0), (own_rows, a.shape[1]))

    x2_own = mine(x2)
    result = (
        lax.psum_scatter(down, "ulysses", scatter_dimension=0, tiled=True)
        + x2_own
        + down_bias_all
    )
    g_w_down = mm_tn(act, df)
    g_w_up = mm_tn(h2, du)
    g_up_bias = jnp.sum(du.astype(F32), axis=0)
    g_down_bias = jnp.sum(df_own.astype(F32), axis=0)

    n2_own, r2_own = normalized(x2_own)
    dx2 = cotangent + norm_back(dh2, gain_two, n2_own, r2_own)
    g_gain_two = jnp.sum(dh2 * n2_own, axis=0)
    g_shift_two = jnp.sum(dh2, axis=0)
    dc_own = dx2.astype(BF16)
    g_out_bias = jnp.sum(dc_own.astype(F32), axis=0)
    dc = to_all(dc_own).reshape(rows, width)
    dctx = mm_nt(dc, w_out_u).astype(BF16)
    g_w_out = mm_tn(ctx_low, dc)

    delta = jnp.sum((dctx.astype(F32) * ctx).reshape(rows, heads, HEAD_DIM), axis=2)
    lse_cols = lse[:heads].T
    packed = jnp.concatenate(
        [
            dctx,
            three_parts(-lse_cols).reshape(rows, 3 * heads),
            three_parts(-delta).reshape(rows, 3 * heads),
            jnp.zeros((rows, 256 - part - 6 * heads), BF16),
        ],
        axis=1,
    )
    packed_all = lax.all_gather(packed, "blk", axis=0, tiled=True)
    delta_rows = jnp.pad(delta.T, ((0, 8 - heads), (0, 0)))
    d_query = query_grad(order, own, qpad, head_lanes(dctx, heads, 64), lse, delta_rows, kv_all)
    kpad = head_lanes(kv[:, :part], heads, 0, part)
    vpad = head_lanes(kv[:, part:], heads, 0, part + 3 * heads)
    d_key, d_value = key_grad(order, own, kpad, vpad, q_all, packed_all)
    d_proj = jnp.concatenate([d_query, d_key, d_value], axis=1)
    dh1 = summed_at_owner(mm_nt(d_proj, w_qkv_u))
    g_w_qkv = mm_tn(h1, d_proj)
    n1_own, r1_own = normalized(tokens.astype(F32))
    d_tokens = dx2 + norm_back(dh1, gains[:width], n1_own, r1_own)
    g_gain_one = jnp.sum(dh1 * n1_own, axis=0)
    g_shift_one = jnp.sum(dh1, axis=0)

    early = jnp.concatenate(
        [
            g_w_up,
            g_w_down,
            g_w_out.reshape(wide, held, ways, part).reshape(wide * held * ways, part),
        ],
        axis=1,
    )
    early = lax.psum_scatter(early, WIDE, scatter_dimension=0, tiled=True)
    g_up_rows = early[:, :ff_part]
    o_w_down = early[:, ff_part : ff_part + width]
    out_rows = early[:, ff_part + width :].reshape(held, ways * part)
    count = wide * ways
    o_w_out = lax.ppermute(
        out_rows, ALL, [(w * ways + u, u * wide + w) for w in range(wide) for u in range(ways)]
    )

    d_sums = jnp.sum(d_proj.astype(F32), axis=0)
    g_qv = jnp.zeros((2, ways, part), F32)
    g_qv = lax.dynamic_update_slice(g_qv, d_sums[:part].reshape(1, 1, part), (0, me, 0))
    g_qv = lax.dynamic_update_slice(g_qv, d_sums[2 * part :].reshape(1, 1, part), (1, me, 0))
    g_up_full = jnp.zeros((wide, ways, ff_held), F32)
    g_up_full = lax.dynamic_update_slice(
        g_up_full, g_up_bias.reshape(wide, 1, ff_held), (0, me, 0)
    )
    small_grads = jnp.concatenate(
        [
            jnp.concatenate([g_gain_one, g_gain_two]).reshape(count, 1, pair),
            jnp.concatenate([g_shift_one, g_shift_two]).reshape(count, 1, pair),
            g_qv.reshape(count, 1, pair),
            jnp.concatenate(
                [g_out_bias.reshape(count, 1, held), g_down_bias.reshape(count, 1, held)], axis=2
            ),
            g_up_full.reshape(count, 2, pair),
        ],
        axis=1,
    ).reshape(count * held, pair)
    late = jnp.concatenate([g_w_qkv, jnp.pad(small_grads, ((0, 0), (0, 64 - pair)))], axis=1)
    late = summed_at_owner(late, WIDE)
    last = jnp.concatenate([late, g_up_rows], axis=1).reshape(ways, held, -1)
    last = lax.all_to_all(last, "ulysses", split_axis=0, concat_axis=0, tiled=True)
    o_w_qkv = last[:, :, : 3 * part].reshape(ways, held, 3, part).transpose(1, 2, 0, 3)
    o_small = jnp.sum(last[:, :, 3 * part : 3 * part + pair], axis=0)
    o_w_up = last[:, :, 3 * part + 64 :].reshape(ways, held, wide, ff_held).transpose(1, 2, 0, 3)
    return (
        result,
        d_tokens,
        o_small[0:1],
        o_small[1:2],
        o_w_qkv.reshape(1, held, 3 * width),
        o_small[2:3],
        o_w_out[None],
        o_small[3:4, :held],
        o_w_up.reshape(1, held, -1),
        o_small[4:6].reshape(1, ff_held),
        o_w_down[None],
        o_small[3:4, held:],
    )


def solution(mesh):
    rows = P(ALL, None)
    flat = P(None, ALL)
    deep = P(None, ALL, None)
    return jax.shard_map(
        on_device,
        mesh=mesh,
        in_specs=(
            rows, P("batch", None), flat, flat, deep, flat, deep, flat, deep, flat, deep, flat, rows,
        ),
        out_specs=(rows, rows, flat, flat, deep, flat, deep, flat, deep, flat, deep, flat),
        check_vma=False,
    )
```

```python
import functools
import math

import jax
import jax.numpy as jnp
from jax import lax
from jax.experimental import pallas as pl
from jax.experimental.pallas import tpu as pltpu
from jax.sharding import PartitionSpec as P

HEADS = 12
HEAD_DIM = 64
NORM_EPS = 1e-05
FLOOR = -1e25
BELOW_FLOOR = -1e30
ALL = ("batch", "blk", "ulysses")
WIDE = ("batch", "blk")
BF16 = jnp.bfloat16
F32 = jnp.float32
NT = (((1,), (1,)), ((), ()))
VMEM_LIMIT = 60 * 1024 * 1024


def mm(a, b):
    return jnp.dot(a, b, preferred_element_type=F32)


def mm_nt(a, b):
    return lax.dot_general(a, b, NT, preferred_element_type=F32)


def mm_tn(a, b):
    return lax.dot_general(a, b, (((0,), (0,)), ((), ())), preferred_element_type=F32)


def allowed_tile(key_ranks, query_ranks, half, key_rows, query_cols):
    rows = lax.broadcasted_iota(jnp.int32, (key_rows, 1), 0)
    cols = lax.broadcasted_iota(jnp.int32, (1, query_cols), 1)

    def positions(index, ranks):
        if len(ranks) == 1:
            return ranks[0] * half + index
        return jnp.where(index < half, ranks[0] * half + index, (ranks[1] - 1) * half + index)

    return positions(rows, key_ranks) <= positions(cols, query_ranks)


def attend_kernel(
    ranks, own, qpad, kv, ctx_low, ctx, lse, v_turned, row_max, row_sum, total, *, half, heads
):
    step = pl.program_id(0)
    width = HEAD_DIM

    @pl.when(step == 0)
    def _():
        row_max[...] = jnp.full_like(row_max, FLOOR)
        row_sum[...] = jnp.zeros_like(row_sum)
        total[...] = jnp.zeros_like(total)

    key_ranks = (ranks[2 * step], ranks[2 * step + 1])
    low_rank = jnp.minimum(*key_ranks)
    high_rank = jnp.maximum(*key_ranks)
    v_turned[...] = kv[:, 128:].T

    def tile(part, masked):
        cols = slice(part * half, (part + 1) * half)
        if masked:
            allowed = allowed_tile(key_ranks, (own[part],), half, 2 * half, half)
        for h in range(heads):
            logits = mm_nt(kv[:, :256], qpad[h, cols, :])
            if masked:
                logits = jnp.where(allowed, logits, BELOW_FLOOR)
            old_max = row_max[h : h + 1, cols]
            new_max = jnp.maximum(old_max, jnp.max(logits, axis=0, keepdims=True))
            scale = jnp.exp(old_max - new_max)
            probs = jnp.exp(logits - new_max)
            row_max[h : h + 1, cols] = new_max
            row_sum[h : h + 1, cols] = row_sum[h : h + 1, cols] * scale + jnp.sum(
                probs, axis=0, keepdims=True
            )
            rows = slice(h * width, (h + 1) * width)
            values = v_turned[width * (h + 1) : width * (h + 2), :]
            total[rows, cols] = total[rows, cols] * scale + mm(values, probs.astype(BF16))

    for part in range(2):
        own_rank = own[part]

        @pl.when(high_rank < own_rank)
        def _():
            tile(part, False)

        @pl.when(jnp.logical_and(low_rank <= own_rank, own_rank <= high_rank))
        def _():
            tile(part, True)

    @pl.when(step == pl.num_programs(0) - 1)
    def _():
        for h in range(heads):
            rows = slice(h * width, (h + 1) * width)
            total[rows, :] = total[rows, :] / row_sum[h : h + 1, :]
        done = total[...].T
        ctx[...] = done
        ctx_low[...] = done.astype(BF16)
        lse[...] = row_max[...] + jnp.log(row_sum[...])


def query_grad_kernel(
    ranks, own, qpad, dpad, lse, delta, kv, d_query, k_turned, total, *, half, heads
):
    step = pl.program_id(0)
    width = HEAD_DIM

    @pl.when(step == 0)
    def _():
        total[...] = jnp.zeros_like(total)

    key_ranks = (ranks[2 * step], ranks[2 * step + 1])
    low_rank = jnp.minimum(*key_ranks)
    high_rank = jnp.maximum(*key_ranks)
    k_turned[...] = kv[:, :256].T

    def tile(part, masked):
        cols = slice(part * half, (part + 1) * half)
        if masked:
            allowed = allowed_tile(key_ranks, (own[part],), half, 2 * half, half)
        for h in range(heads):
            probs = jnp.exp(mm_nt(kv[:, :256], qpad[h, cols, :]) - lse[h : h + 1, cols])
            if masked:
                probs = jnp.where(allowed, probs, 0.0)
            d_probs = mm_nt(kv[:, 128:], dpad[h, cols, :])
            d_logits = (probs * (d_probs - delta[h : h + 1, cols])).astype(BF16)
            rows = slice(h * width, (h + 1) * width)
            total[rows, cols] += mm(k_turned[rows, :], d_logits)

    for part in range(2):
        own_rank = own[part]

        @pl.when(high_rank < own_rank)
        def _():
            tile(part, False)

        @pl.when(jnp.logical_and(low_rank <= own_rank, own_rank <= high_rank))
        def _():
            tile(part, True)

    @pl.when(step == pl.num_programs(0) - 1)
    def _():
        d_query[...] = (total[...] * (1.0 / math.sqrt(HEAD_DIM))).T.astype(BF16)


def key_grad_kernel(ranks, own, kpad, vpad, q_all, p_all, d_key, d_value, k_sum, v_sum, *, half, heads):
    step = pl.program_id(0)
    width = HEAD_DIM

    @pl.when(step == 0)
    def _():
        k_sum[...] = jnp.zeros_like(k_sum)
        v_sum[...] = jnp.zeros_like(v_sum)

    query_ranks = (ranks[2 * step], ranks[2 * step + 1])
    low_rank = jnp.minimum(*query_ranks)
    high_rank = jnp.maximum(*query_ranks)

    def tile(part, masked):
        rows = slice(part * half, (part + 1) * half)
        lane = lax.broadcasted_iota(jnp.int32, (2 * half, 256), 1)
        queries = q_all[...]
        packed = p_all[...]
        q_ext = jnp.where(lane < heads * width, queries, packed)
        if masked:
            allowed = allowed_tile((own[part],), query_ranks, half, half, 2 * half)
        k_new = jnp.zeros((half, 256), F32)
        v_new = jnp.zeros((half, 256), F32)
        zero = jnp.zeros_like(queries)
        for h in range(heads):
            here = jnp.logical_and(lane >= h * width, lane < (h + 1) * width)
            probs = jnp.exp(mm_nt(kpad[h, rows, :], q_ext))
            if masked:
                probs = jnp.where(allowed, probs, 0.0)
            d_probs = mm_nt(vpad[h, rows, :], packed)
            d_logits = (probs * d_probs).astype(BF16)
            k_new += mm(d_logits, jnp.where(here, queries, zero))
            v_new += mm(probs.astype(BF16), jnp.where(here, packed, zero))
        k_sum[rows, :] += k_new
        v_sum[rows, :] += v_new

    for part in range(2):
        own_rank = own[part]

        @pl.when(own_rank < low_rank)
        def _():
            tile(part, False)

        @pl.when(jnp.logical_and(low_rank <= own_rank, own_rank <= high_rank))
        def _():
            tile(part, True)

    @pl.when(step == pl.num_programs(0) - 1)
    def _():
        d_key[...] = k_sum[:, : heads * width].astype(BF16)
        d_value[...] = v_sum[:, : heads * width].astype(BF16)


def whole(shape):
    return pl.BlockSpec(shape, lambda i, *_: (0,) * len(shape))


def streamed(rows, cols):
    return pl.BlockSpec((rows, cols), lambda i, *_: (i, 0))


def cost(rows, keys, heads, products):
    area = rows * keys * heads
    return pl.CostEstimate(
        flops=2 * area * 256 * products, bytes_accessed=keys * 768, transcendentals=area
    )


def params():
    return pltpu.CompilerParams(
        dimension_semantics=("arbitrary",), vmem_limit_bytes=VMEM_LIMIT
    )


def attend(ranks, own, qpad, kv):
    heads, rows, _ = qpad.shape
    keys = kv.shape[0]
    width = heads * HEAD_DIM
    return pl.pallas_call(
        functools.partial(attend_kernel, half=rows // 2, heads=heads),
        out_shape=(
            jax.ShapeDtypeStruct((rows, width), BF16),
            jax.ShapeDtypeStruct((rows, width), F32),
            jax.ShapeDtypeStruct((8, rows), F32),
        ),
        grid_spec=pltpu.PrefetchScalarGridSpec(
            num_scalar_prefetch=2,
            grid=(keys // rows,),
            in_specs=[whole(qpad.shape), streamed(rows, kv.shape[1])],
            out_specs=[whole((rows, width)), whole((rows, width)), whole((8, rows))],
            scratch_shapes=[
                pltpu.VMEM((256, rows), BF16),
                pltpu.VMEM((8, rows), F32),
                pltpu.VMEM((8, rows), F32),
                pltpu.VMEM((width, rows), F32),
            ],
        ),
        compiler_params=params(),
        cost_estimate=cost(rows, keys, heads, 2),
        name="attend",
    )(ranks, own, qpad, kv)


def query_grad(ranks, own, qpad, dpad, lse, delta, kv):
    heads, rows, _ = qpad.shape
    keys = kv.shape[0]
    width = heads * HEAD_DIM
    return pl.pallas_call(
        functools.partial(query_grad_kernel, half=rows // 2, heads=heads),
        out_shape=jax.ShapeDtypeStruct((rows, width), BF16),
        grid_spec=pltpu.PrefetchScalarGridSpec(
            num_scalar_prefetch=2,
            grid=(keys // rows,),
            in_specs=[
                whole(qpad.shape),
                whole(dpad.shape),
                whole((8, rows)),
                whole((8, rows)),
                streamed(rows, kv.shape[1]),
            ],
            out_specs=whole((rows, width)),
            scratch_shapes=[pltpu.VMEM((256, rows), BF16), pltpu.VMEM((width, rows), F32)],
        ),
        compiler_params=params(),
        cost_estimate=cost(rows, keys, heads, 3),
        name="query_grad",
    )(ranks, own, qpad, dpad, lse, delta, kv)


def key_grad(ranks, own, kpad, vpad, q_all, p_all):
    heads, rows, _ = kpad.shape
    queries = q_all.shape[0]
    width = heads * HEAD_DIM
    return pl.pallas_call(
        functools.partial(key_grad_kernel, half=rows // 2, heads=heads),
        out_shape=(
            jax.ShapeDtypeStruct((rows, width), BF16),
            jax.ShapeDtypeStruct((rows, width), BF16),
        ),
        grid_spec=pltpu.PrefetchScalarGridSpec(
            num_scalar_prefetch=2,
            grid=(queries // rows,),
            in_specs=[
                whole(kpad.shape),
                whole(vpad.shape),
                streamed(rows, 256),
                streamed(rows, 256),
            ],
            out_specs=[whole((rows, width)), whole((rows, width))],
            scratch_shapes=[pltpu.VMEM((rows, 256), F32), pltpu.VMEM((rows, 256), F32)],
        ),
        compiler_params=params(),
        cost_estimate=cost(rows, queries, heads, 4),
        name="key_grad",
    )(ranks, own, kpad, vpad, q_all, p_all)


def weight_grads_kernel(h2, du, act, df, ctx, dc, out, g_out, *, owners):
    each = h2.shape[1] // owners
    few = ctx.shape[1] // owners
    chunk = h2.shape[1] // 2
    for i in range(2):
        cols = slice(i * chunk, (i + 1) * chunk)
        mine = slice(i * owners // 2, (i + 1) * owners // 2)
        shape = (owners // 2, each, du.shape[1])
        out[mine, :each, :] = mm_tn(h2[:, cols], du[...]).reshape(shape)
        out[mine, each : 2 * each, :] = mm_tn(act[:, cols], df[...]).reshape(shape)
    g_out[...] = mm_tn(ctx[...], dc[...])
    out[:, 2 * each :, :] = jnp.zeros((owners, out.shape[1] - 2 * each, out.shape[2]), F32)
    for w in range(owners):
        out[w, 2 * each : 2 * each + few, :] = g_out[w * few : (w + 1) * few, :]


def weight_grads(h2, du, act, df, ctx, dc, owners):
    width = du.shape[1]
    each = h2.shape[1] // owners
    rows = 2 * each + 8
    out = pl.pallas_call(
        functools.partial(weight_grads_kernel, owners=owners),
        out_shape=jax.ShapeDtypeStruct((owners, rows, width), F32),
        scratch_shapes=[pltpu.VMEM((ctx.shape[1], width), F32)],
        compiler_params=pltpu.CompilerParams(vmem_limit_bytes=VMEM_LIMIT),
        cost_estimate=pl.CostEstimate(
            flops=4 * h2.size * width, bytes_accessed=8 * owners * rows * width, transcendentals=0
        ),
        name="weight_grads",
    )(h2, du, act, df, ctx, dc)
    return out.reshape(owners * rows, width)


def normalized(values):
    mean = jnp.mean(values, axis=-1, keepdims=True)
    centered = values - mean
    spread = jnp.mean(centered * centered, axis=-1, keepdims=True)
    scale = lax.rsqrt(spread + NORM_EPS)
    return centered * scale, scale


def norm_back(grad, gain, normed, scale):
    e = grad * gain
    mean_e = jnp.mean(e, axis=-1, keepdims=True)
    mean_en = jnp.mean(e * normed, axis=-1, keepdims=True)
    return scale * (e - mean_e - normed * mean_en)


def gelu_tanh(values):
    return jax.nn.gelu(values, approximate=True)


def head_lanes(x, heads, first, ones_at=None):
    rows, width = x.shape
    wide = jnp.pad(x, ((0, 0), (first, 256 - width - first)))
    lane = lax.broadcasted_iota(jnp.int32, (heads, 1, 256), 2)
    head = lax.broadcasted_iota(jnp.int32, (heads, 1, 256), 0)
    start = first + head * HEAD_DIM
    here = jnp.logical_and(lane >= start, lane < start + HEAD_DIM)
    out = jnp.where(here, wide[None], jnp.zeros((), x.dtype))
    if ones_at is not None:
        at = ones_at + 3 * head
        out = jnp.where(jnp.logical_and(lane >= at, lane < at + 3), jnp.ones((), x.dtype), out)
    return out


def three_parts(x):
    high = lax.reduce_precision(x, 8, 7)
    mid = lax.reduce_precision(x - high, 8, 7)
    return jnp.stack([high, mid, x - high - mid], axis=-1).astype(BF16)


def to_all(x, axis="ulysses"):
    ways = lax.axis_size(axis)
    sent = jnp.broadcast_to(x[None], (ways,) + x.shape)
    return lax.all_to_all(sent, axis, split_axis=0, concat_axis=0, tiled=True)


def summed_at_owner(x, axis="ulysses"):
    ways = lax.axis_size(axis)
    sent = x.astype(BF16).reshape(ways, -1, x.shape[1])
    got = lax.all_to_all(sent, axis, split_axis=0, concat_axis=0, tiled=True)
    return jnp.sum(got.astype(F32), axis=0)


def on_device(
    tokens,
    stretch_order,
    ln_gain,
    ln_bias,
    w_qkv,
    qv_bias,
    w_out,
    out_bias,
    w_up,
    up_bias,
    w_down,
    down_bias,
    cotangent,
):
    own_rows, width = tokens.shape
    ways = lax.axis_size("ulysses")
    wide = lax.axis_size("batch") * lax.axis_size("blk")
    me = lax.axis_index("ulysses")
    rows = own_rows * ways
    heads = HEADS // ways
    part = width // ways
    held = w_qkv.shape[1]
    ff_held = w_down.shape[1]
    ff_part = ff_held * wide
    pair = 2 * held

    order = stretch_order[0]
    own = lax.dynamic_slice(order, (2 * lax.axis_index("blk"),), (2,))

    small = jnp.concatenate(
        [
            ln_gain,
            ln_bias,
            qv_bias,
            jnp.concatenate([out_bias, down_bias], axis=1),
            up_bias.reshape(2, pair),
        ],
        axis=0,
    )
    qkv_slices = w_qkv[0].reshape(held, 3, ways, part).transpose(2, 0, 1, 3).reshape(ways, held, 3 * part)
    up_slices = w_up[0].reshape(held, wide, ways, ff_held).transpose(2, 0, 1, 3).reshape(ways, held, ff_part)
    first = jnp.concatenate(
        [
            up_slices,
            jnp.broadcast_to(w_out[0][None], (ways, held, width)),
            qkv_slices,
            jnp.broadcast_to(small[None], (ways,) + small.shape),
            jnp.zeros((ways, held, 64 - pair), BF16),
        ],
        axis=2,
    )
    first = lax.all_to_all(first, "ulysses", split_axis=0, concat_axis=0, tiled=True)
    first = first.reshape(ways * held, -1)
    ffn = jnp.concatenate([first[:, : ff_part + width], w_down[0]], axis=1)
    ffn_all = lax.all_gather(ffn, WIDE, axis=0, tiled=True)
    filled = lax.all_gather(first[:, ff_part + width :], WIDE, axis=0, tiled=True)
    filled, tokens_late = lax.optimization_barrier((filled, tokens))
    x = to_all(tokens_late).reshape(rows, width).astype(F32)
    w_qkv_u = filled[:, : 3 * part]
    smalls = filled[:, 3 * part : 3 * part + pair].reshape(wide * ways, held, pair).astype(F32)
    gains = smalls[:, 0].reshape(-1)
    shifts = smalls[:, 1].reshape(-1)
    qv_all = smalls[:, 2].reshape(-1)
    out_bias_all = smalls[:, 3, :held].reshape(-1)
    down_bias_all = smalls[:, 3, held:].reshape(-1)
    up_bias_all = smalls[:, 4:].reshape(wide, ways, ff_held)
    up_bias_u = lax.dynamic_index_in_dim(up_bias_all, me, axis=1, keepdims=False).reshape(-1)
    bias_q = lax.dynamic_slice(qv_all, (me * part,), (part,))
    bias_v = lax.dynamic_slice(qv_all, (width + me * part,), (part,))

    n1, r1 = normalized(x)
    h1 = (n1 * gains[:width] + shifts[:width]).astype(BF16)
    proj_bias = jnp.concatenate([bias_q, jnp.zeros((part,), F32), bias_v])
    proj = (mm(h1, w_qkv_u) + proj_bias).astype(BF16)
    q_scaled = proj[:, :part] * jnp.asarray(1.0 / math.sqrt(HEAD_DIM), BF16)
    kv = proj[:, part:]
    kv_all = lax.all_gather(kv, "blk", axis=0, tiled=True)
    qpad = head_lanes(q_scaled, heads, 0)

    df_own = cotangent.astype(BF16)
    df_own, kv = lax.optimization_barrier((df_own, kv))
    df = to_all(df_own).reshape(rows, width)
    w_up_u = ffn_all[:, :ff_part]
    w_out_all = ffn_all[:, ff_part : ff_part + width]
    w_down_u = ffn_all[:, ff_part + width :]
    w_out_u = lax.dynamic_slice(w_out_all, (me * part, 0), (part, width))
    qpad, df, w_up_u, w_out_all, w_down_u, w_out_u = lax.optimization_barrier(
        (qpad, df, w_up_u, w_out_all, w_down_u, w_out_u)
    )
    q_wide = jnp.pad(q_scaled, ((0, 0), (0, 256 - part)))
    q_wide, kv_all = lax.optimization_barrier((q_wide, kv_all))
    q_all = lax.all_gather(q_wide, "blk", axis=0, tiled=True)

    ctx_low, ctx, lse = attend(order, own, qpad, kv_all)
    ctx_all = to_all(ctx_low)
    out = mm(ctx_all[0], w_out_all[:part])
    for u in range(1, ways):
        out += mm(ctx_all[u], w_out_all[u * part : (u + 1) * part])
    x2 = x + out + out_bias_all
    n2, r2 = normalized(x2)
    gain_two = gains[width:]
    h2 = (n2 * gain_two + shifts[width:]).astype(BF16)

    up = mm(h2, w_up_u) + up_bias_u
    act = gelu_tanh(up).astype(BF16)
    down = mm(act, w_down_u)
    d_act = mm_nt(df, w_down_u)
    _, gelu_pull = jax.vjp(gelu_tanh, up)
    du = gelu_pull(d_act)[0].astype(BF16)
    both = jnp.concatenate([mm_nt(du, w_up_u).astype(BF16), down.astype(BF16)], axis=1)
    both = summed_at_owner(both)
    dh2 = both[:, :width]

    def mine(a):
        return lax.dynamic_slice(a, (me * own_rows, 0), (own_rows, a.shape[1]))

    x2_own = mine(x2)
    result = both[:, width:] + x2_own + down_bias_all
    g_up_bias = jnp.sum(du.astype(F32), axis=0)
    g_down_bias = jnp.sum(df_own.astype(F32), axis=0)

    n2_own, r2_own = normalized(x2_own)
    dx2 = cotangent + norm_back(dh2, gain_two, n2_own, r2_own)
    g_gain_two = jnp.sum(dh2 * n2_own, axis=0)
    g_shift_two = jnp.sum(dh2, axis=0)
    dc_own, q_all = lax.optimization_barrier((dx2.astype(BF16), q_all))
    g_out_bias = jnp.sum(dc_own.astype(F32), axis=0)
    dc = to_all(dc_own).reshape(rows, width)
    dctx = mm_nt(dc, w_out_u).astype(BF16)
    early = weight_grads(h2, du, act, df, ctx_low, dc, wide)

    delta = jnp.sum((dctx.astype(F32) * ctx).reshape(rows, heads, HEAD_DIM), axis=2)
    lse_cols = lse[:heads].T
    packed = jnp.concatenate(
        [
            dctx,
            three_parts(-lse_cols).reshape(rows, 3 * heads),
            three_parts(-delta).reshape(rows, 3 * heads),
            jnp.zeros((rows, 256 - part - 6 * heads), BF16),
        ],
        axis=1,
    )
    packed_all = lax.all_gather(packed, "blk", axis=0, tiled=True)
    delta_rows = jnp.pad(delta.T, ((0, 8 - heads), (0, 0)))
    d_query = query_grad(order, own, qpad, head_lanes(dctx, heads, 64), lse, delta_rows, kv_all)
    kpad = head_lanes(kv[:, :part], heads, 0, part)
    vpad = head_lanes(kv[:, part:], heads, 0, part + 3 * heads)
    d_key, d_value = key_grad(order, own, kpad, vpad, q_all, packed_all)
    d_proj = jnp.concatenate([d_query, d_key, d_value], axis=1)
    dh1 = summed_at_owner(mm_nt(d_proj, w_qkv_u))
    g_w_qkv = mm_tn(h1, d_proj)
    n1_own, r1_own = normalized(tokens.astype(F32))
    d_tokens = dx2 + norm_back(dh1, gains[:width], n1_own, r1_own)
    g_gain_one = jnp.sum(dh1 * n1_own, axis=0)
    g_shift_one = jnp.sum(dh1, axis=0)

    early = lax.psum_scatter(early, WIDE, scatter_dimension=0, tiled=True)
    g_up_rows = early[:ff_held]
    o_w_down = early[ff_held : 2 * ff_held]
    out_rows = early[2 * ff_held : 2 * ff_held + held]
    count = wide * ways
    o_w_out = lax.ppermute(
        out_rows, ALL, [(w * ways + u, u * wide + w) for w in range(wide) for u in range(ways)]
    )

    d_sums = jnp.sum(d_proj.astype(F32), axis=0)
    g_qv = jnp.zeros((2, ways, part), F32)
    g_qv = lax.dynamic_update_slice(g_qv, d_sums[:part].reshape(1, 1, part), (0, me, 0))
    g_qv = lax.dynamic_update_slice(g_qv, d_sums[2 * part :].reshape(1, 1, part), (1, me, 0))
    g_up_full = jnp.zeros((wide, ways, ff_held), F32)
    g_up_full = lax.dynamic_update_slice(
        g_up_full, g_up_bias.reshape(wide, 1, ff_held), (0, me, 0)
    )
    small_grads = jnp.concatenate(
        [
            jnp.concatenate([g_gain_one, g_gain_two]).reshape(count, 1, pair),
            jnp.concatenate([g_shift_one, g_shift_two]).reshape(count, 1, pair),
            g_qv.reshape(count, 1, pair),
            jnp.concatenate(
                [g_out_bias.reshape(count, 1, held), g_down_bias.reshape(count, 1, held)], axis=2
            ),
            g_up_full.reshape(count, 2, pair),
        ],
        axis=1,
    ).reshape(count * held, pair)
    late = jnp.concatenate([g_w_qkv, jnp.pad(small_grads, ((0, 0), (0, 64 - pair)))], axis=1)
    late = summed_at_owner(late, WIDE)
    last = jnp.concatenate([late, g_up_rows], axis=1).reshape(ways, held, -1)
    last = lax.all_to_all(last, "ulysses", split_axis=0, concat_axis=0, tiled=True)
    o_w_qkv = last[:, :, : 3 * part].reshape(ways, held, 3, part).transpose(1, 2, 0, 3)
    o_small = jnp.sum(last[:, :, 3 * part : 3 * part + pair], axis=0)
    o_w_up = last[:, :, 3 * part + 64 :].reshape(ways, held, wide, ff_held).transpose(1, 2, 0, 3)
    return (
        result,
        d_tokens,
        o_small[0:1],
        o_small[1:2],
        o_w_qkv.reshape(1, held, 3 * width),
        o_small[2:3],
        o_w_out[None],
        o_small[3:4, :held],
        o_w_up.reshape(1, held, -1),
        o_small[4:6].reshape(1, ff_held),
        o_w_down[None],
        o_small[3:4, held:],
    )


def solution(mesh):
    rows = P(ALL, None)
    flat = P(None, ALL)
    deep = P(None, ALL, None)
    return jax.shard_map(
        on_device,
        mesh=mesh,
        in_specs=(
            rows, P("batch", None), flat, flat, deep, flat, deep, flat, deep, flat, deep, flat, rows,
        ),
        out_specs=(rows, rows, flat, flat, deep, flat, deep, flat, deep, flat, deep, flat),
        check_vma=False,
    )
```

```python
import functools
import math

import jax
import jax.numpy as jnp
from jax import lax
from jax.experimental import pallas as pl
from jax.experimental.pallas import tpu as pltpu
from jax.sharding import Mesh, PartitionSpec as P

HEADS = 12
HEAD_DIM = 64
NORM_EPS = 1e-05
FLOOR = -1e25
BELOW_FLOOR = -1e30
BLK = ("xlo", "z", "core")
CHIPS = ("batch", "xlo", "z")
WIDE = ("batch", "xlo", "z", "core")
ALL = ("batch", "xlo", "z", "core", "ulysses")
BF16 = jnp.bfloat16
F32 = jnp.float32
NT = (((1,), (1,)), ((), ()))
VMEM_LIMIT = 60 * 1024 * 1024


def mm(a, b):
    return jnp.dot(a, b, preferred_element_type=F32)


def mm_nt(a, b):
    return lax.dot_general(a, b, NT, preferred_element_type=F32)


def mm_tn(a, b):
    return lax.dot_general(a, b, (((0,), (0,)), ((), ())), preferred_element_type=F32)


def allowed_tile(key_ranks, query_ranks, half, key_rows, query_cols):
    rows = lax.broadcasted_iota(jnp.int32, (key_rows, 1), 0)
    cols = lax.broadcasted_iota(jnp.int32, (1, query_cols), 1)

    def positions(index, ranks):
        if len(ranks) == 1:
            return ranks[0] * half + index
        return jnp.where(index < half, ranks[0] * half + index, (ranks[1] - 1) * half + index)

    return positions(rows, key_ranks) <= positions(cols, query_ranks)


def attend_kernel(
    ranks, own, qpad, kv, ctx_low, ctx, lse, v_turned, row_max, row_sum, total, *, half, heads
):
    step = pl.program_id(0)
    width = HEAD_DIM

    @pl.when(step == 0)
    def _():
        row_max[...] = jnp.full_like(row_max, FLOOR)
        row_sum[...] = jnp.zeros_like(row_sum)
        total[...] = jnp.zeros_like(total)

    key_ranks = (ranks[2 * step], ranks[2 * step + 1])
    low_rank = jnp.minimum(*key_ranks)
    high_rank = jnp.maximum(*key_ranks)
    v_turned[...] = kv[:, 128:].T

    def tile(part, masked):
        cols = slice(part * half, (part + 1) * half)
        if masked:
            allowed = allowed_tile(key_ranks, (own[part],), half, 2 * half, half)
        for h in range(heads):
            logits = mm_nt(kv[:, :256], qpad[h, cols, :])
            if masked:
                logits = jnp.where(allowed, logits, BELOW_FLOOR)
            old_max = row_max[h : h + 1, cols]
            new_max = jnp.maximum(old_max, jnp.max(logits, axis=0, keepdims=True))
            scale = jnp.exp(old_max - new_max)
            probs = jnp.exp(logits - new_max)
            row_max[h : h + 1, cols] = new_max
            row_sum[h : h + 1, cols] = row_sum[h : h + 1, cols] * scale + jnp.sum(
                probs, axis=0, keepdims=True
            )
            rows = slice(h * width, (h + 1) * width)
            values = v_turned[width * (h + 1) : width * (h + 2), :]
            total[rows, cols] = total[rows, cols] * scale + mm(values, probs.astype(BF16))

    for part in range(2):
        own_rank = own[part]

        @pl.when(high_rank < own_rank)
        def _():
            tile(part, False)

        @pl.when(jnp.logical_and(low_rank <= own_rank, own_rank <= high_rank))
        def _():
            tile(part, True)

    @pl.when(step == pl.num_programs(0) - 1)
    def _():
        for h in range(heads):
            rows = slice(h * width, (h + 1) * width)
            total[rows, :] = total[rows, :] / row_sum[h : h + 1, :]
        done = total[...].T
        ctx[...] = done
        ctx_low[...] = done.astype(BF16)
        lse[...] = row_max[...] + jnp.log(row_sum[...])


def query_grad_kernel(
    ranks, own, qpad, dpad, lse, delta, kv, d_query, k_turned, total, *, half, heads
):
    step = pl.program_id(0)
    width = HEAD_DIM

    @pl.when(step == 0)
    def _():
        total[...] = jnp.zeros_like(total)

    key_ranks = (ranks[2 * step], ranks[2 * step + 1])
    low_rank = jnp.minimum(*key_ranks)
    high_rank = jnp.maximum(*key_ranks)
    k_turned[...] = kv[:, :256].T

    def tile(part, masked):
        cols = slice(part * half, (part + 1) * half)
        if masked:
            allowed = allowed_tile(key_ranks, (own[part],), half, 2 * half, half)
        for h in range(heads):
            probs = jnp.exp(mm_nt(kv[:, :256], qpad[h, cols, :]) - lse[h : h + 1, cols])
            if masked:
                probs = jnp.where(allowed, probs, 0.0)
            d_probs = mm_nt(kv[:, 128:], dpad[h, cols, :])
            d_logits = (probs * (d_probs - delta[h : h + 1, cols])).astype(BF16)
            rows = slice(h * width, (h + 1) * width)
            total[rows, cols] += mm(k_turned[rows, :], d_logits)

    for part in range(2):
        own_rank = own[part]

        @pl.when(high_rank < own_rank)
        def _():
            tile(part, False)

        @pl.when(jnp.logical_and(low_rank <= own_rank, own_rank <= high_rank))
        def _():
            tile(part, True)

    @pl.when(step == pl.num_programs(0) - 1)
    def _():
        d_query[...] = (total[...] * (1.0 / math.sqrt(HEAD_DIM))).T.astype(BF16)


def key_grad_kernel(ranks, own, kpad, vpad, q_all, p_all, d_key, d_value, k_sum, v_sum, *, half, heads):
    step = pl.program_id(0)
    width = HEAD_DIM

    @pl.when(step == 0)
    def _():
        k_sum[...] = jnp.zeros_like(k_sum)
        v_sum[...] = jnp.zeros_like(v_sum)

    query_ranks = (ranks[2 * step], ranks[2 * step + 1])
    low_rank = jnp.minimum(*query_ranks)
    high_rank = jnp.maximum(*query_ranks)

    def tile(part, masked):
        rows = slice(part * half, (part + 1) * half)
        lane = lax.broadcasted_iota(jnp.int32, (2 * half, 256), 1)
        queries = q_all[...]
        packed = p_all[...]
        q_ext = jnp.where(lane < heads * width, queries, packed)
        if masked:
            allowed = allowed_tile((own[part],), query_ranks, half, half, 2 * half)
        k_new = jnp.zeros((half, 256), F32)
        v_new = jnp.zeros((half, 256), F32)
        zero = jnp.zeros_like(queries)
        for h in range(heads):
            here = jnp.logical_and(lane >= h * width, lane < (h + 1) * width)
            probs = jnp.exp(mm_nt(kpad[h, rows, :], q_ext))
            if masked:
                probs = jnp.where(allowed, probs, 0.0)
            d_probs = mm_nt(vpad[h, rows, :], packed)
            d_logits = (probs * d_probs).astype(BF16)
            k_new += mm(d_logits, jnp.where(here, queries, zero))
            v_new += mm(probs.astype(BF16), jnp.where(here, packed, zero))
        k_sum[rows, :] += k_new
        v_sum[rows, :] += v_new

    for part in range(2):
        own_rank = own[part]

        @pl.when(own_rank < low_rank)
        def _():
            tile(part, False)

        @pl.when(jnp.logical_and(low_rank <= own_rank, own_rank <= high_rank))
        def _():
            tile(part, True)

    @pl.when(step == pl.num_programs(0) - 1)
    def _():
        d_key[...] = k_sum[:, : heads * width].astype(BF16)
        d_value[...] = v_sum[:, : heads * width].astype(BF16)


def whole(shape):
    return pl.BlockSpec(shape, lambda i, *_: (0,) * len(shape))


def streamed(rows, cols):
    return pl.BlockSpec((rows, cols), lambda i, *_: (i, 0))


def cost(rows, keys, heads, products):
    area = rows * keys * heads
    return pl.CostEstimate(
        flops=2 * area * 256 * products, bytes_accessed=keys * 768, transcendentals=area
    )


def params():
    return pltpu.CompilerParams(
        dimension_semantics=("arbitrary",), vmem_limit_bytes=VMEM_LIMIT
    )


def attend(ranks, own, qpad, kv):
    heads, rows, _ = qpad.shape
    keys = kv.shape[0]
    width = heads * HEAD_DIM
    return pl.pallas_call(
        functools.partial(attend_kernel, half=rows // 2, heads=heads),
        out_shape=(
            jax.ShapeDtypeStruct((rows, width), BF16),
            jax.ShapeDtypeStruct((rows, width), F32),
            jax.ShapeDtypeStruct((8, rows), F32),
        ),
        grid_spec=pltpu.PrefetchScalarGridSpec(
            num_scalar_prefetch=2,
            grid=(keys // rows,),
            in_specs=[whole(qpad.shape), streamed(rows, kv.shape[1])],
            out_specs=[whole((rows, width)), whole((rows, width)), whole((8, rows))],
            scratch_shapes=[
                pltpu.VMEM((256, rows), BF16),
                pltpu.VMEM((8, rows), F32),
                pltpu.VMEM((8, rows), F32),
                pltpu.VMEM((width, rows), F32),
            ],
        ),
        compiler_params=params(),
        cost_estimate=cost(rows, keys, heads, 2),
        name="attend",
    )(ranks, own, qpad, kv)


def query_grad(ranks, own, qpad, dpad, lse, delta, kv):
    heads, rows, _ = qpad.shape
    keys = kv.shape[0]
    width = heads * HEAD_DIM
    return pl.pallas_call(
        functools.partial(query_grad_kernel, half=rows // 2, heads=heads),
        out_shape=jax.ShapeDtypeStruct((rows, width), BF16),
        grid_spec=pltpu.PrefetchScalarGridSpec(
            num_scalar_prefetch=2,
            grid=(keys // rows,),
            in_specs=[
                whole(qpad.shape),
                whole(dpad.shape),
                whole((8, rows)),
                whole((8, rows)),
                streamed(rows, kv.shape[1]),
            ],
            out_specs=whole((rows, width)),
            scratch_shapes=[pltpu.VMEM((256, rows), BF16), pltpu.VMEM((width, rows), F32)],
        ),
        compiler_params=params(),
        cost_estimate=cost(rows, keys, heads, 3),
        name="query_grad",
    )(ranks, own, qpad, dpad, lse, delta, kv)


def key_grad(ranks, own, kpad, vpad, q_all, p_all):
    heads, rows, _ = kpad.shape
    queries = q_all.shape[0]
    width = heads * HEAD_DIM
    return pl.pallas_call(
        functools.partial(key_grad_kernel, half=rows // 2, heads=heads),
        out_shape=(
            jax.ShapeDtypeStruct((rows, width), BF16),
            jax.ShapeDtypeStruct((rows, width), BF16),
        ),
        grid_spec=pltpu.PrefetchScalarGridSpec(
            num_scalar_prefetch=2,
            grid=(queries // rows,),
            in_specs=[
                whole(kpad.shape),
                whole(vpad.shape),
                streamed(rows, 256),
                streamed(rows, 256),
            ],
            out_specs=[whole((rows, width)), whole((rows, width))],
            scratch_shapes=[pltpu.VMEM((rows, 256), F32), pltpu.VMEM((rows, 256), F32)],
        ),
        compiler_params=params(),
        cost_estimate=cost(rows, queries, heads, 4),
        name="key_grad",
    )(ranks, own, kpad, vpad, q_all, p_all)


def feed_forward_kernel(
    me, x, ctx, df, vectors, w_up, w_out, w_down, x2_own, h2, act, du, dh2, down
):
    part = ctx.shape[2]
    total = x[...].astype(F32) + vectors[2:3, :]
    for u in range(ctx.shape[0]):
        total += mm(ctx[u], w_out[u * part : (u + 1) * part, :])

    @pl.when(pl.program_id(0) == me[0])
    def _():
        x2_own[...] = total

    normed, _ = normalized(total)
    h2_low = (normed * vectors[0:1, :] + vectors[1:2, :]).astype(BF16)
    h2[...] = h2_low
    up = mm(h2_low, w_up[...]) + vectors[3:4, :]
    bend = math.sqrt(2.0 / math.pi)
    square = up * up
    turn = jnp.tanh(bend * (up + 0.044715 * square * up))
    half = 0.5 * (1.0 + turn)
    act_low = (up * half).astype(BF16)
    act[...] = act_low
    down[...] = mm(act_low, w_down[...]).astype(BF16)
    slope = half + 0.5 * up * (1.0 - turn * turn) * (bend * (1.0 + 3 * 0.044715 * square))
    du_low = (slope * mm_nt(df[...], w_down[...])).astype(BF16)
    du[...] = du_low
    dh2[...] = mm_nt(du_low, w_up[...]).astype(BF16)


def feed_forward(me, x, ctx, df, vectors, weights):
    rows, width = x.shape
    ways, _, part = ctx.shape
    step = rows // ways

    def along(cols):
        return pl.BlockSpec((step, cols), lambda i, *_: (i, 0))

    def third(c):
        return pl.BlockSpec((weights.shape[0], width), lambda i, *_: (0, c))

    flat = jax.ShapeDtypeStruct((rows, width), BF16)
    return pl.pallas_call(
        feed_forward_kernel,
        out_shape=(jax.ShapeDtypeStruct((step, width), F32), flat, flat, flat, flat, flat),
        grid_spec=pltpu.PrefetchScalarGridSpec(
            num_scalar_prefetch=1,
            grid=(ways,),
            in_specs=[
                along(width),
                pl.BlockSpec((ways, step, part), lambda i, *_: (0, i, 0)),
                along(width),
                whole(vectors.shape),
                third(0),
                third(1),
                third(2),
            ],
            out_specs=[whole((step, width))] + [along(width)] * 5,
        ),
        compiler_params=params(),
        cost_estimate=pl.CostEstimate(
            flops=10 * rows * width * width, bytes_accessed=6 * width * width, transcendentals=rows * width
        ),
        name="feed_forward",
    )(me, x, ctx, df, vectors, weights, weights, weights)


def weight_grads_kernel(core, h2, du, act, df, ctx, dc, kept, sent, g_up, g_down, g_out):
    chips, rows, width = kept.shape
    owners = 2 * chips
    each = h2.shape[1] // owners
    few = ctx.shape[1] // owners
    chunk = h2.shape[1] // 2
    for i in range(2):
        cols = slice(i * chunk, (i + 1) * chunk)
        g_up[cols, :] = mm_tn(h2[:, cols], du[...])
        g_down[cols, :] = mm_tn(act[:, cols], df[...])
    g_out[...] = mm_tn(ctx[...], dc[...])

    def put(target, which):
        target[:, 2 * each :, :] = jnp.zeros((chips, rows - 2 * each, width), target.dtype)
        for g in range(chips):
            w = 2 * g + which
            target[g, :each, :] = g_up[w * each : (w + 1) * each, :].astype(target.dtype)
            target[g, each : 2 * each, :] = g_down[w * each : (w + 1) * each, :].astype(target.dtype)
            target[g, 2 * each : 2 * each + few, :] = g_out[w * few : (w + 1) * few, :].astype(
                target.dtype
            )

    for which in range(2):

        @pl.when(core[0] == which)
        def _():
            put(kept, which)
            put(sent, 1 - which)


def weight_grads(core, h2, du, act, df, ctx, dc, owners):
    width = du.shape[1]
    units = h2.shape[1]
    rows = 2 * units // owners + 8
    chips = owners // 2
    arrays = (h2, du, act, df, ctx, dc)
    kept, sent = pl.pallas_call(
        weight_grads_kernel,
        out_shape=(
            jax.ShapeDtypeStruct((chips, rows, width), F32),
            jax.ShapeDtypeStruct((chips, rows, width), BF16),
        ),
        grid_spec=pltpu.PrefetchScalarGridSpec(
            num_scalar_prefetch=1,
            grid=(1,),
            in_specs=[whole(a.shape) for a in arrays],
            out_specs=[whole((chips, rows, width))] * 2,
            scratch_shapes=[
                pltpu.VMEM((units, width), F32),
                pltpu.VMEM((units, width), F32),
                pltpu.VMEM((ctx.shape[1], width), F32),
            ],
        ),
        compiler_params=params(),
        cost_estimate=pl.CostEstimate(
            flops=4 * h2.size * width, bytes_accessed=6 * chips * rows * width, transcendentals=0
        ),
        name="weight_grads",
    )(core, *arrays)
    return kept.reshape(chips * rows, width), sent.reshape(chips * rows, width)


def normalized(values):
    mean = jnp.mean(values, axis=-1, keepdims=True)
    centered = values - mean
    spread = jnp.mean(centered * centered, axis=-1, keepdims=True)
    scale = lax.rsqrt(spread + NORM_EPS)
    return centered * scale, scale


def norm_back(grad, gain, normed, scale):
    e = grad * gain
    mean_e = jnp.mean(e, axis=-1, keepdims=True)
    mean_en = jnp.mean(e * normed, axis=-1, keepdims=True)
    return scale * (e - mean_e - normed * mean_en)


def gelu_tanh(values):
    return jax.nn.gelu(values, approximate=True)


def head_lanes(x, heads, first, ones_at=None):
    rows, width = x.shape
    wide = jnp.pad(x, ((0, 0), (first, 256 - width - first)))
    lane = lax.broadcasted_iota(jnp.int32, (heads, 1, 256), 2)
    head = lax.broadcasted_iota(jnp.int32, (heads, 1, 256), 0)
    start = first + head * HEAD_DIM
    here = jnp.logical_and(lane >= start, lane < start + HEAD_DIM)
    out = jnp.where(here, wide[None], jnp.zeros((), x.dtype))
    if ones_at is not None:
        at = ones_at + 3 * head
        out = jnp.where(jnp.logical_and(lane >= at, lane < at + 3), jnp.ones((), x.dtype), out)
    return out


def three_parts(x):
    high = lax.reduce_precision(x, 8, 7)
    mid = lax.reduce_precision(x - high, 8, 7)
    return jnp.stack([high, mid, x - high - mid], axis=-1).astype(BF16)


def to_all(x, axis="ulysses"):
    ways = lax.axis_size(axis)
    sent = jnp.broadcast_to(x[None], (ways,) + x.shape)
    return lax.all_to_all(sent, axis, split_axis=0, concat_axis=0, tiled=True)


def summed_at_owner(x, axis="ulysses"):
    ways = lax.axis_size(axis)
    sent = x.astype(BF16).reshape(ways, -1, x.shape[1])
    got = lax.all_to_all(sent, axis, split_axis=0, concat_axis=0, tiled=True)
    return jnp.sum(got.astype(F32), axis=0)


def on_device(
    tokens,
    stretch_order,
    ln_gain,
    ln_bias,
    w_qkv,
    qv_bias,
    w_out,
    out_bias,
    w_up,
    up_bias,
    w_down,
    down_bias,
    cotangent,
):
    own_rows, width = tokens.shape
    ways = lax.axis_size("ulysses")
    wide = lax.axis_size(WIDE)
    me = lax.axis_index("ulysses")
    rows = own_rows * ways
    heads = HEADS // ways
    part = width // ways
    held = w_qkv.shape[1]
    ff_held = w_down.shape[1]
    ff_part = ff_held * wide
    pair = 2 * held

    order = stretch_order[0]
    own = lax.dynamic_slice(order, (2 * lax.axis_index(BLK),), (2,))

    small = jnp.concatenate(
        [
            ln_gain,
            ln_bias,
            qv_bias,
            jnp.concatenate([out_bias, down_bias], axis=1),
            up_bias.reshape(2, pair),
        ],
        axis=0,
    )
    qkv_slices = w_qkv[0].reshape(held, 3, ways, part).transpose(2, 0, 1, 3).reshape(ways, held, 3 * part)
    up_slices = w_up[0].reshape(held, wide, ways, ff_held).transpose(2, 0, 1, 3).reshape(ways, held, ff_part)
    first = jnp.concatenate(
        [
            qkv_slices,
            jnp.broadcast_to(small[None], (ways,) + small.shape),
            jnp.zeros((ways, held, width - 3 * part - pair), BF16),
        ],
        axis=2,
    )
    blank = jnp.zeros((ways, 8 - held, width), BF16)
    sent = jnp.concatenate(
        [
            jnp.broadcast_to(tokens[None], (ways,) + tokens.shape),
            first,
            blank,
            up_slices,
            blank,
            jnp.broadcast_to(w_out[0][None], (ways, held, width)),
            blank,
        ],
        axis=1,
    )
    got = lax.all_to_all(sent, "ulysses", split_axis=0, concat_axis=0, tiled=True)
    x = got[:, :own_rows].reshape(rows, width)
    at = own_rows
    piece = got[:, at : at + held, : 3 * part + 64].reshape(ways * held, 3 * part + 64)
    filled = lax.all_gather(piece, WIDE, axis=0, tiled=True)
    ffn = jnp.concatenate(
        [
            got[:, at + 8 : at + 8 + held].reshape(ways * held, width),
            got[:, at + 16 : at + 16 + held].reshape(ways * held, width),
            w_down[0],
        ],
        axis=1,
    )
    w_qkv_u = filled[:, : 3 * part]
    smalls = filled[:, 3 * part : 3 * part + pair].reshape(wide * ways, held, pair).astype(F32)
    gains = smalls[:, 0].reshape(-1)
    shifts = smalls[:, 1].reshape(-1)
    qv_all = smalls[:, 2].reshape(-1)
    out_bias_all = smalls[:, 3, :held].reshape(-1)
    down_bias_all = smalls[:, 3, held:].reshape(-1)
    up_bias_all = smalls[:, 4:].reshape(wide, ways, ff_held)
    up_bias_u = lax.dynamic_index_in_dim(up_bias_all, me, axis=1, keepdims=False).reshape(-1)
    bias_q = lax.dynamic_slice(qv_all, (me * part,), (part,))
    bias_v = lax.dynamic_slice(qv_all, (width + me * part,), (part,))

    n1, r1 = normalized(x.astype(F32))
    h1 = (n1 * gains[:width] + shifts[:width]).astype(BF16)
    proj_bias = jnp.concatenate([bias_q, jnp.zeros((part,), F32), bias_v])
    proj = (mm(h1, w_qkv_u) + proj_bias).astype(BF16)
    q_scaled = proj[:, :part] * jnp.asarray(1.0 / math.sqrt(HEAD_DIM), BF16)
    kv = proj[:, part:]
    kv_all = lax.all_gather(kv, BLK, axis=0, tiled=True)
    qpad = head_lanes(q_scaled, heads, 0)

    df_own = cotangent.astype(BF16)
    df_own, kv = lax.optimization_barrier((df_own, kv))
    df = to_all(df_own).reshape(rows, width)
    qpad, df = lax.optimization_barrier((qpad, df))
    ffn, kv_all = lax.optimization_barrier((ffn, kv_all))
    ffn_all = lax.all_gather(ffn, WIDE, axis=0, tiled=True)
    q_wide = jnp.pad(q_scaled, ((0, 0), (0, 256 - part)))
    q_wide, ffn_all = lax.optimization_barrier((q_wide, ffn_all))
    q_all = lax.all_gather(q_wide, BLK, axis=0, tiled=True)

    ctx_low, ctx, lse = attend(order, own, qpad, kv_all)
    ctx_all = to_all(ctx_low)
    gain_two = gains[width:]
    vectors = jnp.stack(
        [gain_two, shifts[width:], out_bias_all, up_bias_u] + [jnp.zeros((width,), F32)] * 4
    )
    x2_own, h2, act, du, dh2, down = feed_forward(me[None], x, ctx_all, df, vectors, ffn_all)
    dh2 = summed_at_owner(dh2)
    w_out_u = lax.dynamic_slice(ffn_all, (me * part, width), (part, width))
    result = summed_at_owner(down) + x2_own + down_bias_all
    g_up_bias = jnp.sum(du.astype(F32), axis=0)
    g_down_bias = jnp.sum(df_own.astype(F32), axis=0)

    n2_own, r2_own = normalized(x2_own)
    dx2 = cotangent + norm_back(dh2, gain_two, n2_own, r2_own)
    g_gain_two = jnp.sum(dh2 * n2_own, axis=0)
    g_shift_two = jnp.sum(dh2, axis=0)
    dc_own, q_all = lax.optimization_barrier((dx2.astype(BF16), q_all))
    g_out_bias = jnp.sum(dc_own.astype(F32), axis=0)
    dc = to_all(dc_own).reshape(rows, width)
    dctx = mm_nt(dc, w_out_u).astype(BF16)
    core = lax.axis_index("core")
    early, early_sent = weight_grads(core[None], h2, du, act, df, ctx_low, dc, wide)

    delta = jnp.sum((dctx.astype(F32) * ctx).reshape(rows, heads, HEAD_DIM), axis=2)
    lse_cols = lse[:heads].T
    packed = jnp.concatenate(
        [
            dctx,
            three_parts(-lse_cols).reshape(rows, 3 * heads),
            three_parts(-delta).reshape(rows, 3 * heads),
            jnp.zeros((rows, 256 - part - 6 * heads), BF16),
        ],
        axis=1,
    )
    packed_all = lax.all_gather(packed, BLK, axis=0, tiled=True)
    delta_rows = jnp.pad(delta.T, ((0, 8 - heads), (0, 0)))
    d_query = query_grad(order, own, qpad, head_lanes(dctx, heads, 64), lse, delta_rows, kv_all)
    kpad = head_lanes(kv[:, :part], heads, 0, part)
    vpad = head_lanes(kv[:, part:], heads, 0, part + 3 * heads)
    d_key, d_value = key_grad(order, own, kpad, vpad, q_all, packed_all)
    d_proj = jnp.concatenate([d_query, d_key, d_value], axis=1)
    dh1 = summed_at_owner(mm_nt(d_proj, w_qkv_u))
    g_w_qkv = mm_tn(h1, d_proj)
    n1_own, r1_own = normalized(tokens.astype(F32))
    d_tokens = dx2 + norm_back(dh1, gains[:width], n1_own, r1_own)
    g_gain_one = jnp.sum(dh1 * n1_own, axis=0)
    g_shift_one = jnp.sum(dh1, axis=0)

    early = early + lax.ppermute(early_sent, "core", [(0, 1), (1, 0)]).astype(F32)
    early = summed_at_owner(early, CHIPS)
    g_up_rows = early[:ff_held]
    o_w_down = early[ff_held : 2 * ff_held]
    out_rows = early[2 * ff_held : 2 * ff_held + held]
    count = wide * ways
    o_w_out = lax.ppermute(
        out_rows, ALL, [(w * ways + u, u * wide + w) for w in range(wide) for u in range(ways)]
    )

    d_sums = jnp.sum(d_proj.astype(F32), axis=0)
    g_qv = jnp.zeros((2, ways, part), F32)
    g_qv = lax.dynamic_update_slice(g_qv, d_sums[:part].reshape(1, 1, part), (0, me, 0))
    g_qv = lax.dynamic_update_slice(g_qv, d_sums[2 * part :].reshape(1, 1, part), (1, me, 0))
    g_up_full = jnp.zeros((wide, ways, ff_held), F32)
    g_up_full = lax.dynamic_update_slice(
        g_up_full, g_up_bias.reshape(wide, 1, ff_held), (0, me, 0)
    )
    small_grads = jnp.concatenate(
        [
            jnp.concatenate([g_gain_one, g_gain_two]).reshape(count, 1, pair),
            jnp.concatenate([g_shift_one, g_shift_two]).reshape(count, 1, pair),
            g_qv.reshape(count, 1, pair),
            jnp.concatenate(
                [g_out_bias.reshape(count, 1, held), g_down_bias.reshape(count, 1, held)], axis=2
            ),
            g_up_full.reshape(count, 2, pair),
        ],
        axis=1,
    ).reshape(count * held, pair)
    late = jnp.concatenate([g_w_qkv, jnp.pad(small_grads, ((0, 0), (0, 64 - pair)))], axis=1)
    late = late.reshape(wide // 2, 2, ways * held, late.shape[1])
    late_sent = lax.dynamic_index_in_dim(late, 1 - core, axis=1, keepdims=False).astype(BF16)
    late = lax.dynamic_index_in_dim(late, core, axis=1, keepdims=False)
    late = late + lax.ppermute(late_sent, "core", [(0, 1), (1, 0)]).astype(F32)
    late = summed_at_owner(late.reshape(-1, late.shape[2]), CHIPS)
    last = jnp.concatenate([late, g_up_rows], axis=1).reshape(ways, held, -1)
    last = lax.all_to_all(last, "ulysses", split_axis=0, concat_axis=0, tiled=True)
    o_w_qkv = last[:, :, : 3 * part].reshape(ways, held, 3, part).transpose(1, 2, 0, 3)
    o_small = jnp.sum(last[:, :, 3 * part : 3 * part + pair], axis=0)
    o_w_up = last[:, :, 3 * part + 64 :].reshape(ways, held, wide, ff_held).transpose(1, 2, 0, 3)
    return (
        result,
        d_tokens,
        o_small[0:1],
        o_small[1:2],
        o_w_qkv.reshape(1, held, 3 * width),
        o_small[2:3],
        o_w_out[None],
        o_small[3:4, :held],
        o_w_up.reshape(1, held, -1),
        o_small[4:6].reshape(1, ff_held),
        o_w_down[None],
        o_small[3:4, held:],
    )


def solution(mesh):
    chips_z = mesh.shape["blk"] // 4
    parts = Mesh(
        mesh.devices.reshape(mesh.shape["batch"], 2, chips_z, 2, mesh.shape["ulysses"]), ALL
    )
    rows = P(ALL, None)
    flat = P(None, ALL)
    deep = P(None, ALL, None)
    return jax.shard_map(
        on_device,
        mesh=parts,
        in_specs=(
            rows, P("batch", None), flat, flat, deep, flat, deep, flat, deep, flat, deep, flat, rows,
        ),
        out_specs=(rows, rows, flat, flat, deep, flat, deep, flat, deep, flat, deep, flat),
        check_vma=False,
    )
```

```python
import functools
import math

import jax
import jax.numpy as jnp
from jax import lax
from jax.experimental import pallas as pl
from jax.experimental.pallas import tpu as pltpu
from jax.sharding import Mesh, PartitionSpec as P

HEADS = 12
HEAD_DIM = 64
NORM_EPS = 1e-05
FLOOR = -1e25
HIGHEST_ABOVE = 60.0
LANES = 256
EXTRA = 64
BELOW_FLOOR = -1e30
BLK = ("xlo", "z", "core")
CHIPS = ("batch", "xlo", "z")
WIDE = ("batch", "xlo", "z", "core")
ALL = ("batch", "xlo", "z", "core", "ulysses")
BF16 = jnp.bfloat16
F32 = jnp.float32
NT = (((1,), (1,)), ((), ()))
VMEM_LIMIT = 60 * 1024 * 1024


def mm(a, b):
    return jnp.dot(a, b, preferred_element_type=F32)


def mm_nt(a, b):
    return lax.dot_general(a, b, NT, preferred_element_type=F32)


def mm_tn(a, b):
    return lax.dot_general(a, b, (((0,), (0,)), ((), ())), preferred_element_type=F32)


def stretch(index, half):
    return pl.ds(pl.multiple_of(index * half, half), half)


def lanes_of(rows):
    return lax.broadcasted_iota(jnp.int32, (rows, LANES), 1)


def ones_after(k, first):
    return jnp.where(lanes_of(k.shape[0]) < first, k, jnp.ones_like(k))


def ones_before(v):
    return jnp.where(lanes_of(v.shape[0]) < EXTRA, jnp.ones_like(v), v)


def three(x):
    high = x.astype(BF16).astype(F32)
    mid = (x - high).astype(BF16).astype(F32)
    return high, mid, x - high - mid


def causal(half, heads, keys_first):
    rows = lax.broadcasted_iota(jnp.int32, (heads * half, half), 0) & (half - 1)
    cols = lax.broadcasted_iota(jnp.int32, (heads * half, half), 1)
    return rows <= cols if keys_first else cols <= rows


def merged_heads(stacked, half, heads, first):
    lane = lanes_of(half)
    out = stacked[:half]
    for h in range(1, heads):
        out = jnp.where(lane < first + h * HEAD_DIM, out, stacked[h * half : (h + 1) * half])
    return out


def in_groups(first, count, tiles):
    def eight(i, _):
        tiles([first + 8 * i + j for j in range(8)])
        return 0

    lax.fori_loop(0, count // 8, eight, 0)
    for size in (4, 2, 1):

        @pl.when((count & size) != 0)
        def _():
            begin = first + (count & ~(2 * size - 1))
            tiles([begin + j for j in range(size)])


def one_ahead(items, produce, consume):
    ready = produce(items[0])
    for n, item in enumerate(items):
        now = ready
        if n + 1 < len(items):
            ready = produce(items[n + 1])
        consume(item, now)


def attend_kernel(
    slots, own, q_heads, kv, ctx_low, ctx, lse, shift, total, q_ext, top, *, half, heads
):
    deep = heads * half
    lane = lanes_of(deep)

    def one_half(part, _):
        rank_own = own[part]
        mask = causal(half, heads, False)
        here = stretch(slots[rank_own], half)
        scores = jnp.where(mask, mm_nt(q_heads[part], kv[here, :LANES]), BELOW_FLOOR)
        first = jnp.max(scores, axis=1, keepdims=True).astype(BF16).astype(F32)
        shift[...] = first
        q_ext[...] = jnp.where(lane == heads * HEAD_DIM, -first, q_heads[part].astype(F32)).astype(
            BF16
        )
        top[...] = jnp.zeros_like(top)
        total[...] = mm(jnp.exp(scores - first).astype(BF16), ones_before(kv[here, 128:]))

        def tiles(ranks):
            at = [stretch(slots[r], half) for r in ranks]
            added = [total[...], top[...]]

            def produce(a):
                return mm_nt(q_ext[...], ones_after(kv[a, :LANES], heads * HEAD_DIM))

            def consume(a, above):
                added[1] = jnp.maximum(added[1], jnp.max(above.reshape(deep // 8, 8, half), axis=0))
                added[0] += mm(jnp.exp(above).astype(BF16), ones_before(kv[a, 128:]))

            one_ahead(at, produce, consume)
            total[...] = added[0]
            top[...] = added[1]

        in_groups(0, rank_own, tiles)

        @pl.when(jnp.logical_not(jnp.max(top[...]) < HIGHEST_ABOVE))
        def _():
            shift[...] = jnp.full_like(shift, FLOOR)
            total[...] = jnp.zeros_like(total)

            def again(rank, _):
                a = stretch(slots[rank], half)
                allowed = jnp.logical_or(mask, rank < rank_own)
                scores = jnp.where(allowed, mm_nt(q_heads[part], kv[a, :LANES]), BELOW_FLOOR)
                new = jnp.maximum(shift[...], jnp.max(scores, axis=1, keepdims=True))
                total[...] = total[...] * jnp.exp(shift[...] - new) + mm(
                    jnp.exp(scores - new).astype(BF16), ones_before(kv[a, 128:])
                )
                shift[...] = new
                return 0

            lax.fori_loop(0, rank_own + 1, again, 0)

        row_sum = total[:, :1]
        lse[part] = shift[...] + jnp.log(row_sum)
        done = merged_heads(total[...] / row_sum, half, heads, EXTRA)
        rows = stretch(part, half)
        ctx[rows, :] = done
        ctx_low[rows, :] = done[:, EXTRA:].astype(BF16)
        return 0

    lax.fori_loop(0, 2, one_half, 0)


def query_grad_kernel(slots, own, q_ext, d_ext, kv, d_query, total, *, half, heads):
    def one_half(part, _):
        rank_own = own[part]
        total[...] = jnp.zeros_like(total)

        def tiles(ranks, mask=None):
            at = [stretch(slots[r], half) for r in ranks]
            added = [total[...]]

            def produce(a):
                return (
                    mm_nt(q_ext[part], ones_after(kv[a, :LANES], heads * HEAD_DIM)),
                    mm_nt(d_ext[part], ones_before(kv[a, 128:])),
                )

            def consume(a, ready):
                probs = jnp.exp(ready[0])
                if mask is not None:
                    probs = jnp.where(mask, probs, 0.0)
                added[0] += mm((probs * ready[1]).astype(BF16), kv[a, :LANES])

            one_ahead(at, produce, consume)
            total[...] = added[0]

        in_groups(0, rank_own, tiles)
        tiles([rank_own], causal(half, heads, False))
        done = merged_heads(total[...], half, heads, 0)[:, : heads * HEAD_DIM]
        d_query[stretch(part, half), :] = (done * (1.0 / math.sqrt(HEAD_DIM))).astype(BF16)
        return 0

    lax.fori_loop(0, 2, one_half, 0)


def key_grad_kernel(
    slots, own, k_heads, v_heads, q_all, p_all, d_key, d_value, k_sum, v_sum, *, half, heads
):
    count = slots.shape[0]
    lane = lanes_of(half)

    def one_half(part, _):
        rank_own = own[part]
        k_sum[...] = jnp.zeros_like(k_sum)
        v_sum[...] = jnp.zeros_like(v_sum)

        def tiles(ranks, mask=None):
            at = [stretch(slots[r], half) for r in ranks]
            added = [k_sum[...], v_sum[...]]

            def produce(a):
                return (
                    mm_nt(k_heads[part], jnp.where(lane < EXTRA, p_all[a, :], q_all[a, :])),
                    mm_nt(v_heads[part], p_all[a, :]),
                )

            def consume(a, ready):
                probs = jnp.exp(ready[0])
                if mask is not None:
                    probs = jnp.where(mask, probs, 0.0)
                added[1] += mm(probs.astype(BF16), p_all[a, :])
                added[0] += mm((probs * ready[1]).astype(BF16), q_all[a, :])

            one_ahead(at, produce, consume)
            k_sum[...], v_sum[...] = added

        tiles([rank_own], causal(half, heads, True))
        in_groups(rank_own + 1, count - 1 - rank_own, tiles)
        rows = stretch(part, half)
        d_key[rows, :] = merged_heads(k_sum[...], half, heads, EXTRA)[:, EXTRA:].astype(BF16)
        d_value[rows, :] = merged_heads(v_sum[...], half, heads, EXTRA)[:, EXTRA:].astype(BF16)
        return 0

    lax.fori_loop(0, 2, one_half, 0)


def prepare_kernel(dc, w_out, ctx, lse, q_heads, packed, q_ext, d_ext, *, half, heads):
    lane = lanes_of(half)
    d_ctx = mm_nt(dc[...], w_out[...]).astype(BF16)
    for part in range(2):
        rows = slice(part * half, (part + 1) * half)
        grads = d_ctx[rows, :]
        terms = grads.astype(F32) * ctx[rows, :]
        extra = grads.astype(F32)
        for h in range(heads):
            deep = slice(h * half, (h + 1) * half)
            first = EXTRA + h * HEAD_DIM
            here = jnp.logical_and(lane >= first, lane < first + HEAD_DIM)
            delta = jnp.sum(jnp.where(here, terms, 0.0), axis=1, keepdims=True)
            minus_lse = three(-lse[part, deep, :])
            minus_delta = three(-delta)
            q_new = q_heads[part, deep, :].astype(F32)
            d_new = jnp.where(here, grads.astype(F32), 0.0)
            for i in range(3):
                q_new = jnp.where(lane == heads * HEAD_DIM + i, minus_lse[i], q_new)
                d_new = jnp.where(lane == i, minus_delta[i], d_new)
                extra = jnp.where(lane == 3 * h + i, minus_lse[i], extra)
                extra = jnp.where(lane == 3 * (heads + h) + i, minus_delta[i], extra)
            q_ext[part, deep, :] = q_new.astype(BF16)
            d_ext[part, deep, :] = d_new.astype(BF16)
        packed[rows, :] = extra.astype(BF16)


def whole(shape):
    return pl.BlockSpec(shape, lambda i, *_: (0,) * len(shape))


def params():
    return pltpu.CompilerParams(
        dimension_semantics=("arbitrary",), vmem_limit_bytes=VMEM_LIMIT
    )


def cost(rows, keys, heads, products):
    area = rows * keys * heads
    return pl.CostEstimate(
        flops=2 * area * 256 * products, bytes_accessed=keys * 768, transcendentals=area
    )


def call(kernel, name, scalars, arrays, outs, scratch, estimate, **static):
    return pl.pallas_call(
        functools.partial(kernel, **static),
        out_shape=tuple(jax.ShapeDtypeStruct(s, t) for s, t in outs),
        grid_spec=pltpu.PrefetchScalarGridSpec(
            num_scalar_prefetch=len(scalars),
            grid=(1,),
            in_specs=[whole(a.shape) for a in arrays],
            out_specs=[whole(s) for s, _ in outs],
            scratch_shapes=[pltpu.VMEM(s, t) for s, t in scratch],
        ),
        compiler_params=params(),
        cost_estimate=estimate,
        name=name,
    )(*scalars, *arrays)


def attend(slots, own, q_heads, kv, heads):
    _, deep, _ = q_heads.shape
    half = deep // heads
    width = heads * HEAD_DIM
    return call(
        attend_kernel, "attend", (slots, own), (q_heads, kv),
        [((2 * half, width), BF16), ((2 * half, LANES), F32), ((2, deep, 1), F32)],
        [((deep, 1), F32), ((deep, LANES), F32), ((deep, LANES), BF16), ((8, half), F32)],
        cost(2 * half, kv.shape[0], heads, 2), half=half, heads=heads,
    )


def prepare(dc, w_out, ctx, lse, q_heads, heads):
    _, deep, _ = q_heads.shape
    half = deep // heads
    return call(
        prepare_kernel, "prepare", (), (dc, w_out, ctx, lse, q_heads),
        [((2 * half, LANES), BF16), (q_heads.shape, BF16), (q_heads.shape, BF16)], [],
        pl.CostEstimate(flops=2 * dc.size * LANES, bytes_accessed=4 * q_heads.size, transcendentals=0),
        half=half, heads=heads,
    )


def query_grad(slots, own, q_ext, d_ext, kv, heads):
    _, deep, _ = q_ext.shape
    half = deep // heads
    return call(
        query_grad_kernel, "query_grad", (slots, own), (q_ext, d_ext, kv),
        [((2 * half, heads * HEAD_DIM), BF16)], [((deep, LANES), F32)],
        cost(2 * half, kv.shape[0], heads, 3), half=half, heads=heads,
    )[0]


def key_grad(slots, own, k_heads, v_heads, q_all, p_all, heads):
    _, deep, _ = k_heads.shape
    half = deep // heads
    out = ((2 * half, heads * HEAD_DIM), BF16)
    return call(
        key_grad_kernel, "key_grad", (slots, own), (k_heads, v_heads, q_all, p_all),
        [out, out], [((deep, LANES), F32)] * 2,
        cost(2 * half, q_all.shape[0], heads, 4), half=half, heads=heads,
    )


def feed_forward_kernel(
    me, x, ctx, df, vectors, w_up, w_out, w_down, x2_own, h2, act, du, dh2, down
):
    part = ctx.shape[2]
    total = x[...].astype(F32) + vectors[2:3, :]
    for u in range(ctx.shape[0]):
        total += mm(ctx[u], w_out[u * part : (u + 1) * part, :])

    @pl.when(pl.program_id(0) == me[0])
    def _():
        x2_own[...] = total

    normed, _ = normalized(total)
    h2_low = (normed * vectors[0:1, :] + vectors[1:2, :]).astype(BF16)
    h2[...] = h2_low
    up = mm(h2_low, w_up[...]) + vectors[3:4, :]
    bend = math.sqrt(2.0 / math.pi)
    square = up * up
    turn = jnp.tanh(bend * (up + 0.044715 * square * up))
    half = 0.5 * (1.0 + turn)
    act_low = (up * half).astype(BF16)
    act[...] = act_low
    down[...] = mm(act_low, w_down[...]).astype(BF16)
    slope = half + 0.5 * up * (1.0 - turn * turn) * (bend * (1.0 + 3 * 0.044715 * square))
    du_low = (slope * mm_nt(df[...], w_down[...])).astype(BF16)
    du[...] = du_low
    dh2[...] = mm_nt(du_low, w_up[...]).astype(BF16)


def feed_forward(me, x, ctx, df, vectors, weights):
    rows, width = x.shape
    ways, _, part = ctx.shape
    step = rows // ways

    def along(cols):
        return pl.BlockSpec((step, cols), lambda i, *_: (i, 0))

    def third(c):
        return pl.BlockSpec((weights.shape[0], width), lambda i, *_: (0, c))

    flat = jax.ShapeDtypeStruct((rows, width), BF16)
    return pl.pallas_call(
        feed_forward_kernel,
        out_shape=(jax.ShapeDtypeStruct((step, width), F32), flat, flat, flat, flat, flat),
        grid_spec=pltpu.PrefetchScalarGridSpec(
            num_scalar_prefetch=1,
            grid=(ways,),
            in_specs=[
                along(width),
                pl.BlockSpec((ways, step, part), lambda i, *_: (0, i, 0)),
                along(width),
                whole(vectors.shape),
                third(0),
                third(1),
                third(2),
            ],
            out_specs=[whole((step, width))] + [along(width)] * 5,
        ),
        compiler_params=params(),
        cost_estimate=pl.CostEstimate(
            flops=10 * rows * width * width, bytes_accessed=6 * width * width, transcendentals=rows * width
        ),
        name="feed_forward",
    )(me, x, ctx, df, vectors, weights, weights, weights)


def weight_grads_kernel(core, h2, du, act, df, ctx, dc, kept, sent, g_up, g_down, g_out, *, deep):
    chips, rows, width = kept.shape
    owners = 2 * chips
    each = h2.shape[1] // owners
    few = ctx.shape[1] // owners
    chunk = h2.shape[1] // 2
    for i in range(2):
        cols = slice(i * chunk, (i + 1) * chunk)
        g_up[cols, :] = mm_tn(h2[:, cols], du[...])
        g_down[cols, :] = mm_tn(act[:, cols], df[...])
    g_out[...] = mm_tn(ctx[...], dc[...])

    def put(target, which):
        target[:, 2 * each :, :] = jnp.zeros((chips, rows - 2 * each, width), target.dtype)
        for g in range(chips):
            w = 2 * (g % (chips // deep) * deep + g // (chips // deep)) + which
            target[g, :each, :] = g_up[w * each : (w + 1) * each, :].astype(target.dtype)
            target[g, each : 2 * each, :] = g_down[w * each : (w + 1) * each, :].astype(target.dtype)
            target[g, 2 * each : 2 * each + few, :] = g_out[w * few : (w + 1) * few, :].astype(
                target.dtype
            )

    for which in range(2):

        @pl.when(core[0] == which)
        def _():
            put(kept, which)
            put(sent, 1 - which)


def weight_grads(core, h2, du, act, df, ctx, dc, owners, deep):
    width = du.shape[1]
    units = h2.shape[1]
    rows = 2 * units // owners + 8
    chips = owners // 2
    arrays = (h2, du, act, df, ctx, dc)
    kept, sent = pl.pallas_call(
        functools.partial(weight_grads_kernel, deep=deep),
        out_shape=(
            jax.ShapeDtypeStruct((chips, rows, width), F32),
            jax.ShapeDtypeStruct((chips, rows, width), BF16),
        ),
        grid_spec=pltpu.PrefetchScalarGridSpec(
            num_scalar_prefetch=1,
            grid=(1,),
            in_specs=[whole(a.shape) for a in arrays],
            out_specs=[whole((chips, rows, width))] * 2,
            scratch_shapes=[
                pltpu.VMEM((units, width), F32),
                pltpu.VMEM((units, width), F32),
                pltpu.VMEM((ctx.shape[1], width), F32),
            ],
        ),
        compiler_params=params(),
        cost_estimate=pl.CostEstimate(
            flops=4 * h2.size * width, bytes_accessed=6 * chips * rows * width, transcendentals=0
        ),
        name="weight_grads",
    )(core, *arrays)
    return kept, sent


def normalized(values):
    mean = jnp.mean(values, axis=-1, keepdims=True)
    centered = values - mean
    spread = jnp.mean(centered * centered, axis=-1, keepdims=True)
    scale = lax.rsqrt(spread + NORM_EPS)
    return centered * scale, scale


def norm_back(grad, gain, normed, scale):
    e = grad * gain
    mean_e = jnp.mean(e, axis=-1, keepdims=True)
    mean_en = jnp.mean(e * normed, axis=-1, keepdims=True)
    return scale * (e - mean_e - normed * mean_en)


def gelu_tanh(values):
    return jax.nn.gelu(values, approximate=True)


def head_lanes(x, heads, first, ones_at=None):
    rows, width = x.shape
    wide = jnp.pad(x, ((0, 0), (first, LANES - width - first))).reshape(2, 1, rows // 2, LANES)
    lane = lax.broadcasted_iota(jnp.int32, (1, heads, 1, LANES), 3)
    head = lax.broadcasted_iota(jnp.int32, (1, heads, 1, LANES), 1)
    start = first + head * HEAD_DIM
    here = jnp.logical_and(lane >= start, lane < start + HEAD_DIM)
    out = jnp.where(here, wide, jnp.zeros((), x.dtype))
    if ones_at is not None:
        at = ones_at + 3 * head
        out = jnp.where(jnp.logical_and(lane >= at, lane < at + 3), jnp.ones((), x.dtype), out)
    return out.reshape(2, heads * rows // 2, LANES)


def to_all(x, axis="ulysses"):
    ways = lax.axis_size(axis)
    sent = jnp.broadcast_to(x[None], (ways,) + x.shape)
    return lax.all_to_all(sent, axis, split_axis=0, concat_axis=0, tiled=True)


def summed_at_owner(x, axis="ulysses"):
    ways = lax.axis_size(axis)
    sent = x.astype(BF16).reshape(ways, -1, x.shape[1])
    got = lax.all_to_all(sent, axis, split_axis=0, concat_axis=0, tiled=True)
    return jnp.sum(got.astype(F32), axis=0)


def swapped(x, axis="core"):
    return lax.ppermute(x, axis, [(0, 1), (1, 0)])


def reduced(x, axis):
    ways = lax.axis_size(axis)
    me = lax.axis_index(axis)

    def rows_of(k):
        return lax.dynamic_index_in_dim(x, lax.rem(me + k, ways), axis=0, keepdims=False)

    got = [
        lax.ppermute(rows_of(k).astype(BF16), axis, [(i, (i + k) % ways) for i in range(ways)])
        for k in range(1, ways)
    ]
    total = rows_of(0)
    for g in got:
        total += g.astype(F32)
    return total


def on_device(
    tokens,
    stretch_order,
    ln_gain,
    ln_bias,
    w_qkv,
    qv_bias,
    w_out,
    out_bias,
    w_up,
    up_bias,
    w_down,
    down_bias,
    cotangent,
):
    own_rows, width = tokens.shape
    ways = lax.axis_size("ulysses")
    wide = lax.axis_size(WIDE)
    me = lax.axis_index("ulysses")
    rows = own_rows * ways
    heads = HEADS // ways
    part = width // ways
    held = w_qkv.shape[1]
    ff_held = w_down.shape[1]
    ff_part = ff_held * wide
    pair = 2 * held

    order = stretch_order[0]
    own = lax.dynamic_slice(order, (2 * lax.axis_index(BLK),), (2,))
    count = order.shape[0]
    index = jnp.arange(count, dtype=jnp.int32)
    slots = jnp.sum(jnp.where(order[None, :] == index[:, None], index[None, :], 0), axis=1)
    core = lax.axis_index("core")
    deep = lax.axis_size("z")
    flat = lax.axis_size(("batch", "xlo"))

    small = jnp.concatenate(
        [
            ln_gain,
            ln_bias,
            qv_bias,
            jnp.concatenate([out_bias, down_bias], axis=1),
            up_bias.reshape(2, pair),
        ],
        axis=0,
    )
    qkv_slices = w_qkv[0].reshape(held, 3, ways, part).transpose(2, 0, 1, 3).reshape(ways, held, 3 * part)
    up_slices = w_up[0].reshape(held, wide, ways, ff_held).transpose(2, 0, 1, 3).reshape(ways, held, ff_part)
    first = jnp.concatenate(
        [
            qkv_slices,
            jnp.broadcast_to(small[None], (ways,) + small.shape),
            jnp.zeros((ways, held, width - 3 * part - pair), BF16),
        ],
        axis=2,
    )
    blank = jnp.zeros((ways, 8 - held, width), BF16)
    sent = jnp.concatenate(
        [
            jnp.broadcast_to(tokens[None], (ways,) + tokens.shape),
            first,
            blank,
            up_slices,
            blank,
            jnp.broadcast_to(w_out[0][None], (ways, held, width)),
            blank,
        ],
        axis=1,
    )
    got = lax.all_to_all(sent, "ulysses", split_axis=0, concat_axis=0, tiled=True)
    x = got[:, :own_rows].reshape(rows, width)
    at = own_rows
    piece = got[:, at : at + held, : 3 * part + 64].reshape(ways * held, 3 * part + 64)
    filled = lax.all_gather(piece, WIDE, axis=0, tiled=True)
    ffn = jnp.concatenate(
        [
            got[:, at + 8 : at + 8 + held].reshape(ways * held, width),
            got[:, at + 16 : at + 16 + held].reshape(ways * held, width),
            w_down[0],
        ],
        axis=1,
    )
    w_qkv_u = filled[:, : 3 * part]
    smalls = filled[:, 3 * part : 3 * part + pair].reshape(wide * ways, held, pair).astype(F32)
    gains = smalls[:, 0].reshape(-1)
    shifts = smalls[:, 1].reshape(-1)
    qv_all = smalls[:, 2].reshape(-1)
    out_bias_all = smalls[:, 3, :held].reshape(-1)
    down_bias_all = smalls[:, 3, held:].reshape(-1)
    up_bias_all = smalls[:, 4:].reshape(wide, ways, ff_held)
    up_bias_u = lax.dynamic_index_in_dim(up_bias_all, me, axis=1, keepdims=False).reshape(-1)
    bias_q = lax.dynamic_slice(qv_all, (me * part,), (part,))
    bias_v = lax.dynamic_slice(qv_all, (width + me * part,), (part,))

    n1, r1 = normalized(x.astype(F32))
    h1 = (n1 * gains[:width] + shifts[:width]).astype(BF16)
    proj_bias = jnp.concatenate([bias_q, jnp.zeros((part,), F32), bias_v])
    proj = (mm(h1, w_qkv_u) + proj_bias).astype(BF16)
    q_scaled = proj[:, :part] * jnp.asarray(1.0 / math.sqrt(HEAD_DIM), BF16)
    kv = proj[:, part:]
    kv_all = lax.all_gather(kv, BLK, axis=0, tiled=True)
    q_heads = head_lanes(q_scaled, heads, 0)

    df_own = cotangent.astype(BF16)
    df_own, kv = lax.optimization_barrier((df_own, kv))
    df = to_all(df_own).reshape(rows, width)
    ffn, kv_all, df = lax.optimization_barrier((ffn, kv_all, df))
    ffn_all = lax.all_gather(ffn, WIDE, axis=0, tiled=True)

    ctx_low, ctx, lse = attend(slots, own, q_heads, kv_all, heads)
    ctx_all = to_all(ctx_low)
    q_wide = jnp.pad(q_scaled, ((0, 0), (EXTRA, 0)))
    q_wide, ctx_all = lax.optimization_barrier((q_wide, ctx_all))
    q_all = lax.all_gather(q_wide, BLK, axis=0, tiled=True)
    gain_two = gains[width:]
    vectors = jnp.stack(
        [gain_two, shifts[width:], out_bias_all, up_bias_u] + [jnp.zeros((width,), F32)] * 4
    )
    x2_own, h2, act, du, dh2, down = feed_forward(me[None], x, ctx_all, df, vectors, ffn_all)
    dh2 = summed_at_owner(dh2)
    w_out_u = lax.dynamic_slice(ffn_all, (me * part, width), (part, width))
    g_up_bias = jnp.sum(du.astype(F32), axis=0)
    g_down_bias = jnp.sum(df_own.astype(F32), axis=0)

    n2_own, r2_own = normalized(x2_own)
    dx2 = cotangent + norm_back(dh2, gain_two, n2_own, r2_own)
    g_gain_two = jnp.sum(dh2 * n2_own, axis=0)
    g_shift_two = jnp.sum(dh2, axis=0)
    dc_own, q_all = lax.optimization_barrier((dx2.astype(BF16), q_all))
    g_out_bias = jnp.sum(dc_own.astype(F32), axis=0)
    dc = to_all(dc_own).reshape(rows, width)

    w_out_wide = jnp.pad(w_out_u, ((EXTRA, 0), (0, 0)))
    packed, q_ext, d_ext = prepare(dc, w_out_wide, ctx, lse, q_heads, heads)
    packed_all = lax.all_gather(packed, BLK, axis=0, tiled=True)
    down, packed = lax.optimization_barrier((down, packed))
    result = summed_at_owner(down) + x2_own + down_bias_all
    early, early_sent = weight_grads(core[None], h2, du, act, df, ctx_low, dc, wide, deep)
    early = early + swapped(early_sent).astype(F32)
    early, q_ext = lax.optimization_barrier((early, q_ext))
    early = reduced(early.reshape(deep, flat * early.shape[1], width), "z")
    d_query = query_grad(slots, own, q_ext, d_ext, kv_all, heads)
    early, packed_all = lax.optimization_barrier((early, packed_all))
    early = reduced(early.reshape(flat, -1, width), ("batch", "xlo"))
    k_heads = head_lanes(kv[:, :part], heads, EXTRA, 0)
    v_heads = head_lanes(kv[:, part:], heads, EXTRA, 3 * heads)
    d_key, d_value = key_grad(slots, own, k_heads, v_heads, q_all, packed_all, heads)
    d_proj = jnp.concatenate([d_query, d_key, d_value], axis=1)
    dh1 = summed_at_owner(mm_nt(d_proj, w_qkv_u))
    g_w_qkv = mm_tn(h1, d_proj)
    n1_own, r1_own = normalized(tokens.astype(F32))
    d_tokens = dx2 + norm_back(dh1, gains[:width], n1_own, r1_own)
    g_gain_one = jnp.sum(dh1 * n1_own, axis=0)
    g_shift_one = jnp.sum(dh1, axis=0)

    g_up_rows = early[:ff_held]
    o_w_down = early[ff_held : 2 * ff_held]
    out_rows = early[2 * ff_held : 2 * ff_held + held]
    owners = wide * ways
    o_w_out = lax.ppermute(
        out_rows, ALL, [(w * ways + u, u * wide + w) for w in range(wide) for u in range(ways)]
    )

    d_sums = jnp.sum(d_proj.astype(F32), axis=0)
    g_qv = jnp.zeros((2, ways, part), F32)
    g_qv = lax.dynamic_update_slice(g_qv, d_sums[:part].reshape(1, 1, part), (0, me, 0))
    g_qv = lax.dynamic_update_slice(g_qv, d_sums[2 * part :].reshape(1, 1, part), (1, me, 0))
    g_up_full = jnp.zeros((wide, ways, ff_held), F32)
    g_up_full = lax.dynamic_update_slice(
        g_up_full, g_up_bias.reshape(wide, 1, ff_held), (0, me, 0)
    )
    small_grads = jnp.concatenate(
        [
            jnp.concatenate([g_gain_one, g_gain_two]).reshape(owners, 1, pair),
            jnp.concatenate([g_shift_one, g_shift_two]).reshape(owners, 1, pair),
            g_qv.reshape(owners, 1, pair),
            jnp.concatenate(
                [g_out_bias.reshape(owners, 1, held), g_down_bias.reshape(owners, 1, held)], axis=2
            ),
            g_up_full.reshape(owners, 2, pair),
        ],
        axis=1,
    ).reshape(owners * held, pair)
    late = jnp.concatenate([g_w_qkv, jnp.pad(small_grads, ((0, 0), (0, 64 - pair)))], axis=1)
    late = late.reshape(flat, deep, 2, ways * held, late.shape[1]).transpose(2, 1, 0, 3, 4)
    late_sent = lax.dynamic_index_in_dim(late, 1 - core, axis=0, keepdims=False).astype(BF16)
    late = lax.dynamic_index_in_dim(late, core, axis=0, keepdims=False)
    late = late + swapped(late_sent).astype(F32)
    late = reduced(late.reshape(deep, flat * ways * held, -1), "z")
    late = reduced(late.reshape(flat, ways * held, -1), ("batch", "xlo"))
    last = jnp.concatenate([late, g_up_rows], axis=1).reshape(ways, held, -1)
    last = lax.all_to_all(last, "ulysses", split_axis=0, concat_axis=0, tiled=True)
    o_w_qkv = last[:, :, : 3 * part].reshape(ways, held, 3, part).transpose(1, 2, 0, 3)
    o_small = jnp.sum(last[:, :, 3 * part : 3 * part + pair], axis=0)
    o_w_up = last[:, :, 3 * part + 64 :].reshape(ways, held, wide, ff_held).transpose(1, 2, 0, 3)
    return (
        result,
        d_tokens,
        o_small[0:1],
        o_small[1:2],
        o_w_qkv.reshape(1, held, 3 * width),
        o_small[2:3],
        o_w_out[None],
        o_small[3:4, :held],
        o_w_up.reshape(1, held, -1),
        o_small[4:6].reshape(1, ff_held),
        o_w_down[None],
        o_small[3:4, held:],
    )


def solution(mesh):
    chips_z = mesh.shape["blk"] // 4
    parts = Mesh(
        mesh.devices.reshape(mesh.shape["batch"], 2, chips_z, 2, mesh.shape["ulysses"]), ALL
    )
    rows = P(ALL, None)
    flat = P(None, ALL)
    deep = P(None, ALL, None)
    return jax.shard_map(
        on_device,
        mesh=parts,
        in_specs=(
            rows, P("batch", None), flat, flat, deep, flat, deep, flat, deep, flat, deep, flat, rows,
        ),
        out_specs=(rows, rows, flat, flat, deep, flat, deep, flat, deep, flat, deep, flat),
        check_vma=False,
    )
```

```python
import functools
import math

import jax
import jax.numpy as jnp
from jax import lax
from jax.experimental import pallas as pl
from jax.experimental.pallas import tpu as pltpu
from jax.sharding import Mesh, PartitionSpec as P

HEADS = 12
HEAD_DIM = 64
NORM_EPS = 1e-05
FLOOR = -1e25
HIGHEST_ABOVE = 60.0
LANES = 256
EXTRA = 64
BELOW_FLOOR = -1e30
BLK = ("xlo", "z", "core")
WIDE = ("batch", "xlo", "z", "core")
ALL = ("batch", "xlo", "z", "core", "ulysses")
BF16 = jnp.bfloat16
F32 = jnp.float32
NT = (((1,), (1,)), ((), ()))
VMEM_LIMIT = 60 * 1024 * 1024


def mm(a, b):
    return jnp.dot(a, b, preferred_element_type=F32)


def mm_nt(a, b):
    return lax.dot_general(a, b, NT, preferred_element_type=F32)


def mm_tn(a, b):
    return lax.dot_general(a, b, (((0,), (0,)), ((), ())), preferred_element_type=F32)


def stretch(index, half):
    return pl.ds(pl.multiple_of(index * half, half), half)


def lanes_of(rows):
    return lax.broadcasted_iota(jnp.int32, (rows, LANES), 1)


def ones_after(k, first):
    return jnp.where(lanes_of(k.shape[0]) < first, k, jnp.ones_like(k))


def ones_before(v):
    return jnp.where(lanes_of(v.shape[0]) < EXTRA, jnp.ones_like(v), v)


def three(x):
    high = x.astype(BF16).astype(F32)
    mid = (x - high).astype(BF16).astype(F32)
    return high, mid, x - high - mid


def causal(half, heads, keys_first):
    rows = lax.broadcasted_iota(jnp.int32, (heads * half, half), 0) & (half - 1)
    cols = lax.broadcasted_iota(jnp.int32, (heads * half, half), 1)
    return rows <= cols if keys_first else cols <= rows


def merged_heads(stacked, half, heads, first):
    lane = lanes_of(half)
    out = stacked[:half]
    for h in range(1, heads):
        out = jnp.where(lane < first + h * HEAD_DIM, out, stacked[h * half : (h + 1) * half])
    return out


def in_groups(first, count, tiles):
    def eight(i, _):
        tiles([first + 8 * i + j for j in range(8)])
        return 0

    lax.fori_loop(0, count // 8, eight, 0)
    for size in (4, 2, 1):

        @pl.when((count & size) != 0)
        def _():
            begin = first + (count & ~(2 * size - 1))
            tiles([begin + j for j in range(size)])


def one_ahead(items, produce, consume):
    ready = produce(items[0])
    for n, item in enumerate(items):
        now = ready
        if n + 1 < len(items):
            ready = produce(items[n + 1])
        consume(item, now)


def attend_kernel(
    slots, own, q_heads, kv, ctx_low, ctx, lse, shift, total, q_ext, top, *, half, heads
):
    deep = heads * half
    lane = lanes_of(deep)

    def one_half(part, _):
        rank_own = own[part]
        mask = causal(half, heads, False)
        here = stretch(slots[rank_own], half)
        scores = jnp.where(mask, mm_nt(q_heads[part], kv[here, :LANES]), BELOW_FLOOR)
        first = jnp.max(scores, axis=1, keepdims=True).astype(BF16).astype(F32)
        shift[...] = first
        q_ext[...] = jnp.where(lane == heads * HEAD_DIM, -first, q_heads[part].astype(F32)).astype(
            BF16
        )
        top[...] = jnp.zeros_like(top)
        total[...] = mm(jnp.exp(scores - first).astype(BF16), ones_before(kv[here, 128:]))

        def tiles(ranks):
            at = [stretch(slots[r], half) for r in ranks]
            added = [total[...], top[...]]

            def produce(a):
                return mm_nt(q_ext[...], ones_after(kv[a, :LANES], heads * HEAD_DIM))

            def consume(a, above):
                added[1] = jnp.maximum(added[1], jnp.max(above.reshape(deep // 8, 8, half), axis=0))
                added[0] += mm(jnp.exp(above).astype(BF16), ones_before(kv[a, 128:]))

            one_ahead(at, produce, consume)
            total[...] = added[0]
            top[...] = added[1]

        in_groups(0, rank_own, tiles)

        @pl.when(jnp.logical_not(jnp.max(top[...]) < HIGHEST_ABOVE))
        def _():
            shift[...] = jnp.full_like(shift, FLOOR)
            total[...] = jnp.zeros_like(total)

            def again(rank, _):
                a = stretch(slots[rank], half)
                allowed = jnp.logical_or(mask, rank < rank_own)
                scores = jnp.where(allowed, mm_nt(q_heads[part], kv[a, :LANES]), BELOW_FLOOR)
                new = jnp.maximum(shift[...], jnp.max(scores, axis=1, keepdims=True))
                total[...] = total[...] * jnp.exp(shift[...] - new) + mm(
                    jnp.exp(scores - new).astype(BF16), ones_before(kv[a, 128:])
                )
                shift[...] = new
                return 0

            lax.fori_loop(0, rank_own + 1, again, 0)

        row_sum = total[:, :1]
        lse[part] = shift[...] + jnp.log(row_sum)
        done = merged_heads(total[...] / row_sum, half, heads, EXTRA)
        rows = stretch(part, half)
        ctx[rows, :] = done
        ctx_low[:, rows] = done.T[EXTRA:, :].astype(BF16)
        return 0

    lax.fori_loop(0, 2, one_half, 0)


def query_grad_kernel(slots, own, q_ext, d_ext, kv, d_query, total, *, half, heads):
    def one_half(part, _):
        rank_own = own[part]
        total[...] = jnp.zeros_like(total)

        def tiles(ranks, mask=None):
            at = [stretch(slots[r], half) for r in ranks]
            added = [total[...]]

            def produce(a):
                return (
                    mm_nt(q_ext[part], ones_after(kv[a, :LANES], heads * HEAD_DIM)),
                    mm_nt(d_ext[part], ones_before(kv[a, 128:])),
                )

            def consume(a, ready):
                probs = jnp.exp(ready[0])
                if mask is not None:
                    probs = jnp.where(mask, probs, 0.0)
                added[0] += mm((probs * ready[1]).astype(BF16), kv[a, :LANES])

            one_ahead(at, produce, consume)
            total[...] = added[0]

        in_groups(0, rank_own, tiles)
        tiles([rank_own], causal(half, heads, False))
        done = merged_heads(total[...], half, heads, 0)[:, : heads * HEAD_DIM]
        d_query[stretch(part, half), :] = (done * (1.0 / math.sqrt(HEAD_DIM))).astype(BF16)
        return 0

    lax.fori_loop(0, 2, one_half, 0)


def key_grad_kernel(
    slots, own, k_heads, v_heads, q_all, p_all, d_key, d_value, k_sum, v_sum, *, half, heads
):
    count = slots.shape[0]
    lane = lanes_of(half)

    def one_half(part, _):
        rank_own = own[part]
        k_sum[...] = jnp.zeros_like(k_sum)
        v_sum[...] = jnp.zeros_like(v_sum)

        def tiles(ranks, mask=None):
            at = [stretch(slots[r], half) for r in ranks]
            added = [k_sum[...], v_sum[...]]

            def produce(a):
                return (
                    mm_nt(k_heads[part], jnp.where(lane < EXTRA, p_all[a, :], q_all[a, :])),
                    mm_nt(v_heads[part], p_all[a, :]),
                )

            def consume(a, ready):
                probs = jnp.exp(ready[0])
                if mask is not None:
                    probs = jnp.where(mask, probs, 0.0)
                added[1] += mm(probs.astype(BF16), p_all[a, :])
                added[0] += mm((probs * ready[1]).astype(BF16), q_all[a, :])

            one_ahead(at, produce, consume)
            k_sum[...], v_sum[...] = added

        tiles([rank_own], causal(half, heads, True))
        in_groups(rank_own + 1, count - 1 - rank_own, tiles)
        rows = stretch(part, half)
        d_key[rows, :] = merged_heads(k_sum[...], half, heads, EXTRA)[:, EXTRA:].astype(BF16)
        d_value[rows, :] = merged_heads(v_sum[...], half, heads, EXTRA)[:, EXTRA:].astype(BF16)
        return 0

    lax.fori_loop(0, 2, one_half, 0)


def prepare_kernel(dc, w_out, ctx, lse, q_heads, packed, q_ext, d_ext, *, half, heads):
    lane = lanes_of(half)
    d_ctx = mm_nt(dc[...], w_out[...]).astype(BF16)
    for part in range(2):
        rows = slice(part * half, (part + 1) * half)
        grads = d_ctx[rows, :]
        terms = grads.astype(F32) * ctx[rows, :]
        extra = grads.astype(F32)
        for h in range(heads):
            deep = slice(h * half, (h + 1) * half)
            first = EXTRA + h * HEAD_DIM
            here = jnp.logical_and(lane >= first, lane < first + HEAD_DIM)
            delta = jnp.sum(jnp.where(here, terms, 0.0), axis=1, keepdims=True)
            minus_lse = three(-lse[part, deep, :])
            minus_delta = three(-delta)
            q_new = q_heads[part, deep, :].astype(F32)
            d_new = jnp.where(here, grads.astype(F32), 0.0)
            for i in range(3):
                q_new = jnp.where(lane == heads * HEAD_DIM + i, minus_lse[i], q_new)
                d_new = jnp.where(lane == i, minus_delta[i], d_new)
                extra = jnp.where(lane == 3 * h + i, minus_lse[i], extra)
                extra = jnp.where(lane == 3 * (heads + h) + i, minus_delta[i], extra)
            q_ext[part, deep, :] = q_new.astype(BF16)
            d_ext[part, deep, :] = d_new.astype(BF16)
        packed[rows, :] = extra.astype(BF16)


def whole(shape):
    return pl.BlockSpec(shape, lambda i, *_: (0,) * len(shape))


def params():
    return pltpu.CompilerParams(
        dimension_semantics=("arbitrary",), vmem_limit_bytes=VMEM_LIMIT
    )


def cost(rows, keys, heads, products):
    area = rows * keys * heads
    return pl.CostEstimate(
        flops=2 * area * 256 * products, bytes_accessed=keys * 768, transcendentals=area
    )


def call(kernel, name, scalars, arrays, outs, scratch, estimate, **static):
    return pl.pallas_call(
        functools.partial(kernel, **static),
        out_shape=tuple(jax.ShapeDtypeStruct(s, t) for s, t in outs),
        grid_spec=pltpu.PrefetchScalarGridSpec(
            num_scalar_prefetch=len(scalars),
            grid=(1,),
            in_specs=[whole(a.shape) for a in arrays],
            out_specs=[whole(s) for s, _ in outs],
            scratch_shapes=[pltpu.VMEM(s, t) for s, t in scratch],
        ),
        compiler_params=params(),
        cost_estimate=estimate,
        name=name,
    )(*scalars, *arrays)


def attend(slots, own, q_heads, kv, heads):
    _, deep, _ = q_heads.shape
    half = deep // heads
    width = heads * HEAD_DIM
    return call(
        attend_kernel, "attend", (slots, own), (q_heads, kv),
        [((width, 2 * half), BF16), ((2 * half, LANES), F32), ((2, deep, 1), F32)],
        [((deep, 1), F32), ((deep, LANES), F32), ((deep, LANES), BF16), ((8, half), F32)],
        cost(2 * half, kv.shape[0], heads, 2), half=half, heads=heads,
    )


def prepare(dc, w_out, ctx, lse, q_heads, heads):
    _, deep, _ = q_heads.shape
    half = deep // heads
    return call(
        prepare_kernel, "prepare", (), (dc, w_out, ctx, lse, q_heads),
        [((2 * half, LANES), BF16), (q_heads.shape, BF16), (q_heads.shape, BF16)], [],
        pl.CostEstimate(flops=2 * dc.size * LANES, bytes_accessed=4 * q_heads.size, transcendentals=0),
        half=half, heads=heads,
    )


def query_grad(slots, own, q_ext, d_ext, kv, heads):
    _, deep, _ = q_ext.shape
    half = deep // heads
    return call(
        query_grad_kernel, "query_grad", (slots, own), (q_ext, d_ext, kv),
        [((2 * half, heads * HEAD_DIM), BF16)], [((deep, LANES), F32)],
        cost(2 * half, kv.shape[0], heads, 3), half=half, heads=heads,
    )[0]


def key_grad(slots, own, k_heads, v_heads, q_all, p_all, heads):
    _, deep, _ = k_heads.shape
    half = deep // heads
    out = ((2 * half, heads * HEAD_DIM), BF16)
    return call(
        key_grad_kernel, "key_grad", (slots, own), (k_heads, v_heads, q_all, p_all),
        [out, out], [((deep, LANES), F32)] * 2,
        cost(2 * half, q_all.shape[0], heads, 4), half=half, heads=heads,
    )


def feed_forward_kernel(
    me, x, ctx, df, vectors, w_up, w_out, w_down, x2_own, h2, act, du, dh2, down
):
    total = x[...].astype(F32) + vectors[2:3, :] + mm_tn(ctx[...], w_out[...])

    @pl.when(pl.program_id(0) == me[0])
    def _():
        x2_own[...] = total

    normed, _ = normalized(total)
    h2_low = (normed * vectors[0:1, :] + vectors[1:2, :]).astype(BF16)
    h2[...] = h2_low
    up = mm(h2_low, w_up[...]) + vectors[3:4, :]
    bend = math.sqrt(2.0 / math.pi)
    square = up * up
    turn = jnp.tanh(bend * (up + 0.044715 * square * up))
    half = 0.5 * (1.0 + turn)
    act_low = (up * half).astype(BF16)
    act[...] = act_low
    down[...] = mm(act_low, w_down[...])
    slope = half + 0.5 * up * (1.0 - turn * turn) * (bend * (1.0 + 3 * 0.044715 * square))
    du_low = (slope * mm_nt(df[...], w_down[...])).astype(BF16)
    du[...] = du_low
    dh2[...] = mm_nt(du_low, w_up[...]).astype(BF16)


def feed_forward(me, both, ctx, vectors, weights, ways):
    rows = both.shape[0]
    width = both.shape[1] // 2
    step = rows // ways

    def along(c):
        return pl.BlockSpec((step, width), lambda i, *_: (i, c))

    def third(c):
        return pl.BlockSpec((weights.shape[0], width), lambda i, *_: (0, c))

    flat = jax.ShapeDtypeStruct((rows, width), BF16)
    wide = jax.ShapeDtypeStruct((rows, width), F32)
    return pl.pallas_call(
        feed_forward_kernel,
        out_shape=(jax.ShapeDtypeStruct((step, width), F32), flat, flat, flat, flat, wide),
        grid_spec=pltpu.PrefetchScalarGridSpec(
            num_scalar_prefetch=1,
            grid=(ways,),
            in_specs=[
                along(0),
                pl.BlockSpec((width, step), lambda i, *_: (0, i)),
                along(1),
                whole(vectors.shape),
                third(0),
                third(1),
                third(2),
            ],
            out_specs=[whole((step, width))] + [along(0)] * 5,
        ),
        compiler_params=params(),
        cost_estimate=pl.CostEstimate(
            flops=10 * rows * width * width, bytes_accessed=6 * width * width, transcendentals=rows * width
        ),
        name="feed_forward",
    )(me, both, ctx, both, vectors, weights, weights, weights)


def weight_grads_kernel(h2, du, act, df, ctx, dc, out, g_out):
    owners, rows, width = out.shape
    each = h2.shape[1] // owners
    few = ctx.shape[0] // owners
    chunk = h2.shape[1] // 2
    for i in range(2):
        cols = slice(i * chunk, (i + 1) * chunk)
        mine = slice(i * owners // 2, (i + 1) * owners // 2)
        shape = (owners // 2, each, width)
        out[mine, :each, :] = mm_tn(h2[:, cols], du[...]).reshape(shape)
        out[mine, each : 2 * each, :] = mm_tn(act[:, cols], df[...]).reshape(shape)
    g_out[...] = mm(ctx[...], dc[...])
    out[:, 2 * each :, :] = jnp.zeros((owners, rows - 2 * each, width), F32)
    for w in range(owners):
        out[w, 2 * each : 2 * each + few, :] = g_out[w * few : (w + 1) * few, :]


def weight_grads(h2, du, act, both, ctx, dc, owners):
    count, width = du.shape
    units = h2.shape[1]
    shape = (owners, 2 * units // owners + 8, width)
    out = pl.pallas_call(
        weight_grads_kernel,
        out_shape=jax.ShapeDtypeStruct(shape, F32),
        grid_spec=pltpu.PrefetchScalarGridSpec(
            num_scalar_prefetch=0,
            grid=(1,),
            in_specs=[
                whole(h2.shape),
                whole(du.shape),
                whole(act.shape),
                pl.BlockSpec((count, width), lambda i, *_: (0, 1)),
                whole(ctx.shape),
                whole(dc.shape),
            ],
            out_specs=whole(shape),
            scratch_shapes=[pltpu.VMEM((ctx.shape[0], width), F32)],
        ),
        compiler_params=params(),
        cost_estimate=pl.CostEstimate(
            flops=4 * h2.size * width, bytes_accessed=8 * units * width, transcendentals=0
        ),
        name="weight_grads",
    )(h2, du, act, both, ctx, dc)
    return out.reshape(shape[0] * shape[1], width)


def normalized(values):
    mean = jnp.mean(values, axis=-1, keepdims=True)
    centered = values - mean
    spread = jnp.mean(centered * centered, axis=-1, keepdims=True)
    scale = lax.rsqrt(spread + NORM_EPS)
    return centered * scale, scale


def norm_back(grad, gain, normed, scale):
    e = grad * gain
    mean_e = jnp.mean(e, axis=-1, keepdims=True)
    mean_en = jnp.mean(e * normed, axis=-1, keepdims=True)
    return scale * (e - mean_e - normed * mean_en)


def gelu_tanh(values):
    return jax.nn.gelu(values, approximate=True)


def head_lanes(x, heads, first, ones_at=None):
    rows, width = x.shape
    wide = jnp.pad(x, ((0, 0), (first, LANES - width - first))).reshape(2, 1, rows // 2, LANES)
    lane = lax.broadcasted_iota(jnp.int32, (1, heads, 1, LANES), 3)
    head = lax.broadcasted_iota(jnp.int32, (1, heads, 1, LANES), 1)
    start = first + head * HEAD_DIM
    here = jnp.logical_and(lane >= start, lane < start + HEAD_DIM)
    out = jnp.where(here, wide, jnp.zeros((), x.dtype))
    if ones_at is not None:
        at = ones_at + 3 * head
        out = jnp.where(jnp.logical_and(lane >= at, lane < at + 3), jnp.ones((), x.dtype), out)
    return out.reshape(2, heads * rows // 2, LANES)


def to_all(x, axis="ulysses"):
    ways = lax.axis_size(axis)
    sent = jnp.broadcast_to(x[None], (ways,) + x.shape)
    return lax.all_to_all(sent, axis, split_axis=0, concat_axis=0, tiled=True)


def summed_at_owner(x, axis="ulysses"):
    ways = lax.axis_size(axis)
    sent = x.astype(BF16).reshape(ways, -1, x.shape[1])
    got = lax.all_to_all(sent, axis, split_axis=0, concat_axis=0, tiled=True)
    return jnp.sum(got.astype(F32), axis=0)


def reduced(x, axis):
    ways = lax.axis_size(axis)
    me = lax.axis_index(axis)

    def rows_of(k):
        return lax.dynamic_index_in_dim(x, lax.rem(me + k, ways), axis=0, keepdims=False)

    got = [
        lax.ppermute(rows_of(k).astype(BF16), axis, [(i, (i + k) % ways) for i in range(ways)])
        for k in range(1, ways)
    ]
    total = rows_of(0)
    for g in got:
        total += g.astype(F32)
    return total


def on_device(
    tokens,
    stretch_order,
    ln_gain,
    ln_bias,
    w_qkv,
    qv_bias,
    w_out,
    out_bias,
    w_up,
    up_bias,
    w_down,
    down_bias,
    cotangent,
):
    own_rows, width = tokens.shape
    ways = lax.axis_size("ulysses")
    wide = lax.axis_size(WIDE)
    me = lax.axis_index("ulysses")
    rows = own_rows * ways
    heads = HEADS // ways
    part = width // ways
    held = w_qkv.shape[1]
    ff_held = w_down.shape[1]
    ff_part = ff_held * wide
    pair = 2 * held

    order = stretch_order[0]
    own = lax.dynamic_slice(order, (2 * lax.axis_index(BLK),), (2,))
    count = order.shape[0]
    index = jnp.arange(count, dtype=jnp.int32)
    slots = jnp.sum(jnp.where(order[None, :] == index[:, None], index[None, :], 0), axis=1)

    small = jnp.concatenate(
        [
            ln_gain,
            ln_bias,
            qv_bias,
            jnp.concatenate([out_bias, down_bias], axis=1),
            up_bias.reshape(2, pair),
        ],
        axis=0,
    )
    qkv_slices = w_qkv[0].reshape(held, 3, ways, part).transpose(2, 0, 1, 3).reshape(ways, held, 3 * part)
    up_slices = w_up[0].reshape(held, wide, ways, ff_held).transpose(2, 0, 1, 3).reshape(ways, held, ff_part)
    df_own = cotangent.astype(BF16)
    both = lax.all_gather(jnp.concatenate([tokens, df_own], axis=1), "ulysses", axis=0, tiled=True)
    first = jnp.concatenate(
        [
            qkv_slices,
            jnp.broadcast_to(small[None], (ways,) + small.shape),
            jnp.zeros((ways, held, width - 3 * part - pair), BF16),
        ],
        axis=2,
    )
    blank = jnp.zeros((ways, 8 - held, width), BF16)
    wide_out = jnp.broadcast_to(w_out[0][None], (ways, held, width))
    sent = jnp.concatenate([first, blank, up_slices, blank, wide_out, blank], axis=1)
    got = lax.all_to_all(sent, "ulysses", split_axis=0, concat_axis=0, tiled=True)
    piece = got[:, :held, : 3 * part + 64].reshape(ways * held, 3 * part + 64)
    filled = lax.all_gather(piece, WIDE, axis=0, tiled=True)
    ffn = jnp.concatenate(
        [
            got[:, 8 : 8 + held].reshape(ways * held, width),
            got[:, 16 : 16 + held].reshape(ways * held, width),
            w_down[0],
        ],
        axis=1,
    )
    w_qkv_u = filled[:, : 3 * part]
    smalls = filled[:, 3 * part : 3 * part + pair].reshape(wide * ways, held, pair).astype(F32)
    gains = smalls[:, 0].reshape(-1)
    shifts = smalls[:, 1].reshape(-1)
    qv_all = smalls[:, 2].reshape(-1)
    out_bias_all = smalls[:, 3, :held].reshape(-1)
    down_bias_all = smalls[:, 3, held:].reshape(-1)
    up_bias_all = smalls[:, 4:].reshape(wide, ways, ff_held)
    up_bias_u = lax.dynamic_index_in_dim(up_bias_all, me, axis=1, keepdims=False).reshape(-1)
    bias_q = lax.dynamic_slice(qv_all, (me * part,), (part,))
    bias_v = lax.dynamic_slice(qv_all, (width + me * part,), (part,))

    n1, _ = normalized(both[:, :width].astype(F32))
    h1 = (n1 * gains[:width] + shifts[:width]).astype(BF16)
    proj_bias = jnp.concatenate([bias_q, jnp.zeros((part,), F32), bias_v])
    proj = (mm(h1, w_qkv_u) + proj_bias).astype(BF16)
    q_scaled = proj[:, :part] * jnp.asarray(1.0 / math.sqrt(HEAD_DIM), BF16)
    kv = proj[:, part:]
    kv_all = lax.all_gather(kv, BLK, axis=0, tiled=True)
    q_heads = head_lanes(q_scaled, heads, 0)

    ffn, kv_all = lax.optimization_barrier((ffn, kv_all))
    ffn_all = lax.all_gather(ffn, WIDE, axis=0, tiled=True)

    ctx_low, ctx, lse = attend(slots, own, q_heads, kv_all, heads)
    ctx_all = to_all(ctx_low).reshape(width, rows)
    q_wide = jnp.pad(q_scaled, ((0, 0), (EXTRA, 0)))
    q_wide, ctx_all = lax.optimization_barrier((q_wide, ctx_all))
    q_all = lax.all_gather(q_wide, BLK, axis=0, tiled=True)
    gain_two = gains[width:]
    vectors = jnp.stack(
        [gain_two, shifts[width:], out_bias_all, up_bias_u] + [jnp.zeros((width,), F32)] * 4
    )
    x2_own, h2, act, du, dh2, down = feed_forward(
        me[None], both, ctx_all, vectors, ffn_all, ways
    )
    dh2 = summed_at_owner(dh2)
    ctx_rows = lax.dynamic_index_in_dim(
        ctx_all.reshape(wide, ways, held, rows), me, axis=1, keepdims=False
    ).reshape(part, rows)
    w_out_u = lax.dynamic_slice(ffn_all, (me * part, width), (part, width))
    g_up_bias = jnp.sum(du.astype(F32), axis=0)
    g_down_bias = jnp.sum(df_own.astype(F32), axis=0)

    n2_own, r2_own = normalized(x2_own)
    dx2 = cotangent + norm_back(dh2, gain_two, n2_own, r2_own)
    g_gain_two = jnp.sum(dh2 * n2_own, axis=0)
    g_shift_two = jnp.sum(dh2, axis=0)
    dc_own = dx2.astype(BF16)
    g_out_bias = jnp.sum(dc_own.astype(F32), axis=0)
    dc = to_all(dc_own).reshape(rows, width)
    dc, q_all = lax.optimization_barrier((dc, q_all))

    w_out_wide = jnp.pad(w_out_u, ((EXTRA, 0), (0, 0)))
    packed, q_ext, d_ext = prepare(dc, w_out_wide, ctx, lse, q_heads, heads)
    packed_all = lax.all_gather(packed, BLK, axis=0, tiled=True)
    down, packed = lax.optimization_barrier((down, packed))
    result = reduced(down.reshape(ways, own_rows, width), "ulysses") + x2_own + down_bias_all
    early = weight_grads(h2, du, act, both, ctx_rows, dc, wide)
    d_query = query_grad(slots, own, q_ext, d_ext, kv_all, heads)
    early, packed_all, d_query = lax.optimization_barrier((early, packed_all, d_query))
    early = lax.psum_scatter(early, WIDE, scatter_dimension=0, tiled=True)
    k_heads = head_lanes(kv[:, :part], heads, EXTRA, 0)
    v_heads = head_lanes(kv[:, part:], heads, EXTRA, 3 * heads)
    d_key, d_value = key_grad(slots, own, k_heads, v_heads, q_all, packed_all, heads)
    d_proj = jnp.concatenate([d_query, d_key, d_value], axis=1)
    dh1_terms = mm_nt(d_proj, w_qkv_u)
    dh1 = summed_at_owner(dh1_terms)
    g_w_qkv = mm_tn(h1, d_proj)
    n1_own, r1_own = normalized(tokens.astype(F32))
    d_tokens = dx2 + norm_back(dh1, gains[:width], n1_own, r1_own)
    g_gain_one = jnp.sum(dh1_terms * n1, axis=0)
    g_shift_one = jnp.sum(dh1_terms, axis=0)

    owners = wide * ways
    d_sums = jnp.sum(d_proj.astype(F32), axis=0)
    g_qv = jnp.zeros((2, ways, part), F32)
    g_qv = lax.dynamic_update_slice(g_qv, d_sums[:part].reshape(1, 1, part), (0, me, 0))
    g_qv = lax.dynamic_update_slice(g_qv, d_sums[2 * part :].reshape(1, 1, part), (1, me, 0))
    g_up_full = jnp.zeros((wide, ways, ff_held), F32)
    g_up_full = lax.dynamic_update_slice(
        g_up_full, g_up_bias.reshape(wide, 1, ff_held), (0, me, 0)
    )
    small_grads = jnp.concatenate(
        [
            jnp.concatenate([g_gain_one, g_gain_two]).reshape(owners, 1, pair),
            jnp.concatenate([g_shift_one, g_shift_two]).reshape(owners, 1, pair),
            g_qv.reshape(owners, 1, pair),
            jnp.concatenate(
                [g_out_bias.reshape(owners, 1, held), g_down_bias.reshape(owners, 1, held)], axis=2
            ),
            g_up_full.reshape(owners, 2, pair),
        ],
        axis=1,
    ).reshape(owners * held, pair)
    late = jnp.concatenate([g_w_qkv, jnp.pad(small_grads, ((0, 0), (0, 64 - pair)))], axis=1)
    late = summed_at_owner(late, WIDE)
    last = jnp.concatenate([late, early[:ff_held]], axis=1).reshape(ways, held, -1)
    last = lax.all_to_all(last, "ulysses", split_axis=0, concat_axis=0, tiled=True)
    o_w_qkv = last[:, :, : 3 * part].reshape(ways, held, 3, part).transpose(1, 2, 0, 3)
    o_small = jnp.sum(last[:, :, 3 * part : 3 * part + pair], axis=0)
    o_w_up = last[:, :, 3 * part + 64 :].reshape(ways, held, wide, ff_held).transpose(1, 2, 0, 3)
    return (
        result,
        d_tokens,
        o_small[0:1],
        o_small[1:2],
        o_w_qkv.reshape(1, held, 3 * width),
        o_small[2:3],
        early[None, 2 * ff_held : 2 * ff_held + held],
        o_small[3:4, :held],
        o_w_up.reshape(1, held, -1),
        o_small[4:6].reshape(1, ff_held),
        early[None, ff_held : 2 * ff_held],
        o_small[3:4, held:],
    )


def solution(mesh):
    chips_z = mesh.shape["blk"] // 4
    parts = Mesh(
        mesh.devices.reshape(mesh.shape["batch"], 2, chips_z, 2, mesh.shape["ulysses"]), ALL
    )
    rows = P(ALL, None)
    flat = P(None, ALL)
    deep = P(None, ALL, None)
    return jax.shard_map(
        on_device,
        mesh=parts,
        in_specs=(
            rows, P("batch", None), flat, flat, deep, flat, deep, flat, deep, flat, deep, flat, rows,
        ),
        out_specs=(rows, rows, flat, flat, deep, flat, deep, flat, deep, flat, deep, flat),
        check_vma=False,
    )
```

```python
import functools
import math

import jax
import jax.numpy as jnp
from jax import lax
from jax.experimental import pallas as pl
from jax.experimental.pallas import tpu as pltpu
from jax.sharding import Mesh, PartitionSpec as P

HEADS = 12
HEAD_DIM = 64
NORM_EPS = 1e-05
FLOOR = -1e25
HIGHEST_ABOVE = 60.0
LANES = 256
EXTRA = 64
BELOW_FLOOR = -1e30
BLK = ("xlo", "z", "core")
CHIPS = ("batch", "xlo", "z")
WIDE = ("batch", "xlo", "z", "core")
ALL = ("batch", "xlo", "z", "core", "ulysses")
BF16 = jnp.bfloat16
F32 = jnp.float32
NT = (((1,), (1,)), ((), ()))
VMEM_LIMIT = 60 * 1024 * 1024


def mm(a, b):
    return jnp.dot(a, b, preferred_element_type=F32)


def mm_nt(a, b):
    return lax.dot_general(a, b, NT, preferred_element_type=F32)


def mm_tn(a, b):
    return lax.dot_general(a, b, (((0,), (0,)), ((), ())), preferred_element_type=F32)


def stretch(index, half):
    return pl.ds(pl.multiple_of(index * half, half), half)


def lanes_of(rows):
    return lax.broadcasted_iota(jnp.int32, (rows, LANES), 1)


def ones_after(k, first):
    return jnp.where(lanes_of(k.shape[0]) < first, k, jnp.ones_like(k))


def ones_before(v):
    return jnp.where(lanes_of(v.shape[0]) < EXTRA, jnp.ones_like(v), v)


def three(x):
    high = x.astype(BF16).astype(F32)
    mid = (x - high).astype(BF16).astype(F32)
    return high, mid, x - high - mid


def causal(half, heads, keys_first):
    rows = lax.broadcasted_iota(jnp.int32, (heads * half, half), 0) & (half - 1)
    cols = lax.broadcasted_iota(jnp.int32, (heads * half, half), 1)
    return rows <= cols if keys_first else cols <= rows


def merged_heads(stacked, half, heads, first):
    lane = lanes_of(half)
    out = stacked[:half]
    for h in range(1, heads):
        out = jnp.where(lane < first + h * HEAD_DIM, out, stacked[h * half : (h + 1) * half])
    return out


def in_groups(first, count, tiles):
    def eight(i, _):
        tiles([first + 8 * i + j for j in range(8)])
        return 0

    lax.fori_loop(0, count // 8, eight, 0)
    for size in (4, 2, 1):

        @pl.when((count & size) != 0)
        def _():
            begin = first + (count & ~(2 * size - 1))
            tiles([begin + j for j in range(size)])


def one_ahead(items, produce, consume):
    ready = produce(items[0])
    for n, item in enumerate(items):
        now = ready
        if n + 1 < len(items):
            ready = produce(items[n + 1])
        consume(item, now)


def attend_kernel(
    slots, own, q_heads, kv, ctx_low, ctx, lse, shift, total, q_ext, top, *, half, heads
):
    deep = heads * half
    lane = lanes_of(deep)

    def one_half(part, _):
        rank_own = own[part]
        mask = causal(half, heads, False)
        here = stretch(slots[rank_own], half)
        scores = jnp.where(mask, mm_nt(q_heads[part], kv[here, :LANES]), BELOW_FLOOR)
        first = jnp.max(scores, axis=1, keepdims=True).astype(BF16).astype(F32)
        shift[...] = first
        q_ext[...] = jnp.where(lane == heads * HEAD_DIM, -first, q_heads[part].astype(F32)).astype(
            BF16
        )
        top[...] = jnp.zeros_like(top)
        total[...] = mm(jnp.exp(scores - first).astype(BF16), ones_before(kv[here, 128:]))

        def tiles(ranks):
            at = [stretch(slots[r], half) for r in ranks]
            added = [total[...], top[...]]

            def produce(a):
                return mm_nt(q_ext[...], ones_after(kv[a, :LANES], heads * HEAD_DIM))

            def consume(a, above):
                added[1] = jnp.maximum(added[1], jnp.max(above.reshape(deep // 8, 8, half), axis=0))
                added[0] += mm(jnp.exp(above).astype(BF16), ones_before(kv[a, 128:]))

            one_ahead(at, produce, consume)
            total[...] = added[0]
            top[...] = added[1]

        in_groups(0, rank_own, tiles)

        @pl.when(jnp.logical_not(jnp.max(top[...]) < HIGHEST_ABOVE))
        def _():
            shift[...] = jnp.full_like(shift, FLOOR)
            total[...] = jnp.zeros_like(total)

            def again(rank, _):
                a = stretch(slots[rank], half)
                allowed = jnp.logical_or(mask, rank < rank_own)
                scores = jnp.where(allowed, mm_nt(q_heads[part], kv[a, :LANES]), BELOW_FLOOR)
                new = jnp.maximum(shift[...], jnp.max(scores, axis=1, keepdims=True))
                total[...] = total[...] * jnp.exp(shift[...] - new) + mm(
                    jnp.exp(scores - new).astype(BF16), ones_before(kv[a, 128:])
                )
                shift[...] = new
                return 0

            lax.fori_loop(0, rank_own + 1, again, 0)

        row_sum = total[:, :1]
        lse[part] = shift[...] + jnp.log(row_sum)
        done = merged_heads(total[...] / row_sum, half, heads, EXTRA)
        rows = stretch(part, half)
        ctx[rows, :] = done
        ctx_low[:, rows] = done.T[EXTRA:, :].astype(BF16)
        return 0

    lax.fori_loop(0, 2, one_half, 0)


def query_grad_kernel(slots, own, q_ext, d_ext, kv, d_query, total, *, half, heads):
    def one_half(part, _):
        rank_own = own[part]
        total[...] = jnp.zeros_like(total)

        def tiles(ranks, mask=None):
            at = [stretch(slots[r], half) for r in ranks]
            added = [total[...]]

            def produce(a):
                return (
                    mm_nt(q_ext[part], ones_after(kv[a, :LANES], heads * HEAD_DIM)),
                    mm_nt(d_ext[part], ones_before(kv[a, 128:])),
                )

            def consume(a, ready):
                probs = jnp.exp(ready[0])
                if mask is not None:
                    probs = jnp.where(mask, probs, 0.0)
                added[0] += mm((probs * ready[1]).astype(BF16), kv[a, :LANES])

            one_ahead(at, produce, consume)
            total[...] = added[0]

        in_groups(0, rank_own, tiles)
        tiles([rank_own], causal(half, heads, False))
        done = merged_heads(total[...], half, heads, 0)
        d_query[stretch(part, half), :] = (done * (1.0 / math.sqrt(HEAD_DIM))).astype(BF16)
        return 0

    lax.fori_loop(0, 2, one_half, 0)


def key_grad_kernel(
    slots, own, k_heads, v_heads, q_all, p_all, d_key, d_value, k_sum, v_sum, *, half, heads
):
    count = slots.shape[0]
    lane = lanes_of(half)

    def one_half(part, _):
        rank_own = own[part]
        k_sum[...] = jnp.zeros_like(k_sum)
        v_sum[...] = jnp.zeros_like(v_sum)

        def tiles(ranks, mask=None):
            at = [stretch(slots[r], half) for r in ranks]
            added = [k_sum[...], v_sum[...]]

            def produce(a):
                return (
                    mm_nt(k_heads[part], jnp.where(lane < EXTRA, p_all[a, :], q_all[a, :])),
                    mm_nt(v_heads[part], p_all[a, :]),
                )

            def consume(a, ready):
                probs = jnp.exp(ready[0])
                if mask is not None:
                    probs = jnp.where(mask, probs, 0.0)
                added[1] += mm(probs.astype(BF16), p_all[a, :])
                added[0] += mm((probs * ready[1]).astype(BF16), q_all[a, :])

            one_ahead(at, produce, consume)
            k_sum[...], v_sum[...] = added

        tiles([rank_own], causal(half, heads, True))
        in_groups(rank_own + 1, count - 1 - rank_own, tiles)
        rows = stretch(part, half)
        d_key[rows, :] = merged_heads(k_sum[...], half, heads, EXTRA).astype(BF16)
        d_value[rows, :] = merged_heads(v_sum[...], half, heads, EXTRA)[:, EXTRA:].astype(BF16)
        return 0

    lax.fori_loop(0, 2, one_half, 0)


def prepare_kernel(dc, w_out, ctx, lse, q_heads, packed, q_ext, d_ext, *, half, heads):
    lane = lanes_of(half)
    d_ctx = mm_nt(dc[...], w_out[...]).astype(BF16)
    for part in range(2):
        rows = slice(part * half, (part + 1) * half)
        grads = d_ctx[rows, :]
        terms = grads.astype(F32) * ctx[rows, :]
        extra = grads.astype(F32)
        for h in range(heads):
            deep = slice(h * half, (h + 1) * half)
            first = EXTRA + h * HEAD_DIM
            here = jnp.logical_and(lane >= first, lane < first + HEAD_DIM)
            delta = jnp.sum(jnp.where(here, terms, 0.0), axis=1, keepdims=True)
            minus_lse = three(-lse[part, deep, :])
            minus_delta = three(-delta)
            q_new = q_heads[part, deep, :].astype(F32)
            d_new = jnp.where(here, grads.astype(F32), 0.0)
            for i in range(3):
                q_new = jnp.where(lane == heads * HEAD_DIM + i, minus_lse[i], q_new)
                d_new = jnp.where(lane == i, minus_delta[i], d_new)
                extra = jnp.where(lane == 3 * h + i, minus_lse[i], extra)
                extra = jnp.where(lane == 3 * (heads + h) + i, minus_delta[i], extra)
            q_ext[part, deep, :] = q_new.astype(BF16)
            d_ext[part, deep, :] = d_new.astype(BF16)
        packed[rows, :] = extra.astype(BF16)


def finish_kernel(
    core, me, d_query, d_key, d_value, h1, n1, weights, small, terms, kept, sent, d_proj, g, rows_of
):
    chips, deep, _ = kept.shape
    lane = lax.broadcasted_iota(jnp.int32, (d_query.shape[0], 128), 1)
    part = d_value.shape[1]
    d_proj[:, :128] = d_query[:, :128]
    d_proj[:, 128:256] = jnp.where(lane < EXTRA, d_query[:, 128:], d_key[:, :128])
    d_proj[:, 256:384] = d_key[:, 128:]
    d_proj[:, 512:] = jnp.zeros_like(d_proj[:, 512:])
    d_proj[:, 384 : 384 + part] = d_value[...]
    dh1 = mm_nt(d_proj[...], weights[...])
    terms[...] = dh1.astype(BF16)
    g[...] = mm_tn(h1[...], d_proj[...])
    gain_row = jnp.sum(dh1 * n1[...], axis=0, keepdims=True)
    shift_row = jnp.sum(dh1, axis=0, keepdims=True)
    sums = jnp.sum(d_proj[...].astype(F32), axis=0, keepdims=True)
    rows_of[...] = small[...]
    count = 2 * chips
    each = h1.shape[1] // count
    wide = 2 * each
    for w in range(count // 2):
        rows_of[w, 0:1, :wide] = gain_row[:, w * wide : (w + 1) * wide]
        rows_of[w, 1:2, :wide] = shift_row[:, w * wide : (w + 1) * wide]
    many = part // wide
    for i in range(many):
        at = many * me[0] + i
        rows_of[at, 2:3, :wide] = sums[:, i * wide : (i + 1) * wide]
        rows_of[count // 2 + at, 2:3, :wide] = sums[:, 384 + i * wide : 384 + (i + 1) * wide]

    def put(target, which):
        target[:, each:, 128:] = jnp.zeros((chips, deep - each, target.shape[2] - 128), target.dtype)
        for c in range(chips):
            w = 2 * c + which
            target[c, :each, :] = g[w * each : (w + 1) * each, :].astype(target.dtype)
            target[c, each:, :128] = rows_of[w].astype(target.dtype)

    for which in range(2):

        @pl.when(core[0] == which)
        def _():
            put(kept, which)
            put(sent, 1 - which)


def finish(core, me, d_query, d_key, d_value, h1, n1, weights, small):
    rows, width = h1.shape
    count = small.shape[0]
    shape = (count // 2, width // count + 8, weights.shape[1])
    return call(
        finish_kernel, "finish", (core, me), (d_query, d_key, d_value, h1, n1, weights, small),
        [((rows, width), BF16), (shape, F32), (shape, BF16)],
        [((rows, weights.shape[1]), BF16), ((width, weights.shape[1]), F32), (small.shape, F32)],
        pl.CostEstimate(flops=4 * weights.size * rows, bytes_accessed=6 * weights.size, transcendentals=0),
    )


def whole(shape):
    return pl.BlockSpec(shape, lambda i, *_: (0,) * len(shape))


def params():
    return pltpu.CompilerParams(
        dimension_semantics=("arbitrary",), vmem_limit_bytes=VMEM_LIMIT
    )


def cost(rows, keys, heads, products):
    area = rows * keys * heads
    return pl.CostEstimate(
        flops=2 * area * 256 * products, bytes_accessed=keys * 768, transcendentals=area
    )


def call(kernel, name, scalars, arrays, outs, scratch, estimate, **static):
    return pl.pallas_call(
        functools.partial(kernel, **static),
        out_shape=tuple(jax.ShapeDtypeStruct(s, t) for s, t in outs),
        grid_spec=pltpu.PrefetchScalarGridSpec(
            num_scalar_prefetch=len(scalars),
            grid=(1,),
            in_specs=[whole(a.shape) for a in arrays],
            out_specs=[whole(s) for s, _ in outs],
            scratch_shapes=[pltpu.VMEM(s, t) for s, t in scratch],
        ),
        compiler_params=params(),
        cost_estimate=estimate,
        name=name,
    )(*scalars, *arrays)


def attend(slots, own, q_heads, kv, heads):
    _, deep, _ = q_heads.shape
    half = deep // heads
    width = heads * HEAD_DIM
    return call(
        attend_kernel, "attend", (slots, own), (q_heads, kv),
        [((width, 2 * half), BF16), ((2 * half, LANES), F32), ((2, deep, 1), F32)],
        [((deep, 1), F32), ((deep, LANES), F32), ((deep, LANES), BF16), ((8, half), F32)],
        cost(2 * half, kv.shape[0], heads, 2), half=half, heads=heads,
    )


def prepare(dc, w_out, ctx, lse, q_heads, heads):
    _, deep, _ = q_heads.shape
    half = deep // heads
    return call(
        prepare_kernel, "prepare", (), (dc, w_out, ctx, lse, q_heads),
        [((2 * half, LANES), BF16), (q_heads.shape, BF16), (q_heads.shape, BF16)], [],
        pl.CostEstimate(flops=2 * dc.size * LANES, bytes_accessed=4 * q_heads.size, transcendentals=0),
        half=half, heads=heads,
    )


def query_grad(slots, own, q_ext, d_ext, kv, heads):
    _, deep, _ = q_ext.shape
    half = deep // heads
    return call(
        query_grad_kernel, "query_grad", (slots, own), (q_ext, d_ext, kv),
        [((2 * half, LANES), BF16)], [((deep, LANES), F32)],
        cost(2 * half, kv.shape[0], heads, 3), half=half, heads=heads,
    )[0]


def key_grad(slots, own, k_heads, v_heads, q_all, p_all, heads):
    _, deep, _ = k_heads.shape
    half = deep // heads
    return call(
        key_grad_kernel, "key_grad", (slots, own), (k_heads, v_heads, q_all, p_all),
        [((2 * half, LANES), BF16), ((2 * half, heads * HEAD_DIM), BF16)], [((deep, LANES), F32)] * 2,
        cost(2 * half, q_all.shape[0], heads, 4), half=half, heads=heads,
    )


def feed_forward_kernel(
    me, x, ctx, df, vectors, w_up, w_out, w_down, x2_own, h2, act, du, dh2, down
):
    total = x[...].astype(F32) + vectors[2:3, :] + mm_tn(ctx[...], w_out[...])

    @pl.when(pl.program_id(0) == me[0])
    def _():
        x2_own[...] = total

    normed, _ = normalized(total)
    h2_low = (normed * vectors[0:1, :] + vectors[1:2, :]).astype(BF16)
    h2[...] = h2_low
    up = mm(h2_low, w_up[...]) + vectors[3:4, :]
    bend = math.sqrt(2.0 / math.pi)
    square = up * up
    turn = jnp.tanh(bend * (up + 0.044715 * square * up))
    half = 0.5 * (1.0 + turn)
    act_low = (up * half).astype(BF16)
    act[...] = act_low
    down[...] = mm(act_low, w_down[...]).astype(BF16)
    slope = half + 0.5 * up * (1.0 - turn * turn) * (bend * (1.0 + 3 * 0.044715 * square))
    du_low = (slope * mm_nt(df[...], w_down[...])).astype(BF16)
    du[...] = du_low
    dh2[...] = mm_nt(du_low, w_up[...]).astype(BF16)


def feed_forward(me, both, ctx, vectors, weights, ways):
    rows = both.shape[0]
    width = both.shape[1] // 2
    step = rows // ways

    def along(c):
        return pl.BlockSpec((step, width), lambda i, *_: (i, c))

    def third(c):
        return pl.BlockSpec((weights.shape[0], width), lambda i, *_: (0, c))

    flat = jax.ShapeDtypeStruct((rows, width), BF16)
    return pl.pallas_call(
        feed_forward_kernel,
        out_shape=(jax.ShapeDtypeStruct((step, width), F32), flat, flat, flat, flat, flat),
        grid_spec=pltpu.PrefetchScalarGridSpec(
            num_scalar_prefetch=1,
            grid=(ways,),
            in_specs=[
                along(0),
                pl.BlockSpec((width, step), lambda i, *_: (0, i)),
                along(1),
                whole(vectors.shape),
                third(0),
                third(1),
                third(2),
            ],
            out_specs=[whole((step, width))] + [along(0)] * 5,
        ),
        compiler_params=params(),
        cost_estimate=pl.CostEstimate(
            flops=10 * rows * width * width, bytes_accessed=6 * width * width, transcendentals=rows * width
        ),
        name="feed_forward",
    )(me, both, ctx, both, vectors, weights, weights, weights)


def weight_grads_kernel(core, h2, du, act, df, ctx, dc, kept, sent, g_up, g_down, g_out):
    chips, rows, width = kept.shape
    each = h2.shape[1] // (2 * chips)
    few = ctx.shape[0] // (2 * chips)
    chunk = h2.shape[1] // 2
    for i in range(2):
        cols = slice(i * chunk, (i + 1) * chunk)
        g_up[cols, :] = mm_tn(h2[:, cols], du[...])
        g_down[cols, :] = mm_tn(act[:, cols], df[...])
    g_out[...] = mm(ctx[...], dc[...])

    def put(target, which):
        kind = target.dtype
        target[:, 2 * each :, :] = jnp.zeros((chips, rows - 2 * each, width), kind)
        for c in range(chips):
            w = 2 * c + which
            target[c, :each, :] = g_up[w * each : (w + 1) * each, :].astype(kind)
            target[c, each : 2 * each, :] = g_down[w * each : (w + 1) * each, :].astype(kind)
            target[c, 2 * each : 2 * each + few, :] = g_out[w * few : (w + 1) * few, :].astype(kind)

    for which in range(2):

        @pl.when(core[0] == which)
        def _():
            put(kept, which)
            put(sent, 1 - which)


def weight_grads(core, h2, du, act, both, ctx, dc, owners):
    count, width = du.shape
    units = h2.shape[1]
    shape = (owners // 2, 2 * units // owners + 8, width)
    return pl.pallas_call(
        weight_grads_kernel,
        out_shape=(jax.ShapeDtypeStruct(shape, F32), jax.ShapeDtypeStruct(shape, BF16)),
        grid_spec=pltpu.PrefetchScalarGridSpec(
            num_scalar_prefetch=1,
            grid=(1,),
            in_specs=[
                whole(h2.shape),
                whole(du.shape),
                whole(act.shape),
                pl.BlockSpec((count, width), lambda i, *_: (0, 1)),
                whole(ctx.shape),
                whole(dc.shape),
            ],
            out_specs=[whole(shape)] * 2,
            scratch_shapes=[
                pltpu.VMEM((units, width), F32),
                pltpu.VMEM((units, width), F32),
                pltpu.VMEM((ctx.shape[0], width), F32),
            ],
        ),
        compiler_params=params(),
        cost_estimate=pl.CostEstimate(
            flops=4 * h2.size * width, bytes_accessed=6 * units * width, transcendentals=0
        ),
        name="weight_grads",
    )(core, h2, du, act, both, ctx, dc)


def normalized(values):
    mean = jnp.mean(values, axis=-1, keepdims=True)
    centered = values - mean
    spread = jnp.mean(centered * centered, axis=-1, keepdims=True)
    scale = lax.rsqrt(spread + NORM_EPS)
    return centered * scale, scale


def norm_back(grad, gain, normed, scale):
    e = grad * gain
    mean_e = jnp.mean(e, axis=-1, keepdims=True)
    mean_en = jnp.mean(e * normed, axis=-1, keepdims=True)
    return scale * (e - mean_e - normed * mean_en)


def gelu_tanh(values):
    return jax.nn.gelu(values, approximate=True)


def head_lanes(x, heads, first, ones_at=None):
    rows, width = x.shape
    wide = jnp.pad(x, ((0, 0), (first, LANES - width - first))).reshape(2, 1, rows // 2, LANES)
    lane = lax.broadcasted_iota(jnp.int32, (1, heads, 1, LANES), 3)
    head = lax.broadcasted_iota(jnp.int32, (1, heads, 1, LANES), 1)
    start = first + head * HEAD_DIM
    here = jnp.logical_and(lane >= start, lane < start + HEAD_DIM)
    out = jnp.where(here, wide, jnp.zeros((), x.dtype))
    if ones_at is not None:
        at = ones_at + 3 * head
        out = jnp.where(jnp.logical_and(lane >= at, lane < at + 3), jnp.ones((), x.dtype), out)
    return out.reshape(2, heads * rows // 2, LANES)


def to_all(x, axis="ulysses"):
    ways = lax.axis_size(axis)
    sent = jnp.broadcast_to(x[None], (ways,) + x.shape)
    return lax.all_to_all(sent, axis, split_axis=0, concat_axis=0, tiled=True)


def summed_at_owner(x, axis="ulysses"):
    ways = lax.axis_size(axis)
    sent = x.astype(BF16).reshape(ways, -1, x.shape[1])
    got = lax.all_to_all(sent, axis, split_axis=0, concat_axis=0, tiled=True)
    return jnp.sum(got.astype(F32), axis=0)


def other_core(x):
    return lax.ppermute(x, "core", [(0, 1), (1, 0)])


def reduced(x, axis):
    ways = lax.axis_size(axis)
    me = lax.axis_index(axis)

    def rows_of(k):
        return lax.dynamic_index_in_dim(x, lax.rem(me + k, ways), axis=0, keepdims=False)

    got = [
        lax.ppermute(rows_of(k).astype(BF16), axis, [(i, (i + k) % ways) for i in range(ways)])
        for k in range(1, ways)
    ]
    total = rows_of(0).astype(F32)
    for g in got:
        total += g.astype(F32)
    return total


def on_device(
    tokens,
    stretch_order,
    ln_gain,
    ln_bias,
    w_qkv,
    qv_bias,
    w_out,
    out_bias,
    w_up,
    up_bias,
    w_down,
    down_bias,
    cotangent,
):
    own_rows, width = tokens.shape
    ways = lax.axis_size("ulysses")
    wide = lax.axis_size(WIDE)
    me = lax.axis_index("ulysses")
    rows = own_rows * ways
    heads = HEADS // ways
    part = width // ways
    held = w_qkv.shape[1]
    ff_held = w_down.shape[1]
    ff_part = ff_held * wide
    pair = 2 * held

    order = stretch_order[0]
    own = lax.dynamic_slice(order, (2 * lax.axis_index(BLK),), (2,))
    count = order.shape[0]
    index = jnp.arange(count, dtype=jnp.int32)
    slots = jnp.sum(jnp.where(order[None, :] == index[:, None], index[None, :], 0), axis=1)

    small = jnp.concatenate(
        [
            ln_gain,
            ln_bias,
            qv_bias,
            jnp.concatenate([out_bias, down_bias], axis=1),
            up_bias.reshape(2, pair),
        ],
        axis=0,
    )
    qkv_slices = w_qkv[0].reshape(held, 3, ways, part).transpose(2, 0, 1, 3).reshape(ways, held, 3 * part)
    up_slices = w_up[0].reshape(held, wide, ways, ff_held).transpose(2, 0, 1, 3).reshape(ways, held, ff_part)
    df_own = cotangent.astype(BF16)
    both = lax.all_gather(jnp.concatenate([tokens, df_own], axis=1), "ulysses", axis=0, tiled=True)
    first = jnp.concatenate(
        [
            qkv_slices,
            jnp.broadcast_to(small[None], (ways,) + small.shape),
            jnp.zeros((ways, held, width - 3 * part - pair), BF16),
        ],
        axis=2,
    )
    blank = jnp.zeros((ways, 8 - held, width), BF16)
    wide_out = jnp.broadcast_to(w_out[0][None], (ways, held, width))
    sent = jnp.concatenate([first, blank, up_slices, blank, wide_out, blank], axis=1)
    got = lax.all_to_all(sent, "ulysses", split_axis=0, concat_axis=0, tiled=True)
    piece = got[:, :held, : 3 * part + 64].reshape(ways * held, 3 * part + 64)
    filled = lax.all_gather(piece, WIDE, axis=0, tiled=True)
    ffn = jnp.concatenate(
        [
            got[:, 8 : 8 + held].reshape(ways * held, width),
            got[:, 16 : 16 + held].reshape(ways * held, width),
            w_down[0],
        ],
        axis=1,
    )
    w_qkv_u = filled[:, : 3 * part]
    smalls = filled[:, 3 * part : 3 * part + pair].reshape(wide * ways, held, pair).astype(F32)
    gains = smalls[:, 0].reshape(-1)
    shifts = smalls[:, 1].reshape(-1)
    qv_all = smalls[:, 2].reshape(-1)
    out_bias_all = smalls[:, 3, :held].reshape(-1)
    down_bias_all = smalls[:, 3, held:].reshape(-1)
    up_bias_all = smalls[:, 4:].reshape(wide, ways, ff_held)
    up_bias_u = lax.dynamic_index_in_dim(up_bias_all, me, axis=1, keepdims=False).reshape(-1)
    bias_q = lax.dynamic_slice(qv_all, (me * part,), (part,))
    bias_v = lax.dynamic_slice(qv_all, (width + me * part,), (part,))

    n1, _ = normalized(both[:, :width].astype(F32))
    h1 = (n1 * gains[:width] + shifts[:width]).astype(BF16)
    proj_bias = jnp.concatenate([bias_q, jnp.zeros((part,), F32), bias_v])
    proj = (mm(h1, w_qkv_u) + proj_bias).astype(BF16)
    q_scaled = proj[:, :part] * jnp.asarray(1.0 / math.sqrt(HEAD_DIM), BF16)
    kv = proj[:, part:]
    kv_all = lax.all_gather(kv, BLK, axis=0, tiled=True)
    q_heads = head_lanes(q_scaled, heads, 0)

    k_heads = head_lanes(kv[:, :part], heads, EXTRA, 0)
    v_heads = head_lanes(kv[:, part:], heads, EXTRA, 3 * heads)
    q_wide = jnp.pad(q_scaled, ((0, 0), (EXTRA, 0)))
    gain_two = gains[width:]
    vectors = jnp.stack(
        [gain_two, shifts[width:], out_bias_all, up_bias_u] + [jnp.zeros((width,), F32)] * 4
    )
    (ffn, kv_all, slots, own, q_heads, k_heads, v_heads, q_wide, vectors, n1) = (
        lax.optimization_barrier(
            (ffn, kv_all, slots, own, q_heads, k_heads, v_heads, q_wide, vectors, n1)
        )
    )
    ffn_all = lax.all_gather(ffn, WIDE, axis=0, tiled=True)

    ctx_low, ctx, lse = attend(slots, own, q_heads, kv_all, heads)
    ctx_all = to_all(ctx_low).reshape(width, rows)
    q_wide, ctx_all = lax.optimization_barrier((q_wide, ctx_all))
    q_all = lax.all_gather(q_wide, BLK, axis=0, tiled=True)
    x2_own, h2, act, du, dh2, down = feed_forward(
        me[None], both, ctx_all, vectors, ffn_all, ways
    )
    dh2 = summed_at_owner(dh2)
    ctx_rows = lax.dynamic_index_in_dim(
        ctx_all.reshape(wide, ways, held, rows), me, axis=1, keepdims=False
    ).reshape(part, rows)
    w_out_u = lax.dynamic_slice(ffn_all, (me * part, width), (part, width))
    g_up_bias = jnp.sum(du.astype(F32), axis=0)
    g_down_bias = jnp.sum(df_own.astype(F32), axis=0)

    n2_own, r2_own = normalized(x2_own)
    dx2 = cotangent + norm_back(dh2, gain_two, n2_own, r2_own)
    g_gain_two = jnp.sum(dh2 * n2_own, axis=0)
    g_shift_two = jnp.sum(dh2, axis=0)
    dc_own = dx2.astype(BF16)
    g_out_bias = jnp.sum(dc_own.astype(F32), axis=0)
    owners = wide * ways
    blank = jnp.zeros((width,), F32)
    small_grads = jnp.stack(
        [
            jnp.concatenate([blank, g_gain_two]).reshape(wide, -1),
            jnp.concatenate([blank, g_shift_two]).reshape(wide, -1),
            jnp.zeros((wide, ways * pair), F32),
            jnp.concatenate(
                [g_out_bias.reshape(owners, held), g_down_bias.reshape(owners, held)], axis=1
            ).reshape(wide, -1),
        ],
        axis=1,
    )
    g_up_full = jnp.zeros((wide, 2, ways, pair), F32)
    g_up_full = lax.dynamic_update_slice(
        g_up_full, g_up_bias.reshape(wide, 2, 1, pair), (0, 0, me, 0)
    )
    small_grads = jnp.concatenate([small_grads, g_up_full.reshape(wide, 2, ways * pair)], axis=1)
    small_grads = jnp.pad(small_grads, ((0, 0), (0, 2), (0, 128 - ways * pair)))
    dc = to_all(dc_own).reshape(rows, width)
    dc, q_all, small_grads, ctx_rows = lax.optimization_barrier((dc, q_all, small_grads, ctx_rows))
    w_out_u = lax.dynamic_slice(ffn_all, (me * part, width), (part, width))

    w_out_wide = jnp.pad(w_out_u, ((EXTRA, 0), (0, 0)))
    packed, q_ext, d_ext = prepare(dc, w_out_wide, ctx, lse, q_heads, heads)
    packed_all = lax.all_gather(packed, BLK, axis=0, tiled=True)
    core = lax.axis_index("core")
    early, early_sent = weight_grads(core[None], h2, du, act, both, ctx_rows, dc, wide)
    early = (early + other_core(early_sent).astype(F32)).astype(BF16)
    early, q_ext = lax.optimization_barrier((early, q_ext))
    early = lax.all_to_all(early, CHIPS, split_axis=0, concat_axis=0, tiled=True)
    d_query = query_grad(slots, own, q_ext, d_ext, kv_all, heads)
    early, packed_all, d_query = lax.optimization_barrier((early, packed_all, d_query))
    early = jnp.sum(early.astype(F32), axis=0)
    d_key, d_value = key_grad(slots, own, k_heads, v_heads, q_all, packed_all, heads)
    terms, late, late_sent = finish(
        core[None], me[None], d_query, d_key, d_value, h1, n1, filled, small_grads
    )
    terms, late_got = lax.optimization_barrier((terms, other_core(late_sent)))
    pair_sums = reduced(
        jnp.concatenate([terms, down], axis=1).reshape(ways, own_rows, 2 * width), "ulysses"
    )
    dh1 = pair_sums[:, :width]
    result = pair_sums[:, width:] + x2_own + down_bias_all
    late = (late + late_got.astype(F32)).astype(BF16)
    late = lax.all_to_all(late, CHIPS, split_axis=0, concat_axis=0, tiled=True)
    late = jnp.sum(late.astype(F32), axis=0)
    n1_own, r1_own = normalized(tokens.astype(F32))
    d_tokens = dx2 + norm_back(dh1, gains[:width], n1_own, r1_own)

    small_rows = late[ways * held : ways * held + 6, : ways * pair].reshape(6, ways, pair)
    last = jnp.concatenate(
        [
            late[: ways * held, : 3 * part].reshape(ways, held, 3 * part),
            jnp.pad(small_rows.transpose(1, 0, 2), ((0, 0), (0, 0), (0, 64 - pair))),
            early[:ff_held].reshape(ways, held, -1),
        ],
        axis=2,
    )
    last = lax.all_to_all(last, "ulysses", split_axis=0, concat_axis=0, tiled=True)
    o_w_qkv = last[:, :, : 3 * part].reshape(ways, held, 3, part).transpose(1, 2, 0, 3)
    o_small = jnp.sum(last[:, :, 3 * part : 3 * part + pair], axis=0)
    o_w_up = last[:, :, 3 * part + 64 :].reshape(ways, held, wide, ff_held).transpose(1, 2, 0, 3)
    return (
        result,
        d_tokens,
        o_small[0:1],
        o_small[1:2],
        o_w_qkv.reshape(1, held, 3 * width),
        o_small[2:3],
        early[None, 2 * ff_held : 2 * ff_held + held],
        o_small[3:4, :held],
        o_w_up.reshape(1, held, -1),
        o_small[4:6].reshape(1, ff_held),
        early[None, ff_held : 2 * ff_held],
        o_small[3:4, held:],
    )


def solution(mesh):
    chips_z = mesh.shape["blk"] // 4
    parts = Mesh(
        mesh.devices.reshape(mesh.shape["batch"], 2, chips_z, 2, mesh.shape["ulysses"]), ALL
    )
    rows = P(ALL, None)
    flat = P(None, ALL)
    deep = P(None, ALL, None)
    return jax.shard_map(
        on_device,
        mesh=parts,
        in_specs=(
            rows, P("batch", None), flat, flat, deep, flat, deep, flat, deep, flat, deep, flat, rows,
        ),
        out_specs=(rows, rows, flat, flat, deep, flat, deep, flat, deep, flat, deep, flat),
        check_vma=False,
    )
```

```python
import functools
import math

import jax
import jax.numpy as jnp
from jax import lax
from jax.experimental import pallas as pl
from jax.experimental.pallas import tpu as pltpu
from jax.sharding import Mesh, PartitionSpec as P

HEADS = 12
HEAD_DIM = 64
NORM_EPS = 1e-05
FLOOR = -1e25
HIGHEST_ABOVE = 60.0
LANES = 256
EXTRA = 64
BELOW_FLOOR = -1e30
BLK = ("xlo", "z", "core")
CHIPS = ("batch", "xlo", "z")
WIDE = ("batch", "xlo", "z", "core")
ALL = ("batch", "xlo", "z", "core", "ulysses")
BF16 = jnp.bfloat16
F32 = jnp.float32
NT = (((1,), (1,)), ((), ()))
VMEM_LIMIT = 60 * 1024 * 1024


def mm(a, b):
    return jnp.dot(a, b, preferred_element_type=F32)


def mm_nt(a, b):
    return lax.dot_general(a, b, NT, preferred_element_type=F32)


def mm_tn(a, b):
    return lax.dot_general(a, b, (((0,), (0,)), ((), ())), preferred_element_type=F32)


def stretch(index, half):
    return pl.ds(pl.multiple_of(index * half, half), half)


def lanes_of(rows):
    return lax.broadcasted_iota(jnp.int32, (rows, LANES), 1)


def ones_after(k, first):
    return jnp.where(lanes_of(k.shape[0]) < first, k, jnp.ones_like(k))


def ones_before(v):
    return jnp.where(lanes_of(v.shape[0]) < EXTRA, jnp.ones_like(v), v)


def three(x):
    high = x.astype(BF16).astype(F32)
    mid = (x - high).astype(BF16).astype(F32)
    return high, mid, x - high - mid


def causal(half, heads, keys_first):
    rows = lax.broadcasted_iota(jnp.int32, (heads * half, half), 0) & (half - 1)
    cols = lax.broadcasted_iota(jnp.int32, (heads * half, half), 1)
    return rows <= cols if keys_first else cols <= rows


def merged_heads(stacked, half, heads, first):
    lane = lanes_of(half)
    out = stacked[:half]
    for h in range(1, heads):
        out = jnp.where(lane < first + h * HEAD_DIM, out, stacked[h * half : (h + 1) * half])
    return out


def in_groups(first, count, tiles):
    def eight(i, _):
        tiles([first + 8 * i + j for j in range(8)])
        return 0

    lax.fori_loop(0, count // 8, eight, 0)
    for size in (4, 2, 1):

        @pl.when((count & size) != 0)
        def _():
            begin = first + (count & ~(2 * size - 1))
            tiles([begin + j for j in range(size)])


def one_ahead(items, produce, consume):
    ready = produce(items[0])
    for n, item in enumerate(items):
        now = ready
        if n + 1 < len(items):
            ready = produce(items[n + 1])
        consume(item, now)


def attend_kernel(
    slots, own, q_heads, kv, ctx_low, ctx, lse, shift, total, q_ext, top, *, half, heads
):
    deep = heads * half
    lane = lanes_of(deep)

    def one_half(part, _):
        rank_own = own[part]
        mask = causal(half, heads, False)
        here = stretch(slots[rank_own], half)
        scores = jnp.where(mask, mm_nt(q_heads[part], kv[here, :LANES]), BELOW_FLOOR)
        first = jnp.max(scores, axis=1, keepdims=True).astype(BF16).astype(F32)
        shift[...] = first
        q_ext[...] = jnp.where(lane == heads * HEAD_DIM, -first, q_heads[part].astype(F32)).astype(
            BF16
        )
        top[...] = jnp.zeros_like(top)
        total[...] = mm(jnp.exp(scores - first).astype(BF16), ones_before(kv[here, 128:]))

        def tiles(ranks):
            at = [stretch(slots[r], half) for r in ranks]
            added = [total[...], top[...]]

            def produce(a):
                return mm_nt(q_ext[...], ones_after(kv[a, :LANES], heads * HEAD_DIM))

            def consume(a, above):
                added[1] = jnp.maximum(added[1], jnp.max(above.reshape(deep // 8, 8, half), axis=0))
                added[0] += mm(jnp.exp(above).astype(BF16), ones_before(kv[a, 128:]))

            one_ahead(at, produce, consume)
            total[...] = added[0]
            top[...] = added[1]

        in_groups(0, rank_own, tiles)

        @pl.when(jnp.logical_not(jnp.max(top[...]) < HIGHEST_ABOVE))
        def _():
            shift[...] = jnp.full_like(shift, FLOOR)
            total[...] = jnp.zeros_like(total)

            def again(rank, _):
                a = stretch(slots[rank], half)
                allowed = jnp.logical_or(mask, rank < rank_own)
                scores = jnp.where(allowed, mm_nt(q_heads[part], kv[a, :LANES]), BELOW_FLOOR)
                new = jnp.maximum(shift[...], jnp.max(scores, axis=1, keepdims=True))
                total[...] = total[...] * jnp.exp(shift[...] - new) + mm(
                    jnp.exp(scores - new).astype(BF16), ones_before(kv[a, 128:])
                )
                shift[...] = new
                return 0

            lax.fori_loop(0, rank_own + 1, again, 0)

        row_sum = total[:, :1]
        lse[part] = shift[...] + jnp.log(row_sum)
        done = merged_heads(total[...] / row_sum, half, heads, EXTRA)
        rows = stretch(part, half)
        ctx[rows, :] = done
        ctx_low[:, rows] = done.T[EXTRA:, :].astype(BF16)
        return 0

    lax.fori_loop(0, 2, one_half, 0)


def query_grad_kernel(slots, own, q_ext, d_ext, kv, d_query, total, *, half, heads):
    def one_half(part, _):
        rank_own = own[part]
        total[...] = jnp.zeros_like(total)

        def tiles(ranks, mask=None):
            at = [stretch(slots[r], half) for r in ranks]
            added = [total[...]]

            def produce(a):
                return (
                    mm_nt(q_ext[part], ones_after(kv[a, :LANES], heads * HEAD_DIM)),
                    mm_nt(d_ext[part], ones_before(kv[a, 128:])),
                )

            def consume(a, ready):
                probs = jnp.exp(ready[0])
                if mask is not None:
                    probs = jnp.where(mask, probs, 0.0)
                added[0] += mm((probs * ready[1]).astype(BF16), kv[a, :LANES])

            one_ahead(at, produce, consume)
            total[...] = added[0]

        in_groups(0, rank_own, tiles)
        tiles([rank_own], causal(half, heads, False))
        done = merged_heads(total[...], half, heads, 0)
        d_query[stretch(part, half), :] = (done * (1.0 / math.sqrt(HEAD_DIM))).astype(BF16)
        return 0

    lax.fori_loop(0, 2, one_half, 0)


def key_grad_kernel(
    slots, own, k_heads, v_heads, q_all, p_all, d_key, d_value, k_sum, v_sum, *, half, heads
):
    count = slots.shape[0]
    lane = lanes_of(half)

    def one_half(part, _):
        rank_own = own[part]
        k_sum[...] = jnp.zeros_like(k_sum)
        v_sum[...] = jnp.zeros_like(v_sum)

        def tiles(ranks, mask=None):
            at = [stretch(slots[r], half) for r in ranks]
            added = [k_sum[...], v_sum[...]]

            def produce(a):
                return (
                    mm_nt(k_heads[part], jnp.where(lane < EXTRA, p_all[a, :], q_all[a, :])),
                    mm_nt(v_heads[part], p_all[a, :]),
                )

            def consume(a, ready):
                probs = jnp.exp(ready[0])
                if mask is not None:
                    probs = jnp.where(mask, probs, 0.0)
                added[1] += mm(probs.astype(BF16), p_all[a, :])
                added[0] += mm((probs * ready[1]).astype(BF16), q_all[a, :])

            one_ahead(at, produce, consume)
            k_sum[...], v_sum[...] = added

        tiles([rank_own], causal(half, heads, True))
        in_groups(rank_own + 1, count - 1 - rank_own, tiles)
        rows = stretch(part, half)
        d_key[rows, :] = merged_heads(k_sum[...], half, heads, EXTRA).astype(BF16)
        d_value[rows, :] = merged_heads(v_sum[...], half, heads, EXTRA)[:, EXTRA:].astype(BF16)
        return 0

    lax.fori_loop(0, 2, one_half, 0)


def prepare_kernel(dc, w_out, ctx, lse, q_heads, packed, q_ext, d_ext, *, half, heads):
    lane = lanes_of(half)
    d_ctx = mm_nt(dc[...], w_out[...]).astype(BF16)
    for part in range(2):
        rows = slice(part * half, (part + 1) * half)
        grads = d_ctx[rows, :]
        terms = grads.astype(F32) * ctx[rows, :]
        extra = grads.astype(F32)
        for h in range(heads):
            deep = slice(h * half, (h + 1) * half)
            first = EXTRA + h * HEAD_DIM
            here = jnp.logical_and(lane >= first, lane < first + HEAD_DIM)
            delta = jnp.sum(jnp.where(here, terms, 0.0), axis=1, keepdims=True)
            minus_lse = three(-lse[part, deep, :])
            minus_delta = three(-delta)
            q_new = q_heads[part, deep, :].astype(F32)
            d_new = jnp.where(here, grads.astype(F32), 0.0)
            for i in range(3):
                q_new = jnp.where(lane == heads * HEAD_DIM + i, minus_lse[i], q_new)
                d_new = jnp.where(lane == i, minus_delta[i], d_new)
                extra = jnp.where(lane == 3 * h + i, minus_lse[i], extra)
                extra = jnp.where(lane == 3 * (heads + h) + i, minus_delta[i], extra)
            q_ext[part, deep, :] = q_new.astype(BF16)
            d_ext[part, deep, :] = d_new.astype(BF16)
        packed[rows, :] = extra.astype(BF16)


def project_kernel(me, x, weights, h1, n1, kv, q, vec, bias, *, wide, ways, pair, part):
    count = ways * pair
    each = weights.shape[0] // wide
    for w in range(wide):
        block = weights[w * each : w * each + 8, 512:].astype(F32)
        vec[:, w * count : (w + 1) * count] = block[:, 64 : 64 + count]
    width = x.shape[1]
    bias[...] = jnp.zeros_like(bias)
    for u in range(ways):

        @pl.when(me[0] == u)
        def _():
            bias[0:1, :part] = vec[2:3, u * part : (u + 1) * part]
            bias[0:1, 2 * part : 3 * part] = vec[2:3, width + u * part : width + (u + 1) * part]

    normed, _ = normalized(x[...].astype(F32))
    n1[...] = normed
    h1_low = (normed * vec[0:1, :width] + vec[1:2, :width]).astype(BF16)
    h1[...] = h1_low
    proj = (mm(h1_low, weights[...]) + bias[0:1, :]).astype(BF16)
    q[...] = proj[:, :part] * jnp.asarray(1.0 / math.sqrt(HEAD_DIM), BF16)
    kv[...] = proj[:, part : 3 * part]


def project(me, both, weights, part, wide, ways, pair):
    rows = both.shape[0]
    width = both.shape[1] // 2
    outs = [
        ((rows, width), BF16),
        ((rows, width), F32),
        ((rows, 2 * part), BF16),
        ((rows, part), BF16),
        ((8, wide * ways * pair), F32),
    ]
    return pl.pallas_call(
        functools.partial(project_kernel, wide=wide, ways=ways, pair=pair, part=part),
        out_shape=tuple(jax.ShapeDtypeStruct(s, t) for s, t in outs),
        grid_spec=pltpu.PrefetchScalarGridSpec(
            num_scalar_prefetch=1,
            grid=(1,),
            in_specs=[pl.BlockSpec((rows, width), lambda i, *_: (0, 0)), whole(weights.shape)],
            out_specs=[whole(s) for s, _ in outs],
            scratch_shapes=[pltpu.VMEM((8, weights.shape[1]), F32)],
        ),
        compiler_params=params(),
        cost_estimate=pl.CostEstimate(
            flops=2 * rows * weights.size, bytes_accessed=8 * rows * width, transcendentals=rows
        ),
        name="project",
    )(me, both, weights)


def finish_kernel(
    core, me, d_query, d_key, d_value, h1, n1, weights, small, terms, kept, sent, d_proj, g, rows_of
):
    chips, deep, _ = kept.shape
    lane = lax.broadcasted_iota(jnp.int32, (d_query.shape[0], 128), 1)
    part = d_value.shape[1]
    d_proj[:, :128] = d_query[:, :128]
    d_proj[:, 128:256] = jnp.where(lane < EXTRA, d_query[:, 128:], d_key[:, :128])
    d_proj[:, 256:384] = d_key[:, 128:]
    d_proj[:, 512:] = jnp.zeros_like(d_proj[:, 512:])
    d_proj[:, 384 : 384 + part] = d_value[...]
    dh1 = mm_nt(d_proj[...], weights[...])
    terms[...] = dh1.astype(BF16)
    g[...] = mm_tn(h1[...], d_proj[...])
    gain_row = jnp.sum(dh1 * n1[...], axis=0, keepdims=True)
    shift_row = jnp.sum(dh1, axis=0, keepdims=True)
    sums = jnp.sum(d_proj[...].astype(F32), axis=0, keepdims=True)
    rows_of[...] = small[...]
    count = 2 * chips
    each = h1.shape[1] // count
    wide = 2 * each
    for w in range(count // 2):
        rows_of[w, 0:1, :wide] = gain_row[:, w * wide : (w + 1) * wide]
        rows_of[w, 1:2, :wide] = shift_row[:, w * wide : (w + 1) * wide]
    many = part // wide
    for i in range(many):
        at = many * me[0] + i
        rows_of[at, 2:3, :wide] = sums[:, i * wide : (i + 1) * wide]
        rows_of[count // 2 + at, 2:3, :wide] = sums[:, 384 + i * wide : 384 + (i + 1) * wide]

    def put(target, which):
        target[:, each:, 128:] = jnp.zeros((chips, deep - each, target.shape[2] - 128), target.dtype)
        for c in range(chips):
            w = 2 * c + which
            target[c, :each, :] = g[w * each : (w + 1) * each, :].astype(target.dtype)
            target[c, each:, :128] = rows_of[w].astype(target.dtype)

    for which in range(2):

        @pl.when(core[0] == which)
        def _():
            put(kept, which)
            put(sent, 1 - which)


def finish(core, me, d_query, d_key, d_value, h1, n1, weights, small):
    rows, width = h1.shape
    count = small.shape[0]
    shape = (count // 2, width // count + 8, weights.shape[1])
    return call(
        finish_kernel, "finish", (core, me), (d_query, d_key, d_value, h1, n1, weights, small),
        [((rows, width), BF16), (shape, F32), (shape, BF16)],
        [((rows, weights.shape[1]), BF16), ((width, weights.shape[1]), F32), (small.shape, F32)],
        pl.CostEstimate(flops=4 * weights.size * rows, bytes_accessed=6 * weights.size, transcendentals=0),
    )


def whole(shape):
    return pl.BlockSpec(shape, lambda i, *_: (0,) * len(shape))


def params():
    return pltpu.CompilerParams(
        dimension_semantics=("arbitrary",), vmem_limit_bytes=VMEM_LIMIT
    )


def cost(rows, keys, heads, products):
    area = rows * keys * heads
    return pl.CostEstimate(
        flops=2 * area * 256 * products, bytes_accessed=keys * 768, transcendentals=area
    )


def call(kernel, name, scalars, arrays, outs, scratch, estimate, **static):
    return pl.pallas_call(
        functools.partial(kernel, **static),
        out_shape=tuple(jax.ShapeDtypeStruct(s, t) for s, t in outs),
        grid_spec=pltpu.PrefetchScalarGridSpec(
            num_scalar_prefetch=len(scalars),
            grid=(1,),
            in_specs=[whole(a.shape) for a in arrays],
            out_specs=[whole(s) for s, _ in outs],
            scratch_shapes=[pltpu.VMEM(s, t) for s, t in scratch],
        ),
        compiler_params=params(),
        cost_estimate=estimate,
        name=name,
    )(*scalars, *arrays)


def attend(slots, own, q_heads, kv, heads):
    _, deep, _ = q_heads.shape
    half = deep // heads
    width = heads * HEAD_DIM
    return call(
        attend_kernel, "attend", (slots, own), (q_heads, kv),
        [((width, 2 * half), BF16), ((2 * half, LANES), F32), ((2, deep, 1), F32)],
        [((deep, 1), F32), ((deep, LANES), F32), ((deep, LANES), BF16), ((8, half), F32)],
        cost(2 * half, kv.shape[0], heads, 2), half=half, heads=heads,
    )


def prepare(dc, w_out, ctx, lse, q_heads, heads):
    _, deep, _ = q_heads.shape
    half = deep // heads
    return call(
        prepare_kernel, "prepare", (), (dc, w_out, ctx, lse, q_heads),
        [((2 * half, LANES), BF16), (q_heads.shape, BF16), (q_heads.shape, BF16)], [],
        pl.CostEstimate(flops=2 * dc.size * LANES, bytes_accessed=4 * q_heads.size, transcendentals=0),
        half=half, heads=heads,
    )


def query_grad(slots, own, q_ext, d_ext, kv, heads):
    _, deep, _ = q_ext.shape
    half = deep // heads
    return call(
        query_grad_kernel, "query_grad", (slots, own), (q_ext, d_ext, kv),
        [((2 * half, LANES), BF16)], [((deep, LANES), F32)],
        cost(2 * half, kv.shape[0], heads, 3), half=half, heads=heads,
    )[0]


def key_grad(slots, own, k_heads, v_heads, q_all, p_all, heads):
    _, deep, _ = k_heads.shape
    half = deep // heads
    return call(
        key_grad_kernel, "key_grad", (slots, own), (k_heads, v_heads, q_all, p_all),
        [((2 * half, LANES), BF16), ((2 * half, heads * HEAD_DIM), BF16)], [((deep, LANES), F32)] * 2,
        cost(2 * half, q_all.shape[0], heads, 4), half=half, heads=heads,
    )


def feed_forward_kernel(
    me, x, ctx, df, vectors, w_up, w_out, w_down, x2_own, h2, act, du, dh2, down
):
    total = x[...].astype(F32) + vectors[2:3, :] + mm_tn(ctx[...], w_out[...])

    @pl.when(pl.program_id(0) == me[0])
    def _():
        x2_own[...] = total

    normed, _ = normalized(total)
    h2_low = (normed * vectors[0:1, :] + vectors[1:2, :]).astype(BF16)
    h2[...] = h2_low
    up = mm(h2_low, w_up[...]) + vectors[3:4, :]
    bend = math.sqrt(2.0 / math.pi)
    square = up * up
    turn = jnp.tanh(bend * (up + 0.044715 * square * up))
    half = 0.5 * (1.0 + turn)
    act_low = (up * half).astype(BF16)
    act[...] = act_low
    down[...] = mm(act_low, w_down[...]).astype(BF16)
    slope = half + 0.5 * up * (1.0 - turn * turn) * (bend * (1.0 + 3 * 0.044715 * square))
    du_low = (slope * mm_nt(df[...], w_down[...])).astype(BF16)
    du[...] = du_low
    dh2[...] = mm_nt(du_low, w_up[...]).astype(BF16)


def feed_forward(me, both, ctx, vectors, weights, ways):
    rows = both.shape[0]
    width = both.shape[1] // 2
    step = rows // ways

    def along(c):
        return pl.BlockSpec((step, width), lambda i, *_: (i, c))

    def third(c):
        return pl.BlockSpec((weights.shape[0], width), lambda i, *_: (0, c))

    flat = jax.ShapeDtypeStruct((rows, width), BF16)
    return pl.pallas_call(
        feed_forward_kernel,
        out_shape=(jax.ShapeDtypeStruct((step, width), F32), flat, flat, flat, flat, flat),
        grid_spec=pltpu.PrefetchScalarGridSpec(
            num_scalar_prefetch=1,
            grid=(ways,),
            in_specs=[
                along(0),
                pl.BlockSpec((width, step), lambda i, *_: (0, i)),
                along(1),
                whole(vectors.shape),
                third(0),
                third(1),
                third(2),
            ],
            out_specs=[whole((step, width))] + [along(0)] * 5,
        ),
        compiler_params=params(),
        cost_estimate=pl.CostEstimate(
            flops=10 * rows * width * width, bytes_accessed=6 * width * width, transcendentals=rows * width
        ),
        name="feed_forward",
    )(me, both, ctx, both, vectors, weights, weights, weights)


def weight_grads_kernel(core, h2, du, act, df, ctx, dc, kept, sent, g_up, g_down, g_out):
    chips, rows, width = kept.shape
    each = h2.shape[1] // (2 * chips)
    few = ctx.shape[0] // (2 * chips)
    chunk = h2.shape[1] // 2
    for i in range(2):
        cols = slice(i * chunk, (i + 1) * chunk)
        g_up[cols, :] = mm_tn(h2[:, cols], du[...])
        g_down[cols, :] = mm_tn(act[:, cols], df[...])
    g_out[...] = mm(ctx[...], dc[...])

    def put(target, which):
        kind = target.dtype
        target[:, 2 * each :, :] = jnp.zeros((chips, rows - 2 * each, width), kind)
        for c in range(chips):
            w = 2 * c + which
            target[c, :each, :] = g_up[w * each : (w + 1) * each, :].astype(kind)
            target[c, each : 2 * each, :] = g_down[w * each : (w + 1) * each, :].astype(kind)
            target[c, 2 * each : 2 * each + few, :] = g_out[w * few : (w + 1) * few, :].astype(kind)

    for which in range(2):

        @pl.when(core[0] == which)
        def _():
            put(kept, which)
            put(sent, 1 - which)


def weight_grads(core, h2, du, act, both, ctx, dc, owners):
    count, width = du.shape
    units = h2.shape[1]
    shape = (owners // 2, 2 * units // owners + 8, width)
    return pl.pallas_call(
        weight_grads_kernel,
        out_shape=(jax.ShapeDtypeStruct(shape, F32), jax.ShapeDtypeStruct(shape, BF16)),
        grid_spec=pltpu.PrefetchScalarGridSpec(
            num_scalar_prefetch=1,
            grid=(1,),
            in_specs=[
                whole(h2.shape),
                whole(du.shape),
                whole(act.shape),
                pl.BlockSpec((count, width), lambda i, *_: (0, 1)),
                whole(ctx.shape),
                whole(dc.shape),
            ],
            out_specs=[whole(shape)] * 2,
            scratch_shapes=[
                pltpu.VMEM((units, width), F32),
                pltpu.VMEM((units, width), F32),
                pltpu.VMEM((ctx.shape[0], width), F32),
            ],
        ),
        compiler_params=params(),
        cost_estimate=pl.CostEstimate(
            flops=4 * h2.size * width, bytes_accessed=6 * units * width, transcendentals=0
        ),
        name="weight_grads",
    )(core, h2, du, act, both, ctx, dc)


def normalized(values):
    mean = jnp.mean(values, axis=-1, keepdims=True)
    centered = values - mean
    spread = jnp.mean(centered * centered, axis=-1, keepdims=True)
    scale = lax.rsqrt(spread + NORM_EPS)
    return centered * scale, scale


def norm_back(grad, gain, normed, scale):
    e = grad * gain
    mean_e = jnp.mean(e, axis=-1, keepdims=True)
    mean_en = jnp.mean(e * normed, axis=-1, keepdims=True)
    return scale * (e - mean_e - normed * mean_en)


def gelu_tanh(values):
    return jax.nn.gelu(values, approximate=True)


def head_lanes(x, heads, first, ones_at=None):
    rows, width = x.shape
    wide = jnp.pad(x, ((0, 0), (first, LANES - width - first))).reshape(2, 1, rows // 2, LANES)
    lane = lax.broadcasted_iota(jnp.int32, (1, heads, 1, LANES), 3)
    head = lax.broadcasted_iota(jnp.int32, (1, heads, 1, LANES), 1)
    start = first + head * HEAD_DIM
    here = jnp.logical_and(lane >= start, lane < start + HEAD_DIM)
    out = jnp.where(here, wide, jnp.zeros((), x.dtype))
    if ones_at is not None:
        at = ones_at + 3 * head
        out = jnp.where(jnp.logical_and(lane >= at, lane < at + 3), jnp.ones((), x.dtype), out)
    return out.reshape(2, heads * rows // 2, LANES)


def to_all(x, axis="ulysses"):
    ways = lax.axis_size(axis)
    sent = jnp.broadcast_to(x[None], (ways,) + x.shape)
    return lax.all_to_all(sent, axis, split_axis=0, concat_axis=0, tiled=True)


def summed_at_owner(x, axis="ulysses"):
    ways = lax.axis_size(axis)
    sent = x.astype(BF16).reshape(ways, -1, x.shape[1])
    got = lax.all_to_all(sent, axis, split_axis=0, concat_axis=0, tiled=True)
    return jnp.sum(got.astype(F32), axis=0)


def other_core(x):
    return lax.ppermute(x, "core", [(0, 1), (1, 0)])


def reduced(x, axis):
    ways = lax.axis_size(axis)
    me = lax.axis_index(axis)

    def rows_of(k):
        return lax.dynamic_index_in_dim(x, lax.rem(me + k, ways), axis=0, keepdims=False)

    got = [
        lax.ppermute(rows_of(k).astype(BF16), axis, [(i, (i + k) % ways) for i in range(ways)])
        for k in range(1, ways)
    ]
    total = rows_of(0).astype(F32)
    for g in got:
        total += g.astype(F32)
    return total


def on_device(
    tokens,
    stretch_order,
    ln_gain,
    ln_bias,
    w_qkv,
    qv_bias,
    w_out,
    out_bias,
    w_up,
    up_bias,
    w_down,
    down_bias,
    cotangent,
):
    own_rows, width = tokens.shape
    ways = lax.axis_size("ulysses")
    wide = lax.axis_size(WIDE)
    me = lax.axis_index("ulysses")
    rows = own_rows * ways
    heads = HEADS // ways
    part = width // ways
    held = w_qkv.shape[1]
    ff_held = w_down.shape[1]
    ff_part = ff_held * wide
    pair = 2 * held

    order = stretch_order[0]
    own = lax.dynamic_slice(order, (2 * lax.axis_index(BLK),), (2,))
    count = order.shape[0]
    index = jnp.arange(count, dtype=jnp.int32)
    slots = jnp.sum(jnp.where(order[None, :] == index[:, None], index[None, :], 0), axis=1)

    small = jnp.concatenate(
        [
            ln_gain,
            ln_bias,
            qv_bias,
            jnp.concatenate([out_bias, down_bias], axis=1),
            up_bias.reshape(2, pair),
        ],
        axis=0,
    )
    qkv_slices = w_qkv[0].reshape(held, 3, ways, part).transpose(2, 0, 1, 3).reshape(ways, held, 3 * part)
    up_slices = w_up[0].reshape(held, wide, ways, ff_held).transpose(2, 0, 1, 3).reshape(ways, held, ff_part)
    first = jnp.concatenate(
        [
            qkv_slices,
            jnp.broadcast_to(small[None], (ways,) + small.shape),
            jnp.zeros((ways, held, width - 3 * part - pair), BF16),
        ],
        axis=2,
    )
    blank = jnp.zeros((ways, 8 - held, width), BF16)
    wide_out = jnp.broadcast_to(w_out[0][None], (ways, held, width))
    sent = jnp.concatenate([first, blank, up_slices, blank, wide_out, blank], axis=1)
    sent, tokens_late, cotangent_late = lax.optimization_barrier((sent, tokens, cotangent))
    got = lax.all_to_all(sent, "ulysses", split_axis=0, concat_axis=0, tiled=True)
    df_own = cotangent_late.astype(BF16)
    both = lax.all_gather(
        jnp.concatenate([tokens_late, df_own], axis=1), "ulysses", axis=0, tiled=True
    )
    matrix = got[:, :held, : 3 * part].reshape(ways * held, 3 * part)
    vector = got[:, :held, 3 * part : 3 * part + pair].transpose(1, 0, 2).reshape(held, ways * pair)
    vector = jnp.pad(vector, ((0, (ways - 1) * held), (0, 64 - ways * pair)))
    piece = jnp.concatenate([matrix, vector], axis=1)
    filled = lax.all_gather(piece, WIDE, axis=0, tiled=True)
    ffn = jnp.concatenate(
        [
            got[:, 8 : 8 + held].reshape(ways * held, width),
            got[:, 16 : 16 + held].reshape(ways * held, width),
            w_down[0],
        ],
        axis=1,
    )
    h1, n1, kv, q_scaled, vec = project(me[None], both, filled, part, wide, ways, pair)
    gains, shifts = vec[0], vec[1]
    halves = vec[3].reshape(wide * ways, 2, held)
    out_bias_all = halves[:, 0].reshape(-1)
    down_bias_all = halves[:, 1].reshape(-1)
    up_bias_u = lax.dynamic_index_in_dim(
        vec[4:6].reshape(2, wide, ways, pair), me, axis=2, keepdims=False
    )
    up_bias_u = up_bias_u.transpose(1, 0, 2).reshape(-1)
    kv_all = lax.all_gather(kv, BLK, axis=0, tiled=True)
    q_heads = head_lanes(q_scaled, heads, 0)
    k_heads = head_lanes(kv[:, :part], heads, EXTRA, 0)
    v_heads = head_lanes(kv[:, part:], heads, EXTRA, 3 * heads)
    q_wide = jnp.pad(q_scaled, ((0, 0), (EXTRA, 0)))
    gain_two = gains[width:]
    vectors = jnp.stack(
        [gain_two, shifts[width:], out_bias_all, up_bias_u] + [jnp.zeros((width,), F32)] * 4
    )
    (ffn, kv_all, slots, own, q_heads, k_heads, v_heads, q_wide, vectors, n1) = (
        lax.optimization_barrier(
            (ffn, kv_all, slots, own, q_heads, k_heads, v_heads, q_wide, vectors, n1)
        )
    )
    ffn_all = lax.all_gather(ffn, WIDE, axis=0, tiled=True)

    ctx_low, ctx, lse = attend(slots, own, q_heads, kv_all, heads)
    ctx_all = to_all(ctx_low).reshape(width, rows)
    q_wide, ctx_all = lax.optimization_barrier((q_wide, ctx_all))
    q_all = lax.all_gather(q_wide, BLK, axis=0, tiled=True)
    x2_own, h2, act, du, dh2, down = feed_forward(
        me[None], both, ctx_all, vectors, ffn_all, ways
    )
    dh2 = summed_at_owner(dh2)
    ctx_rows = lax.dynamic_index_in_dim(
        ctx_all.reshape(wide, ways, held, rows), me, axis=1, keepdims=False
    ).reshape(part, rows)
    w_out_u = lax.dynamic_slice(ffn_all, (me * part, width), (part, width))
    g_up_bias = jnp.sum(du.astype(F32), axis=0)
    g_down_bias = jnp.sum(df_own.astype(F32), axis=0)

    n2_own, r2_own = normalized(x2_own)
    dx2 = cotangent + norm_back(dh2, gain_two, n2_own, r2_own)
    g_gain_two = jnp.sum(dh2 * n2_own, axis=0)
    g_shift_two = jnp.sum(dh2, axis=0)
    dc_own = dx2.astype(BF16)
    g_out_bias = jnp.sum(dc_own.astype(F32), axis=0)
    owners = wide * ways
    blank = jnp.zeros((width,), F32)
    small_grads = jnp.stack(
        [
            jnp.concatenate([blank, g_gain_two]).reshape(wide, -1),
            jnp.concatenate([blank, g_shift_two]).reshape(wide, -1),
            jnp.zeros((wide, ways * pair), F32),
            jnp.concatenate(
                [g_out_bias.reshape(owners, held), g_down_bias.reshape(owners, held)], axis=1
            ).reshape(wide, -1),
        ],
        axis=1,
    )
    g_up_full = jnp.zeros((wide, 2, ways, pair), F32)
    g_up_full = lax.dynamic_update_slice(
        g_up_full, g_up_bias.reshape(wide, 2, 1, pair), (0, 0, me, 0)
    )
    small_grads = jnp.concatenate([small_grads, g_up_full.reshape(wide, 2, ways * pair)], axis=1)
    small_grads = jnp.pad(small_grads, ((0, 0), (0, 2), (0, 128 - ways * pair)))
    dc = to_all(dc_own).reshape(rows, width)
    dc, q_all, small_grads, ctx_rows = lax.optimization_barrier((dc, q_all, small_grads, ctx_rows))
    w_out_u = lax.dynamic_slice(ffn_all, (me * part, width), (part, width))

    w_out_wide = jnp.pad(w_out_u, ((EXTRA, 0), (0, 0)))
    packed, q_ext, d_ext = prepare(dc, w_out_wide, ctx, lse, q_heads, heads)
    packed_all = lax.all_gather(packed, BLK, axis=0, tiled=True)
    core = lax.axis_index("core")
    early, early_sent = weight_grads(core[None], h2, du, act, both, ctx_rows, dc, wide)
    early = (early + other_core(early_sent).astype(F32)).astype(BF16)
    early, q_ext = lax.optimization_barrier((early, q_ext))
    d_query = query_grad(slots, own, q_ext, d_ext, kv_all, heads)
    early, packed_all, d_query = lax.optimization_barrier((early, packed_all, d_query))
    early = lax.all_to_all(early, CHIPS, split_axis=0, concat_axis=0, tiled=True)
    d_key, d_value = key_grad(slots, own, k_heads, v_heads, q_all, packed_all, heads)
    early, d_value = lax.optimization_barrier((early, d_value))
    early = jnp.sum(early.astype(F32), axis=0)
    terms, late, late_sent = finish(
        core[None], me[None], d_query, d_key, d_value, h1, n1, filled, small_grads
    )
    terms, late_got = lax.optimization_barrier((terms, other_core(late_sent)))
    pair_sums = reduced(
        jnp.concatenate([terms, down], axis=1).reshape(ways, own_rows, 2 * width), "ulysses"
    )
    dh1 = pair_sums[:, :width]
    result = pair_sums[:, width:] + x2_own + down_bias_all
    late = (late + late_got.astype(F32)).astype(BF16)
    late = lax.all_to_all(late, CHIPS, split_axis=0, concat_axis=0, tiled=True)
    late = jnp.sum(late.astype(F32), axis=0)
    n1_own, r1_own = normalized(tokens.astype(F32))
    d_tokens = dx2 + norm_back(dh1, gains[:width], n1_own, r1_own)

    small_rows = late[ways * held : ways * held + 6, : ways * pair].reshape(6, ways, pair)
    last = jnp.concatenate(
        [
            late[: ways * held, : 3 * part].reshape(ways, held, 3 * part),
            jnp.pad(small_rows.transpose(1, 0, 2), ((0, 0), (0, 0), (0, 64 - pair))),
            early[:ff_held].reshape(ways, held, -1),
        ],
        axis=2,
    )
    last = lax.all_to_all(last, "ulysses", split_axis=0, concat_axis=0, tiled=True)
    o_w_qkv = last[:, :, : 3 * part].reshape(ways, held, 3, part).transpose(1, 2, 0, 3)
    o_small = jnp.sum(last[:, :, 3 * part : 3 * part + pair], axis=0)
    o_w_up = last[:, :, 3 * part + 64 :].reshape(ways, held, wide, ff_held).transpose(1, 2, 0, 3)
    return (
        result,
        d_tokens,
        o_small[0:1],
        o_small[1:2],
        o_w_qkv.reshape(1, held, 3 * width),
        o_small[2:3],
        early[None, 2 * ff_held : 2 * ff_held + held],
        o_small[3:4, :held],
        o_w_up.reshape(1, held, -1),
        o_small[4:6].reshape(1, ff_held),
        early[None, ff_held : 2 * ff_held],
        o_small[3:4, held:],
    )


def solution(mesh):
    chips_z = mesh.shape["blk"] // 4
    parts = Mesh(
        mesh.devices.reshape(mesh.shape["batch"], 2, chips_z, 2, mesh.shape["ulysses"]), ALL
    )
    rows = P(ALL, None)
    flat = P(None, ALL)
    deep = P(None, ALL, None)
    return jax.shard_map(
        on_device,
        mesh=parts,
        in_specs=(
            rows, P("batch", None), flat, flat, deep, flat, deep, flat, deep, flat, deep, flat, rows,
        ),
        out_specs=(rows, rows, flat, flat, deep, flat, deep, flat, deep, flat, deep, flat),
        check_vma=False,
    )
```

```python
import functools
import math

import jax
import jax.numpy as jnp
from jax import lax
from jax.experimental import pallas as pl
from jax.experimental.pallas import tpu as pltpu
from jax.sharding import Mesh, PartitionSpec as P

HEADS = 12
HEAD_DIM = 64
NORM_EPS = 1e-05
FLOOR = -1e25
LARGEST_SUM = 1e25
LANES = 256
EXTRA = 64
BELOW_FLOOR = -1e30
BLK = ("xlo", "z", "core")
CHIPS = ("batch", "xlo", "z")
WIDE = ("batch", "xlo", "z", "core")
ALL = ("batch", "xlo", "z", "core", "ulysses")
BF16 = jnp.bfloat16
F32 = jnp.float32
NT = (((1,), (1,)), ((), ()))
VMEM_LIMIT = 60 * 1024 * 1024


def mm(a, b):
    return jnp.dot(a, b, preferred_element_type=F32)


def mm_nt(a, b):
    return lax.dot_general(a, b, NT, preferred_element_type=F32)


def mm_tn(a, b):
    return lax.dot_general(a, b, (((0,), (0,)), ((), ())), preferred_element_type=F32)


def stretch(index, half):
    return pl.ds(pl.multiple_of(index * half, half), half)


def lanes_of(rows):
    return lax.broadcasted_iota(jnp.int32, (rows, LANES), 1)


def ones_after(k, first):
    return jnp.where(lanes_of(k.shape[0]) < first, k, jnp.ones_like(k))


def ones_before(v):
    return jnp.where(lanes_of(v.shape[0]) < EXTRA, jnp.ones_like(v), v)


def three(x):
    high = x.astype(BF16).astype(F32)
    mid = (x - high).astype(BF16).astype(F32)
    return high, mid, x - high - mid


def causal(half, heads, keys_first):
    rows = lax.broadcasted_iota(jnp.int32, (heads * half, half), 0) & (half - 1)
    cols = lax.broadcasted_iota(jnp.int32, (heads * half, half), 1)
    return rows <= cols if keys_first else cols <= rows


def merged_heads(stacked, half, heads, first):
    lane = lanes_of(half)
    out = stacked[:half]
    for h in range(1, heads):
        out = jnp.where(lane < first + h * HEAD_DIM, out, stacked[h * half : (h + 1) * half])
    return out


def in_groups(first, count, tiles):
    def eight(i, _):
        tiles([first + 8 * i + j for j in range(8)])
        return 0

    lax.fori_loop(0, count // 8, eight, 0)
    for size in (4, 2, 1):

        @pl.when((count & size) != 0)
        def _():
            begin = first + (count & ~(2 * size - 1))
            tiles([begin + j for j in range(size)])


def one_ahead(items, produce, consume):
    ready = produce(items[0])
    for n, item in enumerate(items):
        now = ready
        if n + 1 < len(items):
            ready = produce(items[n + 1])
        consume(item, now)


def attend_kernel(
    slots, own, q_heads, kv, ctx_low, ctx, lse, shift, total, q_ext, *, half, heads
):
    deep = heads * half
    lane = lanes_of(deep)

    def one_half(part, _):
        rank_own = own[part]
        mask = causal(half, heads, False)
        here = stretch(slots[rank_own], half)
        scores = jnp.where(mask, mm_nt(q_heads[part], kv[here, :LANES]), BELOW_FLOOR)
        first = jnp.max(scores, axis=1, keepdims=True).astype(BF16).astype(F32)
        shift[...] = first
        q_ext[...] = jnp.where(lane == heads * HEAD_DIM, -first, q_heads[part].astype(F32)).astype(
            BF16
        )
        total[...] = mm(jnp.exp(scores - first).astype(BF16), ones_before(kv[here, 128:]))

        def tiles(ranks):
            at = [stretch(slots[r], half) for r in ranks]
            added = [total[...]]

            def produce(a):
                return mm_nt(q_ext[...], ones_after(kv[a, :LANES], heads * HEAD_DIM))

            def consume(a, above):
                added[0] += mm(jnp.exp(above).astype(BF16), ones_before(kv[a, 128:]))

            one_ahead(at, produce, consume)
            total[...] = added[0]

        in_groups(0, rank_own, tiles)

        @pl.when(jnp.logical_not(jnp.max(total[:, :EXTRA]) < LARGEST_SUM))
        def _():
            shift[...] = jnp.full_like(shift, FLOOR)
            total[...] = jnp.zeros_like(total)

            def again(rank, _):
                a = stretch(slots[rank], half)
                allowed = jnp.logical_or(mask, rank < rank_own)
                scores = jnp.where(allowed, mm_nt(q_heads[part], kv[a, :LANES]), BELOW_FLOOR)
                new = jnp.maximum(shift[...], jnp.max(scores, axis=1, keepdims=True))
                total[...] = total[...] * jnp.exp(shift[...] - new) + mm(
                    jnp.exp(scores - new).astype(BF16), ones_before(kv[a, 128:])
                )
                shift[...] = new
                return 0

            lax.fori_loop(0, rank_own + 1, again, 0)

        row_sum = total[:, :1]
        lse[part] = shift[...] + jnp.log(row_sum)
        done = merged_heads(total[...] / row_sum, half, heads, EXTRA)
        rows = stretch(part, half)
        ctx[rows, :] = done
        ctx_low[:, rows] = done.T[EXTRA:, :].astype(BF16)
        return 0

    lax.fori_loop(0, 2, one_half, 0)


def query_grad_kernel(
    slots, own, q_heads, packed, kv, d_query, total, q_ext, d_ext, *, half, heads
):
    lane = lanes_of(half)

    def one_half(part, _):
        rank_own = own[part]
        total[...] = jnp.zeros_like(total)
        grads = packed[stretch(part, half), :].astype(F32)
        for h in range(heads):
            deep = slice(h * half, (h + 1) * half)
            first = EXTRA + h * HEAD_DIM
            q_new = q_heads[part, deep, :].astype(F32)
            d_new = jnp.where(
                jnp.logical_and(lane >= first, lane < first + HEAD_DIM), grads, 0.0
            )
            for i in range(3):
                at = 3 * h + i
                q_new = jnp.where(lane == heads * HEAD_DIM + i, grads[:, at : at + 1], q_new)
                at += 3 * heads
                d_new = jnp.where(lane == i, grads[:, at : at + 1], d_new)
            q_ext[deep, :] = q_new.astype(BF16)
            d_ext[deep, :] = d_new.astype(BF16)

        def tiles(ranks, mask=None):
            at = [stretch(slots[r], half) for r in ranks]
            added = [total[...]]

            def produce(a):
                return (
                    mm_nt(q_ext[...], ones_after(kv[a, :LANES], heads * HEAD_DIM)),
                    mm_nt(d_ext[...], ones_before(kv[a, 128:])),
                )

            def consume(a, ready):
                probs = jnp.exp(ready[0])
                if mask is not None:
                    probs = jnp.where(mask, probs, 0.0)
                added[0] += mm((probs * ready[1]).astype(BF16), kv[a, :LANES])

            one_ahead(at, produce, consume)
            total[...] = added[0]

        in_groups(0, rank_own, tiles)
        tiles([rank_own], causal(half, heads, False))
        done = merged_heads(total[...], half, heads, 0)
        d_query[stretch(part, half), :] = (done * (1.0 / math.sqrt(HEAD_DIM))).astype(BF16)
        return 0

    lax.fori_loop(0, 2, one_half, 0)


def key_grad_kernel(
    slots, own, k_heads, v_heads, q_all, p_all, d_key, d_value, k_sum, v_sum, *, half, heads
):
    count = slots.shape[0]
    lane = lanes_of(half)

    def one_half(part, _):
        rank_own = own[part]
        k_sum[...] = jnp.zeros_like(k_sum)
        v_sum[...] = jnp.zeros_like(v_sum)

        def tiles(ranks, mask=None):
            at = [stretch(slots[r], half) for r in ranks]
            added = [k_sum[...], v_sum[...]]

            def produce(a):
                return (
                    mm_nt(k_heads[part], jnp.where(lane < EXTRA, p_all[a, :], q_all[a, :])),
                    mm_nt(v_heads[part], p_all[a, :]),
                )

            def consume(a, ready):
                probs = jnp.exp(ready[0])
                if mask is not None:
                    probs = jnp.where(mask, probs, 0.0)
                added[1] += mm(probs.astype(BF16), p_all[a, :])
                added[0] += mm((probs * ready[1]).astype(BF16), q_all[a, :])

            one_ahead(at, produce, consume)
            k_sum[...], v_sum[...] = added

        tiles([rank_own], causal(half, heads, True))
        in_groups(rank_own + 1, count - 1 - rank_own, tiles)
        rows = stretch(part, half)
        d_key[rows, :] = merged_heads(k_sum[...], half, heads, EXTRA).astype(BF16)
        d_value[rows, :] = merged_heads(v_sum[...], half, heads, EXTRA)[:, EXTRA:].astype(BF16)
        return 0

    lax.fori_loop(0, 2, one_half, 0)


def prepare_kernel(dc, w_out, ctx, lse, packed, *, half, heads):
    lane = lanes_of(half)
    d_ctx = mm_nt(dc[...], w_out[...]).astype(BF16).astype(F32)
    for part in range(2):
        rows = slice(part * half, (part + 1) * half)
        grads = d_ctx[rows, :]
        terms = grads * ctx[rows, :]
        for h in range(heads):
            first = EXTRA + h * HEAD_DIM
            here = jnp.logical_and(lane >= first, lane < first + HEAD_DIM)
            delta = jnp.sum(jnp.where(here, terms, 0.0), axis=1, keepdims=True)
            minus_lse = three(-lse[part, h * half : (h + 1) * half, :])
            minus_delta = three(-delta)
            for i in range(3):
                grads = jnp.where(lane == 3 * h + i, minus_lse[i], grads)
                grads = jnp.where(lane == 3 * (heads + h) + i, minus_delta[i], grads)
        packed[rows, :] = grads.astype(BF16)


def project_kernel(me, x, weights, h1, n1, kv, q, vec, bias, *, wide, ways, pair, part):
    count = ways * pair
    each = weights.shape[0] // wide
    for w in range(wide):
        block = weights[w * each : w * each + 8, 512:].astype(F32)
        vec[:, w * count : (w + 1) * count] = block[:, 64 : 64 + count]
    width = x.shape[1]
    bias[...] = jnp.zeros_like(bias)
    for u in range(ways):

        @pl.when(me[0] == u)
        def _():
            bias[0:1, :part] = vec[2:3, u * part : (u + 1) * part]
            bias[0:1, 2 * part : 3 * part] = vec[2:3, width + u * part : width + (u + 1) * part]

    normed, _ = normalized(x[...].astype(F32))
    n1[...] = normed
    h1_low = (normed * vec[0:1, :width] + vec[1:2, :width]).astype(BF16)
    h1[...] = h1_low
    proj = (mm(h1_low, weights[...]) + bias[0:1, :]).astype(BF16)
    q[...] = proj[:, :part] * jnp.asarray(1.0 / math.sqrt(HEAD_DIM), BF16)
    kv[...] = proj[:, part : 3 * part]


def project(me, both, weights, part, wide, ways, pair):
    rows = both.shape[0]
    width = both.shape[1] // 2
    outs = [
        ((rows, width), BF16),
        ((rows, width), F32),
        ((rows, 2 * part), BF16),
        ((rows, part), BF16),
        ((8, wide * ways * pair), F32),
    ]
    return pl.pallas_call(
        functools.partial(project_kernel, wide=wide, ways=ways, pair=pair, part=part),
        out_shape=tuple(jax.ShapeDtypeStruct(s, t) for s, t in outs),
        grid_spec=pltpu.PrefetchScalarGridSpec(
            num_scalar_prefetch=1,
            grid=(1,),
            in_specs=[pl.BlockSpec((rows, width), lambda i, *_: (0, 0)), whole(weights.shape)],
            out_specs=[whole(s) for s, _ in outs],
            scratch_shapes=[pltpu.VMEM((8, weights.shape[1]), F32)],
        ),
        compiler_params=params(),
        cost_estimate=pl.CostEstimate(
            flops=2 * rows * weights.size, bytes_accessed=8 * rows * width, transcendentals=rows
        ),
        name="project",
    )(me, both, weights)


def finish_kernel(
    core, me, d_query, d_key, d_value, h1, n1, weights, small, terms, kept, sent, d_proj, g, rows_of
):
    chips, deep, _ = kept.shape
    lane = lax.broadcasted_iota(jnp.int32, (d_query.shape[0], 128), 1)
    part = d_value.shape[1]
    d_proj[:, :128] = d_query[:, :128]
    d_proj[:, 128:256] = jnp.where(lane < EXTRA, d_query[:, 128:], d_key[:, :128])
    d_proj[:, 256:384] = d_key[:, 128:]
    d_proj[:, 512:] = jnp.zeros_like(d_proj[:, 512:])
    d_proj[:, 384 : 384 + part] = d_value[...]
    dh1 = mm_nt(d_proj[...], weights[...])
    terms[...] = dh1.astype(BF16)
    g[...] = mm_tn(h1[...], d_proj[...])
    gain_row = jnp.sum(dh1 * n1[...], axis=0, keepdims=True)
    shift_row = jnp.sum(dh1, axis=0, keepdims=True)
    sums = jnp.sum(d_proj[...].astype(F32), axis=0, keepdims=True)
    rows_of[...] = small[...]
    count = 2 * chips
    each = h1.shape[1] // count
    wide = 2 * each
    for w in range(count // 2):
        rows_of[w, 0:1, :wide] = gain_row[:, w * wide : (w + 1) * wide]
        rows_of[w, 1:2, :wide] = shift_row[:, w * wide : (w + 1) * wide]
    many = part // wide
    for i in range(many):
        at = many * me[0] + i
        rows_of[at, 2:3, :wide] = sums[:, i * wide : (i + 1) * wide]
        rows_of[count // 2 + at, 2:3, :wide] = sums[:, 384 + i * wide : 384 + (i + 1) * wide]

    def put(target, which):
        target[:, each:, 128:] = jnp.zeros((chips, deep - each, target.shape[2] - 128), target.dtype)
        for c in range(chips):
            w = 2 * c + which
            target[c, :each, :] = g[w * each : (w + 1) * each, :].astype(target.dtype)
            target[c, each:, :128] = rows_of[w].astype(target.dtype)

    for which in range(2):

        @pl.when(core[0] == which)
        def _():
            put(kept, which)
            put(sent, 1 - which)


def finish(core, me, d_query, d_key, d_value, h1, n1, weights, small):
    rows, width = h1.shape
    count = small.shape[0]
    shape = (count // 2, width // count + 8, weights.shape[1])
    return call(
        finish_kernel, "finish", (core, me), (d_query, d_key, d_value, h1, n1, weights, small),
        [((rows, width), BF16), (shape, F32), (shape, BF16)],
        [((rows, weights.shape[1]), BF16), ((width, weights.shape[1]), F32), (small.shape, F32)],
        pl.CostEstimate(flops=4 * weights.size * rows, bytes_accessed=6 * weights.size, transcendentals=0),
    )


def whole(shape):
    return pl.BlockSpec(shape, lambda i, *_: (0,) * len(shape))


def params():
    return pltpu.CompilerParams(
        dimension_semantics=("arbitrary",), vmem_limit_bytes=VMEM_LIMIT
    )


def cost(rows, keys, heads, products):
    area = rows * keys * heads
    return pl.CostEstimate(
        flops=2 * area * 256 * products, bytes_accessed=keys * 768, transcendentals=area
    )


def call(kernel, name, scalars, arrays, outs, scratch, estimate, **static):
    return pl.pallas_call(
        functools.partial(kernel, **static),
        out_shape=tuple(jax.ShapeDtypeStruct(s, t) for s, t in outs),
        grid_spec=pltpu.PrefetchScalarGridSpec(
            num_scalar_prefetch=len(scalars),
            grid=(1,),
            in_specs=[whole(a.shape) for a in arrays],
            out_specs=[whole(s) for s, _ in outs],
            scratch_shapes=[pltpu.VMEM(s, t) for s, t in scratch],
        ),
        compiler_params=params(),
        cost_estimate=estimate,
        name=name,
    )(*scalars, *arrays)


def attend(slots, own, q_heads, kv, heads):
    _, deep, _ = q_heads.shape
    half = deep // heads
    width = heads * HEAD_DIM
    return call(
        attend_kernel, "attend", (slots, own), (q_heads, kv),
        [((width, 2 * half), BF16), ((2 * half, LANES), F32), ((2, deep, 1), F32)],
        [((deep, 1), F32), ((deep, LANES), F32), ((deep, LANES), BF16)],
        cost(2 * half, kv.shape[0], heads, 2), half=half, heads=heads,
    )


def prepare(dc, w_out, ctx, lse, heads):
    half = dc.shape[0] // 2
    return call(
        prepare_kernel, "prepare", (), (dc, w_out, ctx, lse),
        [((2 * half, LANES), BF16)], [],
        pl.CostEstimate(flops=2 * dc.size * LANES, bytes_accessed=8 * ctx.size, transcendentals=0),
        half=half, heads=heads,
    )[0]


def query_grad(slots, own, q_heads, packed, kv, heads):
    _, deep, _ = q_heads.shape
    half = deep // heads
    return call(
        query_grad_kernel, "query_grad", (slots, own), (q_heads, packed, kv),
        [((2 * half, LANES), BF16)],
        [((deep, LANES), F32), ((deep, LANES), BF16), ((deep, LANES), BF16)],
        cost(2 * half, kv.shape[0], heads, 3), half=half, heads=heads,
    )[0]


def key_grad(slots, own, k_heads, v_heads, q_all, p_all, heads):
    _, deep, _ = k_heads.shape
    half = deep // heads
    return call(
        key_grad_kernel, "key_grad", (slots, own), (k_heads, v_heads, q_all, p_all),
        [((2 * half, LANES), BF16), ((2 * half, heads * HEAD_DIM), BF16)], [((deep, LANES), F32)] * 2,
        cost(2 * half, q_all.shape[0], heads, 4), half=half, heads=heads,
    )


def feed_forward_kernel(
    me, x, ctx, df, vectors, w_up, w_out, w_down, x2_own, h2, act, du, dh2, down
):
    total = x[...].astype(F32) + vectors[2:3, :] + mm_tn(ctx[...], w_out[...])

    @pl.when(pl.program_id(0) == me[0])
    def _():
        x2_own[...] = total

    normed, _ = normalized(total)
    h2_low = (normed * vectors[0:1, :] + vectors[1:2, :]).astype(BF16)
    h2[...] = h2_low
    up = mm(h2_low, w_up[...]) + vectors[3:4, :]
    bend = math.sqrt(2.0 / math.pi)
    square = up * up
    turn = jnp.tanh(bend * (up + 0.044715 * square * up))
    half = 0.5 * (1.0 + turn)
    act_low = (up * half).astype(BF16)
    act[...] = act_low
    down[...] = mm(act_low, w_down[...]).astype(BF16)
    slope = half + 0.5 * up * (1.0 - turn * turn) * (bend * (1.0 + 3 * 0.044715 * square))
    du_low = (slope * mm_nt(df[...], w_down[...])).astype(BF16)
    du[...] = du_low
    dh2[...] = mm_nt(du_low, w_up[...]).astype(BF16)


def feed_forward(me, both, ctx, vectors, weights, ways):
    rows = both.shape[0]
    width = both.shape[1] // 2
    step = rows // ways

    def along(c):
        return pl.BlockSpec((step, width), lambda i, *_: (i, c))

    def third(c):
        return pl.BlockSpec((weights.shape[0], width), lambda i, *_: (0, c))

    flat = jax.ShapeDtypeStruct((rows, width), BF16)
    return pl.pallas_call(
        feed_forward_kernel,
        out_shape=(jax.ShapeDtypeStruct((step, width), F32), flat, flat, flat, flat, flat),
        grid_spec=pltpu.PrefetchScalarGridSpec(
            num_scalar_prefetch=1,
            grid=(ways,),
            in_specs=[
                along(0),
                pl.BlockSpec((width, step), lambda i, *_: (0, i)),
                along(1),
                whole(vectors.shape),
                third(0),
                third(1),
                third(2),
            ],
            out_specs=[whole((step, width))] + [along(0)] * 5,
        ),
        compiler_params=params(),
        cost_estimate=pl.CostEstimate(
            flops=10 * rows * width * width, bytes_accessed=6 * width * width, transcendentals=rows * width
        ),
        name="feed_forward",
    )(me, both, ctx, both, vectors, weights, weights, weights)


def weight_grads_kernel(core, h2, du, act, df, ctx, dc, kept, sent, g_up, g_down, g_out):
    chips, rows, width = kept.shape
    each = h2.shape[1] // (2 * chips)
    few = ctx.shape[0] // (2 * chips)
    chunk = h2.shape[1] // 2
    for i in range(2):
        cols = slice(i * chunk, (i + 1) * chunk)
        g_up[cols, :] = mm_tn(h2[:, cols], du[...])
        g_down[cols, :] = mm_tn(act[:, cols], df[...])
    g_out[...] = mm(ctx[...], dc[...])

    def put(target, which):
        kind = target.dtype
        target[:, 2 * each :, :] = jnp.zeros((chips, rows - 2 * each, width), kind)
        for c in range(chips):
            w = 2 * c + which
            target[c, :each, :] = g_up[w * each : (w + 1) * each, :].astype(kind)
            target[c, each : 2 * each, :] = g_down[w * each : (w + 1) * each, :].astype(kind)
            target[c, 2 * each : 2 * each + few, :] = g_out[w * few : (w + 1) * few, :].astype(kind)

    for which in range(2):

        @pl.when(core[0] == which)
        def _():
            put(kept, which)
            put(sent, 1 - which)


def weight_grads(core, h2, du, act, both, ctx, dc, owners):
    count, width = du.shape
    units = h2.shape[1]
    shape = (owners // 2, 2 * units // owners + 8, width)
    return pl.pallas_call(
        weight_grads_kernel,
        out_shape=(jax.ShapeDtypeStruct(shape, F32), jax.ShapeDtypeStruct(shape, BF16)),
        grid_spec=pltpu.PrefetchScalarGridSpec(
            num_scalar_prefetch=1,
            grid=(1,),
            in_specs=[
                whole(h2.shape),
                whole(du.shape),
                whole(act.shape),
                pl.BlockSpec((count, width), lambda i, *_: (0, 1)),
                whole(ctx.shape),
                whole(dc.shape),
            ],
            out_specs=[whole(shape)] * 2,
            scratch_shapes=[
                pltpu.VMEM((units, width), F32),
                pltpu.VMEM((units, width), F32),
                pltpu.VMEM((ctx.shape[0], width), F32),
            ],
        ),
        compiler_params=params(),
        cost_estimate=pl.CostEstimate(
            flops=4 * h2.size * width, bytes_accessed=6 * units * width, transcendentals=0
        ),
        name="weight_grads",
    )(core, h2, du, act, both, ctx, dc)


def normalized(values):
    mean = jnp.mean(values, axis=-1, keepdims=True)
    centered = values - mean
    spread = jnp.mean(centered * centered, axis=-1, keepdims=True)
    scale = lax.rsqrt(spread + NORM_EPS)
    return centered * scale, scale


def norm_back(grad, gain, normed, scale):
    e = grad * gain
    mean_e = jnp.mean(e, axis=-1, keepdims=True)
    mean_en = jnp.mean(e * normed, axis=-1, keepdims=True)
    return scale * (e - mean_e - normed * mean_en)


def gelu_tanh(values):
    return jax.nn.gelu(values, approximate=True)


def head_lanes(x, heads, first, ones_at=None):
    rows, width = x.shape
    wide = jnp.pad(x, ((0, 0), (first, LANES - width - first))).reshape(2, 1, rows // 2, LANES)
    lane = lax.broadcasted_iota(jnp.int32, (1, heads, 1, LANES), 3)
    head = lax.broadcasted_iota(jnp.int32, (1, heads, 1, LANES), 1)
    start = first + head * HEAD_DIM
    here = jnp.logical_and(lane >= start, lane < start + HEAD_DIM)
    out = jnp.where(here, wide, jnp.zeros((), x.dtype))
    if ones_at is not None:
        at = ones_at + 3 * head
        out = jnp.where(jnp.logical_and(lane >= at, lane < at + 3), jnp.ones((), x.dtype), out)
    return out.reshape(2, heads * rows // 2, LANES)


def to_all(x, axis="ulysses"):
    ways = lax.axis_size(axis)
    sent = jnp.broadcast_to(x[None], (ways,) + x.shape)
    return lax.all_to_all(sent, axis, split_axis=0, concat_axis=0, tiled=True)


def summed_at_owner(x, axis="ulysses"):
    ways = lax.axis_size(axis)
    sent = x.astype(BF16).reshape(ways, -1, x.shape[1])
    got = lax.all_to_all(sent, axis, split_axis=0, concat_axis=0, tiled=True)
    return jnp.sum(got.astype(F32), axis=0)


def other_core(x):
    return lax.ppermute(x, "core", [(0, 1), (1, 0)])


def reduced(x, axis):
    ways = lax.axis_size(axis)
    me = lax.axis_index(axis)

    def rows_of(k):
        return lax.dynamic_index_in_dim(x, lax.rem(me + k, ways), axis=0, keepdims=False)

    got = [
        lax.ppermute(rows_of(k).astype(BF16), axis, [(i, (i + k) % ways) for i in range(ways)])
        for k in range(1, ways)
    ]
    total = rows_of(0).astype(F32)
    for g in got:
        total += g.astype(F32)
    return total


def on_device(
    tokens,
    stretch_order,
    ln_gain,
    ln_bias,
    w_qkv,
    qv_bias,
    w_out,
    out_bias,
    w_up,
    up_bias,
    w_down,
    down_bias,
    cotangent,
):
    own_rows, width = tokens.shape
    ways = lax.axis_size("ulysses")
    wide = lax.axis_size(WIDE)
    me = lax.axis_index("ulysses")
    rows = own_rows * ways
    heads = HEADS // ways
    part = width // ways
    held = w_qkv.shape[1]
    ff_held = w_down.shape[1]
    ff_part = ff_held * wide
    pair = 2 * held

    order = stretch_order[0]
    own = lax.dynamic_slice(order, (2 * lax.axis_index(BLK),), (2,))
    count = order.shape[0]
    index = jnp.arange(count, dtype=jnp.int32)
    slots = jnp.sum(jnp.where(order[None, :] == index[:, None], index[None, :], 0), axis=1)

    small = jnp.concatenate(
        [
            ln_gain,
            ln_bias,
            qv_bias,
            jnp.concatenate([out_bias, down_bias], axis=1),
            up_bias.reshape(2, pair),
        ],
        axis=0,
    )
    qkv_slices = w_qkv[0].reshape(held, 3, ways, part).transpose(2, 0, 1, 3).reshape(ways, held, 3 * part)
    sent = jnp.concatenate(
        [
            qkv_slices,
            jnp.broadcast_to(small[None], (ways,) + small.shape),
            jnp.zeros((ways, held, 64 - pair), BF16),
        ],
        axis=2,
    )
    sent, tokens_late, cotangent_late = lax.optimization_barrier((sent, tokens, cotangent))
    got = lax.all_to_all(sent, "ulysses", split_axis=0, concat_axis=0, tiled=True)
    df_own = cotangent_late.astype(BF16)
    both = lax.all_gather(
        jnp.concatenate([tokens_late, df_own], axis=1), "ulysses", axis=0, tiled=True
    )
    matrix = got[:, :held, : 3 * part].reshape(ways * held, 3 * part)
    vector = got[:, :held, 3 * part : 3 * part + pair].transpose(1, 0, 2).reshape(held, ways * pair)
    vector = jnp.pad(vector, ((0, (ways - 1) * held), (0, 64 - ways * pair)))
    piece = jnp.concatenate([matrix, vector], axis=1)
    filled = lax.all_gather(piece, WIDE, axis=0, tiled=True)
    h1, n1, kv, q_scaled, vec = project(me[None], both, filled, part, wide, ways, pair)
    gains, shifts = vec[0], vec[1]
    halves = vec[3].reshape(wide * ways, 2, held)
    out_bias_all = halves[:, 0].reshape(-1)
    down_bias_all = halves[:, 1].reshape(-1)
    up_bias_u = lax.dynamic_index_in_dim(
        vec[4:6].reshape(2, wide, ways, pair), me, axis=2, keepdims=False
    )
    up_bias_u = up_bias_u.transpose(1, 0, 2).reshape(-1)
    kv_all = lax.all_gather(kv, BLK, axis=0, tiled=True)

    up_late, out_late, kv = lax.optimization_barrier((w_up[0], w_out[0], kv))
    up_slices = up_late.reshape(held, wide, ways, ff_held).transpose(2, 0, 1, 3).reshape(ways, held, ff_part)
    sent = jnp.concatenate([up_slices, jnp.broadcast_to(out_late[None], (ways, held, width))], axis=2)
    got = lax.all_to_all(sent, "ulysses", split_axis=0, concat_axis=0, tiled=True)
    ffn = jnp.concatenate([got.reshape(ways * held, ff_part + width), w_down[0]], axis=1)
    q_heads = head_lanes(q_scaled, heads, 0)
    k_heads = head_lanes(kv[:, :part], heads, EXTRA, 0)
    v_heads = head_lanes(kv[:, part:], heads, EXTRA, 3 * heads)
    q_wide = jnp.pad(q_scaled, ((0, 0), (EXTRA, 0)))
    gain_two = gains[width:]
    vectors = jnp.stack(
        [gain_two, shifts[width:], out_bias_all, up_bias_u] + [jnp.zeros((width,), F32)] * 4
    )
    (ffn, kv_all, slots, own, q_heads, k_heads, v_heads, q_wide, vectors, n1) = (
        lax.optimization_barrier(
            (ffn, kv_all, slots, own, q_heads, k_heads, v_heads, q_wide, vectors, n1)
        )
    )
    ffn_all = lax.all_gather(ffn, WIDE, axis=0, tiled=True)

    ctx_low, ctx, lse = attend(slots, own, q_heads, kv_all, heads)
    ctx_all = to_all(ctx_low).reshape(width, rows)
    q_wide, ctx_all = lax.optimization_barrier((q_wide, ctx_all))
    q_all = lax.all_gather(q_wide, BLK, axis=0, tiled=True)
    x2_own, h2, act, du, dh2, down = feed_forward(
        me[None], both, ctx_all, vectors, ffn_all, ways
    )
    dh2 = summed_at_owner(dh2)
    ctx_rows = lax.dynamic_index_in_dim(
        ctx_all.reshape(wide, ways, held, rows), me, axis=1, keepdims=False
    ).reshape(part, rows)
    w_out_u = lax.dynamic_slice(ffn_all, (me * part, width), (part, width))
    g_up_bias = jnp.sum(du.astype(F32), axis=0)
    g_down_bias = jnp.sum(df_own.astype(F32), axis=0)

    n2_own, r2_own = normalized(x2_own)
    dx2 = cotangent + norm_back(dh2, gain_two, n2_own, r2_own)
    g_gain_two = jnp.sum(dh2 * n2_own, axis=0)
    g_shift_two = jnp.sum(dh2, axis=0)
    dc_own = dx2.astype(BF16)
    g_out_bias = jnp.sum(dc_own.astype(F32), axis=0)
    owners = wide * ways
    blank = jnp.zeros((width,), F32)
    small_grads = jnp.stack(
        [
            jnp.concatenate([blank, g_gain_two]).reshape(wide, -1),
            jnp.concatenate([blank, g_shift_two]).reshape(wide, -1),
            jnp.zeros((wide, ways * pair), F32),
            jnp.concatenate(
                [g_out_bias.reshape(owners, held), g_down_bias.reshape(owners, held)], axis=1
            ).reshape(wide, -1),
        ],
        axis=1,
    )
    g_up_full = jnp.zeros((wide, 2, ways, pair), F32)
    g_up_full = lax.dynamic_update_slice(
        g_up_full, g_up_bias.reshape(wide, 2, 1, pair), (0, 0, me, 0)
    )
    small_grads = jnp.concatenate([small_grads, g_up_full.reshape(wide, 2, ways * pair)], axis=1)
    small_grads = jnp.pad(small_grads, ((0, 0), (0, 2), (0, 128 - ways * pair)))
    dc = to_all(dc_own).reshape(rows, width)
    dc, q_all, small_grads, ctx_rows = lax.optimization_barrier((dc, q_all, small_grads, ctx_rows))
    w_out_u = lax.dynamic_slice(ffn_all, (me * part, width), (part, width))

    w_out_wide = jnp.pad(w_out_u, ((EXTRA, 0), (0, 0)))
    packed = prepare(dc, w_out_wide, ctx, lse, heads)
    packed_all = lax.all_gather(packed, BLK, axis=0, tiled=True)
    core = lax.axis_index("core")
    early, early_sent = weight_grads(core[None], h2, du, act, both, ctx_rows, dc, wide)
    early = (early + other_core(early_sent).astype(F32)).astype(BF16)
    early, q_heads = lax.optimization_barrier((early, q_heads))
    d_query = query_grad(slots, own, q_heads, packed, kv_all, heads)
    early, packed_all, d_query = lax.optimization_barrier((early, packed_all, d_query))
    early = lax.all_to_all(early, CHIPS, split_axis=0, concat_axis=0, tiled=True)
    d_key, d_value = key_grad(slots, own, k_heads, v_heads, q_all, packed_all, heads)
    early, d_value = lax.optimization_barrier((early, d_value))
    early = jnp.sum(early.astype(F32), axis=0)
    terms, late, late_sent = finish(
        core[None], me[None], d_query, d_key, d_value, h1, n1, filled, small_grads
    )
    late = (late + other_core(late_sent).astype(F32)).astype(BF16)
    terms, late = lax.optimization_barrier((terms, late))
    late = lax.all_to_all(late, CHIPS, split_axis=0, concat_axis=0, tiled=True)
    late = jnp.sum(late.astype(F32), axis=0)
    pair_sums = reduced(
        jnp.concatenate([terms, down], axis=1).reshape(ways, own_rows, 2 * width), "ulysses"
    )
    dh1 = pair_sums[:, :width]
    result = pair_sums[:, width:] + x2_own + down_bias_all
    n1_own, r1_own = normalized(tokens.astype(F32))
    d_tokens = dx2 + norm_back(dh1, gains[:width], n1_own, r1_own)

    small_rows = late[ways * held : ways * held + 6, : ways * pair].reshape(6, ways, pair)
    last = jnp.concatenate(
        [
            late[: ways * held, : 3 * part].reshape(ways, held, 3 * part),
            jnp.pad(small_rows.transpose(1, 0, 2), ((0, 0), (0, 0), (0, 64 - pair))),
            early[:ff_held].reshape(ways, held, -1),
        ],
        axis=2,
    )
    last = lax.all_to_all(last, "ulysses", split_axis=0, concat_axis=0, tiled=True)
    o_w_qkv = last[:, :, : 3 * part].reshape(ways, held, 3, part).transpose(1, 2, 0, 3)
    o_small = jnp.sum(last[:, :, 3 * part : 3 * part + pair], axis=0)
    o_w_up = last[:, :, 3 * part + 64 :].reshape(ways, held, wide, ff_held).transpose(1, 2, 0, 3)
    return (
        result,
        d_tokens,
        o_small[0:1],
        o_small[1:2],
        o_w_qkv.reshape(1, held, 3 * width),
        o_small[2:3],
        early[None, 2 * ff_held : 2 * ff_held + held],
        o_small[3:4, :held],
        o_w_up.reshape(1, held, -1),
        o_small[4:6].reshape(1, ff_held),
        early[None, ff_held : 2 * ff_held],
        o_small[3:4, held:],
    )


def solution(mesh):
    chips_z = mesh.shape["blk"] // 4
    parts = Mesh(
        mesh.devices.reshape(mesh.shape["batch"], 2, chips_z, 2, mesh.shape["ulysses"]), ALL
    )
    rows = P(ALL, None)
    flat = P(None, ALL)
    deep = P(None, ALL, None)
    return jax.shard_map(
        on_device,
        mesh=parts,
        in_specs=(
            rows, P("batch", None), flat, flat, deep, flat, deep, flat, deep, flat, deep, flat, rows,
        ),
        out_specs=(rows, rows, flat, flat, deep, flat, deep, flat, deep, flat, deep, flat),
        check_vma=False,
    )
```

```python
import functools
import math

import jax
import jax.numpy as jnp
from jax import lax
from jax.experimental import pallas as pl
from jax.experimental.pallas import tpu as pltpu
from jax.sharding import Mesh, PartitionSpec as P

HEADS = 12
HEAD_DIM = 64
NORM_EPS = 1e-05
FLOOR = -1e25
LARGEST_SUM = 1e25
LANES = 256
EXTRA = 64
BELOW_FLOOR = -1e30
BLK = ("xlo", "z", "core")
CHIPS = ("batch", "xlo", "z")
WIDE = ("batch", "xlo", "z", "core")
ALL = ("batch", "xlo", "z", "core", "ulysses")
BF16 = jnp.bfloat16
F32 = jnp.float32
NT = (((1,), (1,)), ((), ()))
VMEM_LIMIT = 60 * 1024 * 1024


def mm(a, b):
    return jnp.dot(a, b, preferred_element_type=F32)


def mm_nt(a, b):
    return lax.dot_general(a, b, NT, preferred_element_type=F32)


def mm_tn(a, b):
    return lax.dot_general(a, b, (((0,), (0,)), ((), ())), preferred_element_type=F32)


def stretch(index, half):
    return pl.ds(pl.multiple_of(index * half, half), half)


def lanes_of(rows):
    return lax.broadcasted_iota(jnp.int32, (rows, LANES), 1)


def ones_after(k, first):
    return jnp.where(lanes_of(k.shape[0]) < first, k, jnp.ones_like(k))


def ones_before(v):
    return jnp.where(lanes_of(v.shape[0]) < EXTRA, jnp.ones_like(v), v)


def three(x):
    high = x.astype(BF16).astype(F32)
    mid = (x - high).astype(BF16).astype(F32)
    return high, mid, x - high - mid


def causal(half, heads, keys_first):
    rows = lax.broadcasted_iota(jnp.int32, (heads * half, half), 0) & (half - 1)
    cols = lax.broadcasted_iota(jnp.int32, (heads * half, half), 1)
    return rows <= cols if keys_first else cols <= rows


def merged_heads(stacked, half, heads, first):
    lane = lanes_of(half)
    out = stacked[:half]
    for h in range(1, heads):
        out = jnp.where(lane < first + h * HEAD_DIM, out, stacked[h * half : (h + 1) * half])
    return out


def in_groups(first, count, tiles):
    def eight(i, _):
        tiles([first + 8 * i + j for j in range(8)])
        return 0

    lax.fori_loop(0, count // 8, eight, 0)
    for size in (4, 2, 1):

        @pl.when((count & size) != 0)
        def _():
            begin = first + (count & ~(2 * size - 1))
            tiles([begin + j for j in range(size)])


def one_ahead(items, produce, consume):
    ready = produce(items[0])
    for n, item in enumerate(items):
        now = ready
        if n + 1 < len(items):
            ready = produce(items[n + 1])
        consume(item, now)


def attend_kernel(
    slots, own, q_heads, kv, ctx_low, ctx, lse, shift, total, q_ext, *, half, heads
):
    deep = heads * half
    lane = lanes_of(deep)

    def one_half(part, _):
        rank_own = own[part]
        mask = causal(half, heads, False)
        here = stretch(slots[rank_own], half)
        scores = jnp.where(mask, mm_nt(q_heads[part], kv[here, :LANES]), BELOW_FLOOR)
        first = jnp.max(scores, axis=1, keepdims=True).astype(BF16).astype(F32)
        shift[...] = first
        q_ext[...] = jnp.where(lane == heads * HEAD_DIM, -first, q_heads[part].astype(F32)).astype(
            BF16
        )
        total[...] = mm(jnp.exp(scores - first).astype(BF16), ones_before(kv[here, 128:]))

        def tiles(ranks):
            at = [stretch(slots[r], half) for r in ranks]
            added = [total[...]]

            def produce(a):
                return mm_nt(q_ext[...], ones_after(kv[a, :LANES], heads * HEAD_DIM))

            def consume(a, above):
                added[0] += mm(jnp.exp(above).astype(BF16), ones_before(kv[a, 128:]))

            one_ahead(at, produce, consume)
            total[...] = added[0]

        in_groups(0, rank_own, tiles)

        @pl.when(jnp.logical_not(jnp.max(total[:, :EXTRA]) < LARGEST_SUM))
        def _():
            shift[...] = jnp.full_like(shift, FLOOR)
            total[...] = jnp.zeros_like(total)

            def again(rank, _):
                a = stretch(slots[rank], half)
                allowed = jnp.logical_or(mask, rank < rank_own)
                scores = jnp.where(allowed, mm_nt(q_heads[part], kv[a, :LANES]), BELOW_FLOOR)
                new = jnp.maximum(shift[...], jnp.max(scores, axis=1, keepdims=True))
                total[...] = total[...] * jnp.exp(shift[...] - new) + mm(
                    jnp.exp(scores - new).astype(BF16), ones_before(kv[a, 128:])
                )
                shift[...] = new
                return 0

            lax.fori_loop(0, rank_own + 1, again, 0)

        row_sum = total[:, :1]
        lse[part] = shift[...] + jnp.log(row_sum)
        done = merged_heads(total[...] / row_sum, half, heads, EXTRA)
        rows = stretch(part, half)
        ctx[rows, :] = done
        ctx_low[:, rows] = done.T[EXTRA:, :].astype(BF16)
        return 0

    lax.fori_loop(0, 2, one_half, 0)


def query_grad_kernel(
    slots, own, q_heads, packed, kv, d_query, total, q_ext, d_ext, *, half, heads
):
    lane = lanes_of(half)

    def one_half(part, _):
        rank_own = own[part]
        total[...] = jnp.zeros_like(total)
        grads = packed[stretch(part, half), :].astype(F32)
        for h in range(heads):
            deep = slice(h * half, (h + 1) * half)
            first = EXTRA + h * HEAD_DIM
            q_new = q_heads[part, deep, :].astype(F32)
            d_new = jnp.where(
                jnp.logical_and(lane >= first, lane < first + HEAD_DIM), grads, 0.0
            )
            for i in range(3):
                at = 3 * h + i
                q_new = jnp.where(lane == heads * HEAD_DIM + i, grads[:, at : at + 1], q_new)
                at += 3 * heads
                d_new = jnp.where(lane == i, grads[:, at : at + 1], d_new)
            q_ext[deep, :] = q_new.astype(BF16)
            d_ext[deep, :] = d_new.astype(BF16)

        def tiles(ranks, mask=None):
            at = [stretch(slots[r], half) for r in ranks]
            added = [total[...]]

            def produce(a):
                return (
                    mm_nt(q_ext[...], ones_after(kv[a, :LANES], heads * HEAD_DIM)),
                    mm_nt(d_ext[...], ones_before(kv[a, 128:])),
                )

            def consume(a, ready):
                probs = jnp.exp(ready[0])
                if mask is not None:
                    probs = jnp.where(mask, probs, 0.0)
                added[0] += mm((probs * ready[1]).astype(BF16), kv[a, :LANES])

            one_ahead(at, produce, consume)
            total[...] = added[0]

        in_groups(0, rank_own, tiles)
        tiles([rank_own], causal(half, heads, False))
        done = merged_heads(total[...], half, heads, 0)
        d_query[stretch(part, half), :] = (done * (1.0 / math.sqrt(HEAD_DIM))).astype(BF16)
        return 0

    lax.fori_loop(0, 2, one_half, 0)


def key_grad_kernel(
    slots, own, k_heads, v_heads, q_all, p_all, d_key, d_value, k_sum, v_sum, *, half, heads
):
    count = slots.shape[0]
    lane = lanes_of(half)

    def one_half(part, _):
        rank_own = own[part]
        k_sum[...] = jnp.zeros_like(k_sum)
        v_sum[...] = jnp.zeros_like(v_sum)

        def tiles(ranks, mask=None):
            at = [stretch(slots[r], half) for r in ranks]
            added = [k_sum[...], v_sum[...]]

            def produce(a):
                return (
                    mm_nt(k_heads[part], jnp.where(lane < EXTRA, p_all[a, :], q_all[a, :])),
                    mm_nt(v_heads[part], p_all[a, :]),
                )

            def consume(a, ready):
                probs = jnp.exp(ready[0])
                if mask is not None:
                    probs = jnp.where(mask, probs, 0.0)
                added[1] += mm(probs.astype(BF16), p_all[a, :])
                added[0] += mm((probs * ready[1]).astype(BF16), q_all[a, :])

            one_ahead(at, produce, consume)
            k_sum[...], v_sum[...] = added

        tiles([rank_own], causal(half, heads, True))
        in_groups(rank_own + 1, count - 1 - rank_own, tiles)
        rows = stretch(part, half)
        d_key[rows, :] = merged_heads(k_sum[...], half, heads, EXTRA).astype(BF16)
        d_value[rows, :] = merged_heads(v_sum[...], half, heads, EXTRA)[:, EXTRA:].astype(BF16)
        return 0

    lax.fori_loop(0, 2, one_half, 0)


def prepare_kernel(dc, w_out, ctx, lse, packed, *, half, heads):
    lane = lanes_of(half)
    d_ctx = mm_nt(dc[...], w_out[...]).astype(BF16).astype(F32)
    for part in range(2):
        rows = slice(part * half, (part + 1) * half)
        grads = d_ctx[rows, :]
        terms = grads * ctx[rows, :]
        for h in range(heads):
            first = EXTRA + h * HEAD_DIM
            here = jnp.logical_and(lane >= first, lane < first + HEAD_DIM)
            delta = jnp.sum(jnp.where(here, terms, 0.0), axis=1, keepdims=True)
            minus_lse = three(-lse[part, h * half : (h + 1) * half, :])
            minus_delta = three(-delta)
            for i in range(3):
                grads = jnp.where(lane == 3 * h + i, minus_lse[i], grads)
                grads = jnp.where(lane == 3 * (heads + h) + i, minus_delta[i], grads)
        packed[rows, :] = grads.astype(BF16)


def project_kernel(me, x, weights, h1, n1, kv, q, vec, bias, *, wide, ways, pair, part):
    count = ways * pair
    each = weights.shape[0] // wide
    for w in range(wide):
        block = weights[w * each : w * each + 8, 512:].astype(F32)
        vec[:, w * count : (w + 1) * count] = block[:, 64 : 64 + count]
    width = x.shape[1]
    bias[...] = jnp.zeros_like(bias)
    for u in range(ways):

        @pl.when(me[0] == u)
        def _():
            bias[0:1, :part] = vec[2:3, u * part : (u + 1) * part]
            bias[0:1, 2 * part : 3 * part] = vec[2:3, width + u * part : width + (u + 1) * part]

    normed, _ = normalized(x[...].astype(F32))
    n1[...] = normed
    h1_low = (normed * vec[0:1, :width] + vec[1:2, :width]).astype(BF16)
    h1[...] = h1_low
    proj = (mm(h1_low, weights[...]) + bias[0:1, :]).astype(BF16)
    q[...] = proj[:, :part] * jnp.asarray(1.0 / math.sqrt(HEAD_DIM), BF16)
    kv[...] = proj[:, part : 3 * part]


def project(me, both, weights, part, wide, ways, pair):
    rows = both.shape[0]
    width = both.shape[1] // 2
    outs = [
        ((rows, width), BF16),
        ((rows, width), F32),
        ((rows, 2 * part), BF16),
        ((rows, part), BF16),
        ((8, wide * ways * pair), F32),
    ]
    return pl.pallas_call(
        functools.partial(project_kernel, wide=wide, ways=ways, pair=pair, part=part),
        out_shape=tuple(jax.ShapeDtypeStruct(s, t) for s, t in outs),
        grid_spec=pltpu.PrefetchScalarGridSpec(
            num_scalar_prefetch=1,
            grid=(1,),
            in_specs=[pl.BlockSpec((rows, width), lambda i, *_: (0, 0)), whole(weights.shape)],
            out_specs=[whole(s) for s, _ in outs],
            scratch_shapes=[pltpu.VMEM((8, weights.shape[1]), F32)],
        ),
        compiler_params=params(),
        cost_estimate=pl.CostEstimate(
            flops=2 * rows * weights.size, bytes_accessed=8 * rows * width, transcendentals=rows
        ),
        name="project",
    )(me, both, weights)


def finish_kernel(
    core, me, d_query, d_key, d_value, h1, n1, weights, small, terms, kept, sent, d_proj, g, rows_of
):
    chips, deep, _ = kept.shape
    lane = lax.broadcasted_iota(jnp.int32, (d_query.shape[0], 128), 1)
    part = d_value.shape[1]
    d_proj[:, :128] = d_query[:, :128]
    d_proj[:, 128:256] = jnp.where(lane < EXTRA, d_query[:, 128:], d_key[:, :128])
    d_proj[:, 256:384] = d_key[:, 128:]
    d_proj[:, 512:] = jnp.zeros_like(d_proj[:, 512:])
    d_proj[:, 384 : 384 + part] = d_value[...]
    dh1 = mm_nt(d_proj[...], weights[...])
    terms[...] = dh1.astype(BF16)
    g[...] = mm_tn(h1[...], d_proj[...])
    gain_row = jnp.sum(dh1 * n1[...], axis=0, keepdims=True)
    shift_row = jnp.sum(dh1, axis=0, keepdims=True)
    sums = jnp.sum(d_proj[...].astype(F32), axis=0, keepdims=True)
    rows_of[...] = small[...]
    count = 2 * chips
    each = h1.shape[1] // count
    wide = 2 * each
    for w in range(count // 2):
        rows_of[w, 0:1, :wide] = gain_row[:, w * wide : (w + 1) * wide]
        rows_of[w, 1:2, :wide] = shift_row[:, w * wide : (w + 1) * wide]
    many = part // wide
    for i in range(many):
        at = many * me[0] + i
        rows_of[at, 2:3, :wide] = sums[:, i * wide : (i + 1) * wide]
        rows_of[count // 2 + at, 2:3, :wide] = sums[:, 384 + i * wide : 384 + (i + 1) * wide]

    def put(target, which):
        target[:, each:, 128:] = jnp.zeros((chips, deep - each, target.shape[2] - 128), target.dtype)
        for c in range(chips):
            w = 2 * c + which
            target[c, :each, :] = g[w * each : (w + 1) * each, :].astype(target.dtype)
            target[c, each:, :128] = rows_of[w].astype(target.dtype)

    for which in range(2):

        @pl.when(core[0] == which)
        def _():
            put(kept, which)
            put(sent, 1 - which)


def finish(core, me, d_query, d_key, d_value, h1, n1, weights, small):
    rows, width = h1.shape
    count = small.shape[0]
    shape = (count // 2, width // count + 8, weights.shape[1])
    return call(
        finish_kernel, "finish", (core, me), (d_query, d_key, d_value, h1, n1, weights, small),
        [((rows, width), BF16), (shape, F32), (shape, BF16)],
        [((rows, weights.shape[1]), BF16), ((width, weights.shape[1]), F32), (small.shape, F32)],
        pl.CostEstimate(flops=4 * weights.size * rows, bytes_accessed=6 * weights.size, transcendentals=0),
    )


def whole(shape):
    return pl.BlockSpec(shape, lambda i, *_: (0,) * len(shape))


def params():
    return pltpu.CompilerParams(
        dimension_semantics=("arbitrary",), vmem_limit_bytes=VMEM_LIMIT
    )


def cost(rows, keys, heads, products):
    area = rows * keys * heads
    return pl.CostEstimate(
        flops=2 * area * 256 * products, bytes_accessed=keys * 768, transcendentals=area
    )


def call(kernel, name, scalars, arrays, outs, scratch, estimate, **static):
    return pl.pallas_call(
        functools.partial(kernel, **static),
        out_shape=tuple(jax.ShapeDtypeStruct(s, t) for s, t in outs),
        grid_spec=pltpu.PrefetchScalarGridSpec(
            num_scalar_prefetch=len(scalars),
            grid=(1,),
            in_specs=[whole(a.shape) for a in arrays],
            out_specs=[whole(s) for s, _ in outs],
            scratch_shapes=[pltpu.VMEM(s, t) for s, t in scratch],
        ),
        compiler_params=params(),
        cost_estimate=estimate,
        name=name,
    )(*scalars, *arrays)


def attend(slots, own, q_heads, kv, heads):
    _, deep, _ = q_heads.shape
    half = deep // heads
    width = heads * HEAD_DIM
    return call(
        attend_kernel, "attend", (slots, own), (q_heads, kv),
        [((width, 2 * half), BF16), ((2 * half, LANES), F32), ((2, deep, 1), F32)],
        [((deep, 1), F32), ((deep, LANES), F32), ((deep, LANES), BF16)],
        cost(2 * half, kv.shape[0], heads, 2), half=half, heads=heads,
    )


def prepare(dc, w_out, ctx, lse, heads):
    half = dc.shape[0] // 2
    return call(
        prepare_kernel, "prepare", (), (dc, w_out, ctx, lse),
        [((2 * half, LANES), BF16)], [],
        pl.CostEstimate(flops=2 * dc.size * LANES, bytes_accessed=8 * ctx.size, transcendentals=0),
        half=half, heads=heads,
    )[0]


def query_grad(slots, own, q_heads, packed, kv, heads):
    _, deep, _ = q_heads.shape
    half = deep // heads
    return call(
        query_grad_kernel, "query_grad", (slots, own), (q_heads, packed, kv),
        [((2 * half, LANES), BF16)],
        [((deep, LANES), F32), ((deep, LANES), BF16), ((deep, LANES), BF16)],
        cost(2 * half, kv.shape[0], heads, 3), half=half, heads=heads,
    )[0]


def key_grad(slots, own, k_heads, v_heads, q_all, p_all, heads):
    _, deep, _ = k_heads.shape
    half = deep // heads
    return call(
        key_grad_kernel, "key_grad", (slots, own), (k_heads, v_heads, q_all, p_all),
        [((2 * half, LANES), BF16), ((2 * half, heads * HEAD_DIM), BF16)], [((deep, LANES), F32)] * 2,
        cost(2 * half, q_all.shape[0], heads, 4), half=half, heads=heads,
    )


def feed_forward_kernel(
    me, x, ctx, df, vectors, w_up, w_out, w_down, x2_own, h2, act, du, dh2, down
):
    total = x[...].astype(F32) + vectors[2:3, :] + mm_tn(ctx[...], w_out[...])

    own_rows = x2_own.shape[0]
    each = total.shape[0] // own_rows
    for i in range(each):

        @pl.when(pl.program_id(0) * each + i == me[0])
        def _():
            x2_own[...] = total[i * own_rows : (i + 1) * own_rows, :]

    normed, _ = normalized(total)
    h2_low = (normed * vectors[0:1, :] + vectors[1:2, :]).astype(BF16)
    h2[...] = h2_low
    up = mm(h2_low, w_up[...]) + vectors[3:4, :]
    bend = math.sqrt(2.0 / math.pi)
    square = up * up
    turn = jnp.tanh(bend * (up + 0.044715 * square * up))
    half = 0.5 * (1.0 + turn)
    act_low = (up * half).astype(BF16)
    act[...] = act_low
    down[...] = mm(act_low, w_down[...]).astype(BF16)
    slope = half + 0.5 * up * (1.0 - turn * turn) * (bend * (1.0 + 3 * 0.044715 * square))
    du_low = (slope * mm_nt(df[...], w_down[...])).astype(BF16)
    du[...] = du_low
    dh2[...] = mm_nt(du_low, w_up[...]).astype(BF16)


def feed_forward(me, both, ctx, vectors, weights, ways):
    rows = both.shape[0]
    width = both.shape[1] // 2
    step = rows // 2

    def along(c):
        return pl.BlockSpec((step, width), lambda i, *_: (i, c))

    def third(c):
        return pl.BlockSpec((weights.shape[0], width), lambda i, *_: (0, c))

    flat = jax.ShapeDtypeStruct((rows, width), BF16)
    return pl.pallas_call(
        feed_forward_kernel,
        out_shape=(jax.ShapeDtypeStruct((rows // ways, width), F32), flat, flat, flat, flat, flat),
        grid_spec=pltpu.PrefetchScalarGridSpec(
            num_scalar_prefetch=1,
            grid=(2,),
            in_specs=[
                along(0),
                pl.BlockSpec((width, step), lambda i, *_: (0, i)),
                along(1),
                whole(vectors.shape),
                third(0),
                third(1),
                third(2),
            ],
            out_specs=[whole((rows // ways, width))] + [along(0)] * 5,
        ),
        compiler_params=params(),
        cost_estimate=pl.CostEstimate(
            flops=10 * rows * width * width, bytes_accessed=6 * width * width, transcendentals=rows * width
        ),
        name="feed_forward",
    )(me, both, ctx, both, vectors, weights, weights, weights)


def weight_grads_kernel(core, h2, du, act, df, ctx, dc, kept, sent, g_up, g_down, g_out):
    chips, rows, width = kept.shape
    each = h2.shape[1] // (2 * chips)
    few = ctx.shape[0] // (2 * chips)
    chunk = h2.shape[1] // 2
    for i in range(2):
        cols = slice(i * chunk, (i + 1) * chunk)
        g_up[cols, :] = mm_tn(h2[:, cols], du[...])
        g_down[cols, :] = mm_tn(act[:, cols], df[...])
    g_out[...] = mm(ctx[...], dc[...])

    def put(target, which):
        kind = target.dtype
        target[:, 2 * each :, :] = jnp.zeros((chips, rows - 2 * each, width), kind)
        for c in range(chips):
            w = 2 * c + which
            target[c, :each, :] = g_up[w * each : (w + 1) * each, :].astype(kind)
            target[c, each : 2 * each, :] = g_down[w * each : (w + 1) * each, :].astype(kind)
            target[c, 2 * each : 2 * each + few, :] = g_out[w * few : (w + 1) * few, :].astype(kind)

    for which in range(2):

        @pl.when(core[0] == which)
        def _():
            put(kept, which)
            put(sent, 1 - which)


def weight_grads(core, h2, du, act, both, ctx, dc, owners):
    count, width = du.shape
    units = h2.shape[1]
    shape = (owners // 2, 2 * units // owners + 8, width)
    return pl.pallas_call(
        weight_grads_kernel,
        out_shape=(jax.ShapeDtypeStruct(shape, F32), jax.ShapeDtypeStruct(shape, BF16)),
        grid_spec=pltpu.PrefetchScalarGridSpec(
            num_scalar_prefetch=1,
            grid=(1,),
            in_specs=[
                whole(h2.shape),
                whole(du.shape),
                whole(act.shape),
                pl.BlockSpec((count, width), lambda i, *_: (0, 1)),
                whole(ctx.shape),
                whole(dc.shape),
            ],
            out_specs=[whole(shape)] * 2,
            scratch_shapes=[
                pltpu.VMEM((units, width), F32),
                pltpu.VMEM((units, width), F32),
                pltpu.VMEM((ctx.shape[0], width), F32),
            ],
        ),
        compiler_params=params(),
        cost_estimate=pl.CostEstimate(
            flops=4 * h2.size * width, bytes_accessed=6 * units * width, transcendentals=0
        ),
        name="weight_grads",
    )(core, h2, du, act, both, ctx, dc)


def normalized(values):
    mean = jnp.mean(values, axis=-1, keepdims=True)
    centered = values - mean
    spread = jnp.mean(centered * centered, axis=-1, keepdims=True)
    scale = lax.rsqrt(spread + NORM_EPS)
    return centered * scale, scale


def norm_back(grad, gain, normed, scale):
    e = grad * gain
    mean_e = jnp.mean(e, axis=-1, keepdims=True)
    mean_en = jnp.mean(e * normed, axis=-1, keepdims=True)
    return scale * (e - mean_e - normed * mean_en)


def gelu_tanh(values):
    return jax.nn.gelu(values, approximate=True)


def head_lanes(x, heads, first, ones_at=None):
    rows, width = x.shape
    wide = jnp.pad(x, ((0, 0), (first, LANES - width - first))).reshape(2, 1, rows // 2, LANES)
    lane = lax.broadcasted_iota(jnp.int32, (1, heads, 1, LANES), 3)
    head = lax.broadcasted_iota(jnp.int32, (1, heads, 1, LANES), 1)
    start = first + head * HEAD_DIM
    here = jnp.logical_and(lane >= start, lane < start + HEAD_DIM)
    out = jnp.where(here, wide, jnp.zeros((), x.dtype))
    if ones_at is not None:
        at = ones_at + 3 * head
        out = jnp.where(jnp.logical_and(lane >= at, lane < at + 3), jnp.ones((), x.dtype), out)
    return out.reshape(2, heads * rows // 2, LANES)


def to_all(x, axis="ulysses"):
    ways = lax.axis_size(axis)
    sent = jnp.broadcast_to(x[None], (ways,) + x.shape)
    return lax.all_to_all(sent, axis, split_axis=0, concat_axis=0, tiled=True)


def summed_at_owner(x, axis="ulysses"):
    ways = lax.axis_size(axis)
    sent = x.astype(BF16).reshape(ways, -1, x.shape[1])
    got = lax.all_to_all(sent, axis, split_axis=0, concat_axis=0, tiled=True)
    return jnp.sum(got.astype(F32), axis=0)


def other_core(x):
    return lax.ppermute(x, "core", [(0, 1), (1, 0)])


def reduced(x, axis):
    ways = lax.axis_size(axis)
    me = lax.axis_index(axis)

    def rows_of(k):
        return lax.dynamic_index_in_dim(x, lax.rem(me + k, ways), axis=0, keepdims=False)

    got = [
        lax.ppermute(rows_of(k).astype(BF16), axis, [(i, (i + k) % ways) for i in range(ways)])
        for k in range(1, ways)
    ]
    total = rows_of(0).astype(F32)
    for g in got:
        total += g.astype(F32)
    return total


def on_device(
    tokens,
    stretch_order,
    ln_gain,
    ln_bias,
    w_qkv,
    qv_bias,
    w_out,
    out_bias,
    w_up,
    up_bias,
    w_down,
    down_bias,
    cotangent,
):
    own_rows, width = tokens.shape
    ways = lax.axis_size("ulysses")
    wide = lax.axis_size(WIDE)
    me = lax.axis_index("ulysses")
    rows = own_rows * ways
    heads = HEADS // ways
    part = width // ways
    held = w_qkv.shape[1]
    ff_held = w_down.shape[1]
    ff_part = ff_held * wide
    pair = 2 * held

    order = stretch_order[0]
    own = lax.dynamic_slice(order, (2 * lax.axis_index(BLK),), (2,))
    count = order.shape[0]
    index = jnp.arange(count, dtype=jnp.int32)
    slots = jnp.sum(jnp.where(order[None, :] == index[:, None], index[None, :], 0), axis=1)

    small = jnp.concatenate(
        [
            ln_gain,
            ln_bias,
            qv_bias,
            jnp.concatenate([out_bias, down_bias], axis=1),
            up_bias.reshape(2, pair),
        ],
        axis=0,
    )
    qkv_slices = w_qkv[0].reshape(held, 3, ways, part).transpose(2, 0, 1, 3).reshape(ways, held, 3 * part)
    sent = jnp.concatenate(
        [
            qkv_slices,
            jnp.broadcast_to(small[None], (ways,) + small.shape),
            jnp.zeros((ways, held, 64 - pair), BF16),
        ],
        axis=2,
    )
    sent, tokens_late, cotangent_late = lax.optimization_barrier((sent, tokens, cotangent))
    got = lax.all_to_all(sent, "ulysses", split_axis=0, concat_axis=0, tiled=True)
    df_own = cotangent_late.astype(BF16)
    both = lax.all_gather(
        jnp.concatenate([tokens_late, df_own], axis=1), "ulysses", axis=0, tiled=True
    )
    matrix = got[:, :held, : 3 * part].reshape(ways * held, 3 * part)
    vector = got[:, :held, 3 * part : 3 * part + pair].transpose(1, 0, 2).reshape(held, ways * pair)
    vector = jnp.pad(vector, ((0, (ways - 1) * held), (0, 64 - ways * pair)))
    piece = jnp.concatenate([matrix, vector], axis=1)
    filled = lax.all_gather(piece, WIDE, axis=0, tiled=True)
    h1, n1, kv, q_scaled, vec = project(me[None], both, filled, part, wide, ways, pair)
    gains, shifts = vec[0], vec[1]
    halves = vec[3].reshape(wide * ways, 2, held)
    out_bias_all = halves[:, 0].reshape(-1)
    down_bias_all = halves[:, 1].reshape(-1)
    up_bias_u = lax.dynamic_index_in_dim(
        vec[4:6].reshape(2, wide, ways, pair), me, axis=2, keepdims=False
    )
    up_bias_u = up_bias_u.transpose(1, 0, 2).reshape(-1)
    kv_all = lax.all_gather(kv, BLK, axis=0, tiled=True)

    up_late, out_late, kv = lax.optimization_barrier((w_up[0], w_out[0], kv))
    up_slices = up_late.reshape(held, wide, ways, ff_held).transpose(2, 0, 1, 3).reshape(ways, held, ff_part)
    sent = jnp.concatenate([up_slices, jnp.broadcast_to(out_late[None], (ways, held, width))], axis=2)
    got = lax.all_to_all(sent, "ulysses", split_axis=0, concat_axis=0, tiled=True)
    ffn = jnp.concatenate([got.reshape(ways * held, ff_part + width), w_down[0]], axis=1)
    q_heads = head_lanes(q_scaled, heads, 0)
    k_heads = head_lanes(kv[:, :part], heads, EXTRA, 0)
    v_heads = head_lanes(kv[:, part:], heads, EXTRA, 3 * heads)
    q_wide = jnp.pad(q_scaled, ((0, 0), (EXTRA, 0)))
    gain_two = gains[width:]
    vectors = jnp.stack(
        [gain_two, shifts[width:], out_bias_all, up_bias_u] + [jnp.zeros((width,), F32)] * 4
    )
    (ffn, kv_all, slots, own, q_heads, k_heads, v_heads, q_wide, vectors, n1) = (
        lax.optimization_barrier(
            (ffn, kv_all, slots, own, q_heads, k_heads, v_heads, q_wide, vectors, n1)
        )
    )
    ffn_all = lax.all_gather(ffn, WIDE, axis=0, tiled=True)

    ctx_low, ctx, lse = attend(slots, own, q_heads, kv_all, heads)
    ctx_all = to_all(ctx_low).reshape(width, rows)
    q_wide, ctx_all = lax.optimization_barrier((q_wide, ctx_all))
    q_all = lax.all_gather(q_wide, BLK, axis=0, tiled=True)
    x2_own, h2, act, du, dh2, down = feed_forward(
        me[None], both, ctx_all, vectors, ffn_all, ways
    )
    dh2 = summed_at_owner(dh2)
    ctx_rows = lax.dynamic_index_in_dim(
        ctx_all.reshape(wide, ways, held, rows), me, axis=1, keepdims=False
    ).reshape(part, rows)
    w_out_u = lax.dynamic_slice(ffn_all, (me * part, width), (part, width))
    g_up_bias = jnp.sum(du.astype(F32), axis=0)
    g_down_bias = jnp.sum(df_own.astype(F32), axis=0)

    n2_own, r2_own = normalized(x2_own)
    dx2 = cotangent + norm_back(dh2, gain_two, n2_own, r2_own)
    g_gain_two = jnp.sum(dh2 * n2_own, axis=0)
    g_shift_two = jnp.sum(dh2, axis=0)
    dc_own = dx2.astype(BF16)
    g_out_bias = jnp.sum(dc_own.astype(F32), axis=0)
    owners = wide * ways
    blank = jnp.zeros((width,), F32)
    small_grads = jnp.stack(
        [
            jnp.concatenate([blank, g_gain_two]).reshape(wide, -1),
            jnp.concatenate([blank, g_shift_two]).reshape(wide, -1),
            jnp.zeros((wide, ways * pair), F32),
            jnp.concatenate(
                [g_out_bias.reshape(owners, held), g_down_bias.reshape(owners, held)], axis=1
            ).reshape(wide, -1),
        ],
        axis=1,
    )
    g_up_full = jnp.zeros((wide, 2, ways, pair), F32)
    g_up_full = lax.dynamic_update_slice(
        g_up_full, g_up_bias.reshape(wide, 2, 1, pair), (0, 0, me, 0)
    )
    small_grads = jnp.concatenate([small_grads, g_up_full.reshape(wide, 2, ways * pair)], axis=1)
    small_grads = jnp.pad(small_grads, ((0, 0), (0, 2), (0, 128 - ways * pair)))
    dc = to_all(dc_own).reshape(rows, width)
    dc, q_all, small_grads, ctx_rows = lax.optimization_barrier((dc, q_all, small_grads, ctx_rows))
    w_out_u = lax.dynamic_slice(ffn_all, (me * part, width), (part, width))

    w_out_wide = jnp.pad(w_out_u, ((EXTRA, 0), (0, 0)))
    packed = prepare(dc, w_out_wide, ctx, lse, heads)
    packed_all = lax.all_gather(packed, BLK, axis=0, tiled=True)
    core = lax.axis_index("core")
    early, early_sent = weight_grads(core[None], h2, du, act, both, ctx_rows, dc, wide)
    early = (early + other_core(early_sent).astype(F32)).astype(BF16)
    early, q_heads = lax.optimization_barrier((early, q_heads))
    d_query = query_grad(slots, own, q_heads, packed, kv_all, heads)
    early, packed_all, d_query = lax.optimization_barrier((early, packed_all, d_query))
    early = lax.all_to_all(early, CHIPS, split_axis=0, concat_axis=0, tiled=True)
    d_key, d_value = key_grad(slots, own, k_heads, v_heads, q_all, packed_all, heads)
    early, d_value = lax.optimization_barrier((early, d_value))
    early = jnp.sum(early.astype(F32), axis=0)
    terms, late, late_sent = finish(
        core[None], me[None], d_query, d_key, d_value, h1, n1, filled, small_grads
    )
    late = (late + other_core(late_sent).astype(F32)).astype(BF16)
    terms, late = lax.optimization_barrier((terms, late))
    late = lax.all_to_all(late, CHIPS, split_axis=0, concat_axis=0, tiled=True)
    late = jnp.sum(late.astype(F32), axis=0)
    pair_sums = reduced(
        jnp.concatenate([terms, down], axis=1).reshape(ways, own_rows, 2 * width), "ulysses"
    )
    dh1 = pair_sums[:, :width]
    result = pair_sums[:, width:] + x2_own + down_bias_all
    n1_own, r1_own = normalized(tokens.astype(F32))
    d_tokens = dx2 + norm_back(dh1, gains[:width], n1_own, r1_own)

    small_rows = late[ways * held : ways * held + 6, : ways * pair].reshape(6, ways, pair)
    last = jnp.concatenate(
        [
            late[: ways * held, : 3 * part].reshape(ways, held, 3 * part),
            jnp.pad(small_rows.transpose(1, 0, 2), ((0, 0), (0, 0), (0, 64 - pair))),
            early[:ff_held].reshape(ways, held, -1),
        ],
        axis=2,
    )
    last = lax.all_to_all(last, "ulysses", split_axis=0, concat_axis=0, tiled=True)
    o_w_qkv = last[:, :, : 3 * part].reshape(ways, held, 3, part).transpose(1, 2, 0, 3)
    o_small = jnp.sum(last[:, :, 3 * part : 3 * part + pair], axis=0)
    o_w_up = last[:, :, 3 * part + 64 :].reshape(ways, held, wide, ff_held).transpose(1, 2, 0, 3)
    return (
        result,
        d_tokens,
        o_small[0:1],
        o_small[1:2],
        o_w_qkv.reshape(1, held, 3 * width),
        o_small[2:3],
        early[None, 2 * ff_held : 2 * ff_held + held],
        o_small[3:4, :held],
        o_w_up.reshape(1, held, -1),
        o_small[4:6].reshape(1, ff_held),
        early[None, ff_held : 2 * ff_held],
        o_small[3:4, held:],
    )


def solution(mesh):
    chips_z = mesh.shape["blk"] // 4
    parts = Mesh(
        mesh.devices.reshape(mesh.shape["batch"], 2, chips_z, 2, mesh.shape["ulysses"]), ALL
    )
    rows = P(ALL, None)
    flat = P(None, ALL)
    deep = P(None, ALL, None)
    return jax.shard_map(
        on_device,
        mesh=parts,
        in_specs=(
            rows, P("batch", None), flat, flat, deep, flat, deep, flat, deep, flat, deep, flat, rows,
        ),
        out_specs=(rows, rows, flat, flat, deep, flat, deep, flat, deep, flat, deep, flat),
        check_vma=False,
    )
```

```python
import functools
import math

import jax
import jax.numpy as jnp
from jax import lax
from jax.experimental import pallas as pl
from jax.experimental.pallas import tpu as pltpu
from jax.sharding import Mesh, PartitionSpec as P

HEADS = 12
HEAD_DIM = 64
NORM_EPS = 1e-05
FLOOR = -1e25
LARGEST_SUM = 1e25
LANES = 256
EXTRA = 64
BELOW_FLOOR = -1e30
BLK = ("xlo", "z", "core")
CHIPS = ("batch", "xlo", "z")
WIDE = ("batch", "xlo", "z", "core")
ALL = ("batch", "xlo", "z", "core", "ulysses")
BF16 = jnp.bfloat16
F32 = jnp.float32
NT = (((1,), (1,)), ((), ()))
VMEM_LIMIT = 60 * 1024 * 1024


def mm(a, b):
    return jnp.dot(a, b, preferred_element_type=F32)


def mm_nt(a, b):
    return lax.dot_general(a, b, NT, preferred_element_type=F32)


def mm_tn(a, b):
    return lax.dot_general(a, b, (((0,), (0,)), ((), ())), preferred_element_type=F32)


def stretch(index, half):
    return pl.ds(pl.multiple_of(index * half, half), half)


def lanes_of(rows):
    return lax.broadcasted_iota(jnp.int32, (rows, LANES), 1)


def ones_after(k, first):
    return jnp.where(lanes_of(k.shape[0]) < first, k, jnp.ones_like(k))


def ones_before(v):
    return jnp.where(lanes_of(v.shape[0]) < EXTRA, jnp.ones_like(v), v)


def three(x):
    high = x.astype(BF16).astype(F32)
    mid = (x - high).astype(BF16).astype(F32)
    return high, mid, x - high - mid


def causal(half, heads, keys_first):
    rows = lax.broadcasted_iota(jnp.int32, (heads * half, half), 0) & (half - 1)
    cols = lax.broadcasted_iota(jnp.int32, (heads * half, half), 1)
    return rows <= cols if keys_first else cols <= rows


def merged_heads(stacked, half, heads, first):
    lane = lanes_of(half)
    out = stacked[:half]
    for h in range(1, heads):
        out = jnp.where(lane < first + h * HEAD_DIM, out, stacked[h * half : (h + 1) * half])
    return out


def in_groups(first, count, tiles):
    def sixteen(i, _):
        tiles([first + 16 * i + j for j in range(16)])
        return 0

    lax.fori_loop(0, count // 16, sixteen, 0)
    for size in (8, 4, 2, 1):

        @pl.when((count & size) != 0)
        def _():
            begin = first + (count & ~(2 * size - 1))
            tiles([begin + j for j in range(size)])


def one_ahead(items, produce, consume):
    ready = produce(items[0])
    for n, item in enumerate(items):
        now = ready
        if n + 1 < len(items):
            ready = produce(items[n + 1])
        consume(item, now)


def attend_kernel(
    slots, own, q_heads, kv, ctx_low, ctx, lse, shift, total, q_ext, *, half, heads
):
    deep = heads * half
    lane = lanes_of(deep)

    def one_half(part, _):
        rank_own = own[part]
        mask = causal(half, heads, False)
        here = stretch(slots[rank_own], half)
        scores = jnp.where(mask, mm_nt(q_heads[part], kv[here, :LANES]), BELOW_FLOOR)
        first = jnp.max(scores, axis=1, keepdims=True).astype(BF16).astype(F32)
        shift[...] = first
        q_ext[...] = jnp.where(lane == heads * HEAD_DIM, -first, q_heads[part].astype(F32)).astype(
            BF16
        )
        total[...] = mm(jnp.exp(scores - first).astype(BF16), ones_before(kv[here, 128:]))

        def tiles(ranks):
            at = [stretch(slots[r], half) for r in ranks]
            added = [total[...]]

            def produce(a):
                return mm_nt(q_ext[...], ones_after(kv[a, :LANES], heads * HEAD_DIM))

            def consume(a, above):
                added[0] += mm(jnp.exp(above).astype(BF16), ones_before(kv[a, 128:]))

            one_ahead(at, produce, consume)
            total[...] = added[0]

        in_groups(0, rank_own, tiles)

        @pl.when(jnp.logical_not(jnp.max(total[:, :EXTRA]) < LARGEST_SUM))
        def _():
            shift[...] = jnp.full_like(shift, FLOOR)
            total[...] = jnp.zeros_like(total)

            def again(rank, _):
                a = stretch(slots[rank], half)
                allowed = jnp.logical_or(mask, rank < rank_own)
                scores = jnp.where(allowed, mm_nt(q_heads[part], kv[a, :LANES]), BELOW_FLOOR)
                new = jnp.maximum(shift[...], jnp.max(scores, axis=1, keepdims=True))
                total[...] = total[...] * jnp.exp(shift[...] - new) + mm(
                    jnp.exp(scores - new).astype(BF16), ones_before(kv[a, 128:])
                )
                shift[...] = new
                return 0

            lax.fori_loop(0, rank_own + 1, again, 0)

        row_sum = total[:, :1]
        lse[part] = shift[...] + jnp.log(row_sum)
        done = merged_heads(total[...] / row_sum, half, heads, EXTRA)
        rows = stretch(part, half)
        ctx[rows, :] = done
        ctx_low[:, rows] = done.T[EXTRA:, :].astype(BF16)
        return 0

    lax.fori_loop(0, 2, one_half, 0)


def query_grad_kernel(
    slots, own, q_heads, packed, kv, d_query, total, q_ext, d_ext, *, half, heads
):
    lane = lanes_of(half)

    def one_half(part, _):
        rank_own = own[part]
        total[...] = jnp.zeros_like(total)
        grads = packed[stretch(part, half), :].astype(F32)
        for h in range(heads):
            deep = slice(h * half, (h + 1) * half)
            first = EXTRA + h * HEAD_DIM
            q_new = q_heads[part, deep, :].astype(F32)
            d_new = jnp.where(
                jnp.logical_and(lane >= first, lane < first + HEAD_DIM), grads, 0.0
            )
            for i in range(3):
                at = 3 * h + i
                q_new = jnp.where(lane == heads * HEAD_DIM + i, grads[:, at : at + 1], q_new)
                at += 3 * heads
                d_new = jnp.where(lane == i, grads[:, at : at + 1], d_new)
            q_ext[deep, :] = q_new.astype(BF16)
            d_ext[deep, :] = d_new.astype(BF16)

        def tiles(ranks, mask=None):
            at = [stretch(slots[r], half) for r in ranks]
            added = [total[...]]

            def produce(a):
                return (
                    mm_nt(q_ext[...], ones_after(kv[a, :LANES], heads * HEAD_DIM)),
                    mm_nt(d_ext[...], ones_before(kv[a, 128:])),
                )

            def consume(a, ready):
                probs = jnp.exp(ready[0])
                if mask is not None:
                    probs = jnp.where(mask, probs, 0.0)
                added[0] += mm((probs * ready[1]).astype(BF16), kv[a, :LANES])

            one_ahead(at, produce, consume)
            total[...] = added[0]

        in_groups(0, rank_own, tiles)
        tiles([rank_own], causal(half, heads, False))
        done = merged_heads(total[...], half, heads, 0)
        d_query[stretch(part, half), :] = (done * (1.0 / math.sqrt(HEAD_DIM))).astype(BF16)
        return 0

    lax.fori_loop(0, 2, one_half, 0)


def key_grad_kernel(
    slots, own, k_heads, v_heads, q_all, p_all, d_key, d_value, k_sum, v_sum, *, half, heads
):
    count = slots.shape[0]
    lane = lanes_of(half)

    def one_half(part, _):
        rank_own = own[part]
        k_sum[...] = jnp.zeros_like(k_sum)
        v_sum[...] = jnp.zeros_like(v_sum)

        def tiles(ranks, mask=None):
            at = [stretch(slots[r], half) for r in ranks]
            added = [k_sum[...], v_sum[...]]

            def produce(a):
                return (
                    mm_nt(k_heads[part], jnp.where(lane < EXTRA, p_all[a, :], q_all[a, :])),
                    mm_nt(v_heads[part], p_all[a, :]),
                )

            def consume(a, ready):
                probs = jnp.exp(ready[0])
                if mask is not None:
                    probs = jnp.where(mask, probs, 0.0)
                added[1] += mm(probs.astype(BF16), p_all[a, :])
                added[0] += mm((probs * ready[1]).astype(BF16), q_all[a, :])

            one_ahead(at, produce, consume)
            k_sum[...], v_sum[...] = added

        tiles([rank_own], causal(half, heads, True))
        in_groups(rank_own + 1, count - 1 - rank_own, tiles)
        rows = stretch(part, half)
        d_key[rows, :] = merged_heads(k_sum[...], half, heads, EXTRA).astype(BF16)
        d_value[rows, :] = merged_heads(v_sum[...], half, heads, EXTRA)[:, EXTRA:].astype(BF16)
        return 0

    lax.fori_loop(0, 2, one_half, 0)


def prepare_kernel(dc, w_out, ctx, lse, packed, *, half, heads):
    lane = lanes_of(half)
    d_ctx = mm_nt(dc[...], w_out[...]).astype(BF16).astype(F32)
    for part in range(2):
        rows = slice(part * half, (part + 1) * half)
        grads = d_ctx[rows, :]
        terms = grads * ctx[rows, :]
        for h in range(heads):
            first = EXTRA + h * HEAD_DIM
            here = jnp.logical_and(lane >= first, lane < first + HEAD_DIM)
            delta = jnp.sum(jnp.where(here, terms, 0.0), axis=1, keepdims=True)
            minus_lse = three(-lse[part, h * half : (h + 1) * half, :])
            minus_delta = three(-delta)
            for i in range(3):
                grads = jnp.where(lane == 3 * h + i, minus_lse[i], grads)
                grads = jnp.where(lane == 3 * (heads + h) + i, minus_delta[i], grads)
        packed[rows, :] = grads.astype(BF16)


def project_kernel(me, x, weights, h1, n1, kv, q, vec, bias, *, wide, ways, pair, part):
    count = ways * pair
    each = weights.shape[0] // wide
    for w in range(wide):
        block = weights[w * each : w * each + 8, 512:].astype(F32)
        vec[:, w * count : (w + 1) * count] = block[:, 64 : 64 + count]
    width = x.shape[1]
    bias[...] = jnp.zeros_like(bias)
    for u in range(ways):

        @pl.when(me[0] == u)
        def _():
            bias[0:1, :part] = vec[2:3, u * part : (u + 1) * part]
            bias[0:1, 2 * part : 3 * part] = vec[2:3, width + u * part : width + (u + 1) * part]

    normed, _ = normalized(x[...].astype(F32))
    n1[...] = normed
    h1_low = (normed * vec[0:1, :width] + vec[1:2, :width]).astype(BF16)
    h1[...] = h1_low
    proj = (mm(h1_low, weights[...]) + bias[0:1, :]).astype(BF16)
    q[...] = proj[:, :part] * jnp.asarray(1.0 / math.sqrt(HEAD_DIM), BF16)
    kv[...] = proj[:, part : 3 * part]


def project(me, both, weights, part, wide, ways, pair):
    rows = both.shape[0]
    width = both.shape[1] // 2
    outs = [
        ((rows, width), BF16),
        ((rows, width), F32),
        ((rows, 2 * part), BF16),
        ((rows, part), BF16),
        ((8, wide * ways * pair), F32),
    ]
    return pl.pallas_call(
        functools.partial(project_kernel, wide=wide, ways=ways, pair=pair, part=part),
        out_shape=tuple(jax.ShapeDtypeStruct(s, t) for s, t in outs),
        grid_spec=pltpu.PrefetchScalarGridSpec(
            num_scalar_prefetch=1,
            grid=(1,),
            in_specs=[pl.BlockSpec((rows, width), lambda i, *_: (0, 0)), whole(weights.shape)],
            out_specs=[whole(s) for s, _ in outs],
            scratch_shapes=[pltpu.VMEM((8, weights.shape[1]), F32)],
        ),
        compiler_params=params(),
        cost_estimate=pl.CostEstimate(
            flops=2 * rows * weights.size, bytes_accessed=8 * rows * width, transcendentals=rows
        ),
        name="project",
    )(me, both, weights)


def finish_kernel(
    core, me, d_query, d_key, d_value, h1, n1, weights, small, terms, kept, sent, d_proj, g, rows_of
):
    chips, deep, _ = kept.shape
    lane = lax.broadcasted_iota(jnp.int32, (d_query.shape[0], 128), 1)
    part = d_value.shape[1]
    d_proj[:, :128] = d_query[:, :128]
    d_proj[:, 128:256] = jnp.where(lane < EXTRA, d_query[:, 128:], d_key[:, :128])
    d_proj[:, 256:384] = d_key[:, 128:]
    d_proj[:, 512:] = jnp.zeros_like(d_proj[:, 512:])
    d_proj[:, 384 : 384 + part] = d_value[...]
    dh1 = mm_nt(d_proj[...], weights[...])
    terms[...] = dh1.astype(BF16)
    g[...] = mm_tn(h1[...], d_proj[...])
    gain_row = jnp.sum(dh1 * n1[...], axis=0, keepdims=True)
    shift_row = jnp.sum(dh1, axis=0, keepdims=True)
    sums = jnp.sum(d_proj[...].astype(F32), axis=0, keepdims=True)
    rows_of[...] = small[...]
    count = 2 * chips
    each = h1.shape[1] // count
    wide = 2 * each
    for w in range(count // 2):
        rows_of[w, 0:1, :wide] = gain_row[:, w * wide : (w + 1) * wide]
        rows_of[w, 1:2, :wide] = shift_row[:, w * wide : (w + 1) * wide]
    many = part // wide
    for i in range(many):
        at = many * me[0] + i
        rows_of[at, 2:3, :wide] = sums[:, i * wide : (i + 1) * wide]
        rows_of[count // 2 + at, 2:3, :wide] = sums[:, 384 + i * wide : 384 + (i + 1) * wide]

    def put(target, which):
        target[:, each:, 128:] = jnp.zeros((chips, deep - each, target.shape[2] - 128), target.dtype)
        for c in range(chips):
            w = 2 * c + which
            target[c, :each, :] = g[w * each : (w + 1) * each, :].astype(target.dtype)
            target[c, each:, :128] = rows_of[w].astype(target.dtype)

    for which in range(2):

        @pl.when(core[0] == which)
        def _():
            put(kept, which)
            put(sent, 1 - which)


def finish(core, me, d_query, d_key, d_value, h1, n1, weights, small):
    rows, width = h1.shape
    count = small.shape[0]
    shape = (count // 2, width // count + 8, weights.shape[1])
    return call(
        finish_kernel, "finish", (core, me), (d_query, d_key, d_value, h1, n1, weights, small),
        [((rows, width), BF16), (shape, F32), (shape, BF16)],
        [((rows, weights.shape[1]), BF16), ((width, weights.shape[1]), F32), (small.shape, F32)],
        pl.CostEstimate(flops=4 * weights.size * rows, bytes_accessed=6 * weights.size, transcendentals=0),
    )


def whole(shape):
    return pl.BlockSpec(shape, lambda i, *_: (0,) * len(shape))


def params():
    return pltpu.CompilerParams(
        dimension_semantics=("arbitrary",), vmem_limit_bytes=VMEM_LIMIT
    )


def cost(rows, keys, heads, products):
    area = rows * keys * heads
    return pl.CostEstimate(
        flops=2 * area * 256 * products, bytes_accessed=keys * 768, transcendentals=area
    )


def call(kernel, name, scalars, arrays, outs, scratch, estimate, **static):
    return pl.pallas_call(
        functools.partial(kernel, **static),
        out_shape=tuple(jax.ShapeDtypeStruct(s, t) for s, t in outs),
        grid_spec=pltpu.PrefetchScalarGridSpec(
            num_scalar_prefetch=len(scalars),
            grid=(1,),
            in_specs=[whole(a.shape) for a in arrays],
            out_specs=[whole(s) for s, _ in outs],
            scratch_shapes=[pltpu.VMEM(s, t) for s, t in scratch],
        ),
        compiler_params=params(),
        cost_estimate=estimate,
        name=name,
    )(*scalars, *arrays)


def attend(slots, own, q_heads, kv, heads):
    _, deep, _ = q_heads.shape
    half = deep // heads
    width = heads * HEAD_DIM
    return call(
        attend_kernel, "attend", (slots, own), (q_heads, kv),
        [((width, 2 * half), BF16), ((2 * half, LANES), F32), ((2, deep, 1), F32)],
        [((deep, 1), F32), ((deep, LANES), F32), ((deep, LANES), BF16)],
        cost(2 * half, kv.shape[0], heads, 2), half=half, heads=heads,
    )


def prepare(dc, w_out, ctx, lse, heads):
    half = dc.shape[0] // 2
    return call(
        prepare_kernel, "prepare", (), (dc, w_out, ctx, lse),
        [((2 * half, LANES), BF16)], [],
        pl.CostEstimate(flops=2 * dc.size * LANES, bytes_accessed=8 * ctx.size, transcendentals=0),
        half=half, heads=heads,
    )[0]


def query_grad(slots, own, q_heads, packed, kv, heads):
    _, deep, _ = q_heads.shape
    half = deep // heads
    return call(
        query_grad_kernel, "query_grad", (slots, own), (q_heads, packed, kv),
        [((2 * half, LANES), BF16)],
        [((deep, LANES), F32), ((deep, LANES), BF16), ((deep, LANES), BF16)],
        cost(2 * half, kv.shape[0], heads, 3), half=half, heads=heads,
    )[0]


def key_grad(slots, own, k_heads, v_heads, q_all, p_all, heads):
    _, deep, _ = k_heads.shape
    half = deep // heads
    return call(
        key_grad_kernel, "key_grad", (slots, own), (k_heads, v_heads, q_all, p_all),
        [((2 * half, LANES), BF16), ((2 * half, heads * HEAD_DIM), BF16)], [((deep, LANES), F32)] * 2,
        cost(2 * half, q_all.shape[0], heads, 4), half=half, heads=heads,
    )


def feed_forward_kernel(
    me, x, ctx, df, vectors, w_up, w_out, w_down, x2_own, h2, act, du, dh2, down
):
    total = x[...].astype(F32) + vectors[2:3, :] + mm_tn(ctx[...], w_out[...])

    own_rows = x2_own.shape[0]
    each = total.shape[0] // own_rows
    for i in range(each):

        @pl.when(pl.program_id(0) * each + i == me[0])
        def _():
            x2_own[...] = total[i * own_rows : (i + 1) * own_rows, :]

    normed, _ = normalized(total)
    h2_low = (normed * vectors[0:1, :] + vectors[1:2, :]).astype(BF16)
    h2[...] = h2_low
    up = mm(h2_low, w_up[...]) + vectors[3:4, :]
    bend = math.sqrt(2.0 / math.pi)
    square = up * up
    turn = jnp.tanh(bend * (up + 0.044715 * square * up))
    half = 0.5 * (1.0 + turn)
    act_low = (up * half).astype(BF16)
    act[...] = act_low
    down[...] = mm(act_low, w_down[...]).astype(BF16)
    slope = half + 0.5 * up * (1.0 - turn * turn) * (bend * (1.0 + 3 * 0.044715 * square))
    du_low = (slope * mm_nt(df[...], w_down[...])).astype(BF16)
    du[...] = du_low
    dh2[...] = mm_nt(du_low, w_up[...]).astype(BF16)


def feed_forward(me, both, ctx, vectors, weights, ways):
    rows = both.shape[0]
    width = both.shape[1] // 2
    step = rows // 2

    def along(c):
        return pl.BlockSpec((step, width), lambda i, *_: (i, c))

    def third(c):
        return pl.BlockSpec((weights.shape[0], width), lambda i, *_: (0, c))

    flat = jax.ShapeDtypeStruct((rows, width), BF16)
    return pl.pallas_call(
        feed_forward_kernel,
        out_shape=(jax.ShapeDtypeStruct((rows // ways, width), F32), flat, flat, flat, flat, flat),
        grid_spec=pltpu.PrefetchScalarGridSpec(
            num_scalar_prefetch=1,
            grid=(2,),
            in_specs=[
                along(0),
                pl.BlockSpec((width, step), lambda i, *_: (0, i)),
                along(1),
                whole(vectors.shape),
                third(0),
                third(1),
                third(2),
            ],
            out_specs=[whole((rows // ways, width))] + [along(0)] * 5,
        ),
        compiler_params=params(),
        cost_estimate=pl.CostEstimate(
            flops=10 * rows * width * width, bytes_accessed=6 * width * width, transcendentals=rows * width
        ),
        name="feed_forward",
    )(me, both, ctx, both, vectors, weights, weights, weights)


def weight_grads_kernel(core, h2, du, act, df, ctx, dc, kept, sent, g_up, g_down, g_out):
    chips, rows, width = kept.shape
    each = h2.shape[1] // (2 * chips)
    few = ctx.shape[0] // (2 * chips)
    chunk = h2.shape[1] // 2
    for i in range(2):
        cols = slice(i * chunk, (i + 1) * chunk)
        g_up[cols, :] = mm_tn(h2[:, cols], du[...])
        g_down[cols, :] = mm_tn(act[:, cols], df[...])
    g_out[...] = mm(ctx[...], dc[...])

    def put(target, which):
        kind = target.dtype
        target[:, 2 * each :, :] = jnp.zeros((chips, rows - 2 * each, width), kind)
        for c in range(chips):
            w = 2 * c + which
            target[c, :each, :] = g_up[w * each : (w + 1) * each, :].astype(kind)
            target[c, each : 2 * each, :] = g_down[w * each : (w + 1) * each, :].astype(kind)
            target[c, 2 * each : 2 * each + few, :] = g_out[w * few : (w + 1) * few, :].astype(kind)

    for which in range(2):

        @pl.when(core[0] == which)
        def _():
            put(kept, which)
            put(sent, 1 - which)


def weight_grads(core, h2, du, act, both, ctx, dc, owners):
    count, width = du.shape
    units = h2.shape[1]
    shape = (owners // 2, 2 * units // owners + 8, width)
    return pl.pallas_call(
        weight_grads_kernel,
        out_shape=(jax.ShapeDtypeStruct(shape, F32), jax.ShapeDtypeStruct(shape, BF16)),
        grid_spec=pltpu.PrefetchScalarGridSpec(
            num_scalar_prefetch=1,
            grid=(1,),
            in_specs=[
                whole(h2.shape),
                whole(du.shape),
                whole(act.shape),
                pl.BlockSpec((count, width), lambda i, *_: (0, 1)),
                whole(ctx.shape),
                whole(dc.shape),
            ],
            out_specs=[whole(shape)] * 2,
            scratch_shapes=[
                pltpu.VMEM((units, width), F32),
                pltpu.VMEM((units, width), F32),
                pltpu.VMEM((ctx.shape[0], width), F32),
            ],
        ),
        compiler_params=params(),
        cost_estimate=pl.CostEstimate(
            flops=4 * h2.size * width, bytes_accessed=6 * units * width, transcendentals=0
        ),
        name="weight_grads",
    )(core, h2, du, act, both, ctx, dc)


def normalized(values):
    mean = jnp.mean(values, axis=-1, keepdims=True)
    centered = values - mean
    spread = jnp.mean(centered * centered, axis=-1, keepdims=True)
    scale = lax.rsqrt(spread + NORM_EPS)
    return centered * scale, scale


def norm_back(grad, gain, normed, scale):
    e = grad * gain
    mean_e = jnp.mean(e, axis=-1, keepdims=True)
    mean_en = jnp.mean(e * normed, axis=-1, keepdims=True)
    return scale * (e - mean_e - normed * mean_en)


def gelu_tanh(values):
    return jax.nn.gelu(values, approximate=True)


def head_lanes(x, heads, first, ones_at=None):
    rows, width = x.shape
    wide = jnp.pad(x, ((0, 0), (first, LANES - width - first))).reshape(2, 1, rows // 2, LANES)
    lane = lax.broadcasted_iota(jnp.int32, (1, heads, 1, LANES), 3)
    head = lax.broadcasted_iota(jnp.int32, (1, heads, 1, LANES), 1)
    start = first + head * HEAD_DIM
    here = jnp.logical_and(lane >= start, lane < start + HEAD_DIM)
    out = jnp.where(here, wide, jnp.zeros((), x.dtype))
    if ones_at is not None:
        at = ones_at + 3 * head
        out = jnp.where(jnp.logical_and(lane >= at, lane < at + 3), jnp.ones((), x.dtype), out)
    return out.reshape(2, heads * rows // 2, LANES)


def to_all(x, axis="ulysses"):
    ways = lax.axis_size(axis)
    sent = jnp.broadcast_to(x[None], (ways,) + x.shape)
    return lax.all_to_all(sent, axis, split_axis=0, concat_axis=0, tiled=True)


def summed_at_owner(x, axis="ulysses"):
    ways = lax.axis_size(axis)
    sent = x.astype(BF16).reshape(ways, -1, x.shape[1])
    got = lax.all_to_all(sent, axis, split_axis=0, concat_axis=0, tiled=True)
    return jnp.sum(got.astype(F32), axis=0)


def other_core(x):
    return lax.ppermute(x, "core", [(0, 1), (1, 0)])


def reduced(x, axis):
    ways = lax.axis_size(axis)
    me = lax.axis_index(axis)

    def rows_of(k):
        return lax.dynamic_index_in_dim(x, lax.rem(me + k, ways), axis=0, keepdims=False)

    got = [
        lax.ppermute(rows_of(k).astype(BF16), axis, [(i, (i + k) % ways) for i in range(ways)])
        for k in range(1, ways)
    ]
    total = rows_of(0).astype(F32)
    for g in got:
        total += g.astype(F32)
    return total


def on_device(
    tokens,
    stretch_order,
    ln_gain,
    ln_bias,
    w_qkv,
    qv_bias,
    w_out,
    out_bias,
    w_up,
    up_bias,
    w_down,
    down_bias,
    cotangent,
):
    own_rows, width = tokens.shape
    ways = lax.axis_size("ulysses")
    wide = lax.axis_size(WIDE)
    me = lax.axis_index("ulysses")
    rows = own_rows * ways
    heads = HEADS // ways
    part = width // ways
    held = w_qkv.shape[1]
    ff_held = w_down.shape[1]
    ff_part = ff_held * wide
    pair = 2 * held

    order = stretch_order[0]
    own = lax.dynamic_slice(order, (2 * lax.axis_index(BLK),), (2,))
    count = order.shape[0]
    index = jnp.arange(count, dtype=jnp.int32)
    slots = jnp.sum(jnp.where(order[None, :] == index[:, None], index[None, :], 0), axis=1)

    small = jnp.concatenate(
        [
            ln_gain,
            ln_bias,
            qv_bias,
            jnp.concatenate([out_bias, down_bias], axis=1),
            up_bias.reshape(2, pair),
        ],
        axis=0,
    )
    qkv_slices = w_qkv[0].reshape(held, 3, ways, part).transpose(2, 0, 1, 3).reshape(ways, held, 3 * part)
    sent = jnp.concatenate(
        [
            qkv_slices,
            jnp.broadcast_to(small[None], (ways,) + small.shape),
            jnp.zeros((ways, held, 64 - pair), BF16),
        ],
        axis=2,
    )
    sent, tokens_late, cotangent_late = lax.optimization_barrier((sent, tokens, cotangent))
    got = lax.all_to_all(sent, "ulysses", split_axis=0, concat_axis=0, tiled=True)
    df_own = cotangent_late.astype(BF16)
    both = lax.all_gather(
        jnp.concatenate([tokens_late, df_own], axis=1), "ulysses", axis=0, tiled=True
    )
    matrix = got[:, :held, : 3 * part].reshape(ways * held, 3 * part)
    vector = got[:, :held, 3 * part : 3 * part + pair].transpose(1, 0, 2).reshape(held, ways * pair)
    vector = jnp.pad(vector, ((0, (ways - 1) * held), (0, 64 - ways * pair)))
    piece = jnp.concatenate([matrix, vector], axis=1)
    filled = lax.all_gather(piece, WIDE, axis=0, tiled=True)
    h1, n1, kv, q_scaled, vec = project(me[None], both, filled, part, wide, ways, pair)
    gains, shifts = vec[0], vec[1]
    halves = vec[3].reshape(wide * ways, 2, held)
    out_bias_all = halves[:, 0].reshape(-1)
    down_bias_all = halves[:, 1].reshape(-1)
    up_bias_u = lax.dynamic_index_in_dim(
        vec[4:6].reshape(2, wide, ways, pair), me, axis=2, keepdims=False
    )
    up_bias_u = up_bias_u.transpose(1, 0, 2).reshape(-1)
    kv_all = lax.all_gather(kv, BLK, axis=0, tiled=True)

    up_late, out_late, kv = lax.optimization_barrier((w_up[0], w_out[0], kv))
    up_slices = up_late.reshape(held, wide, ways, ff_held).transpose(2, 0, 1, 3).reshape(ways, held, ff_part)
    sent = jnp.concatenate([up_slices, jnp.broadcast_to(out_late[None], (ways, held, width))], axis=2)
    got = lax.all_to_all(sent, "ulysses", split_axis=0, concat_axis=0, tiled=True)
    ffn = jnp.concatenate([got.reshape(ways * held, ff_part + width), w_down[0]], axis=1)
    q_heads = head_lanes(q_scaled, heads, 0)
    k_heads = head_lanes(kv[:, :part], heads, EXTRA, 0)
    v_heads = head_lanes(kv[:, part:], heads, EXTRA, 3 * heads)
    q_wide = jnp.pad(q_scaled, ((0, 0), (EXTRA, 0)))
    gain_two = gains[width:]
    vectors = jnp.stack(
        [gain_two, shifts[width:], out_bias_all, up_bias_u] + [jnp.zeros((width,), F32)] * 4
    )
    (ffn, kv_all, slots, own, q_heads, k_heads, v_heads, q_wide, vectors, n1) = (
        lax.optimization_barrier(
            (ffn, kv_all, slots, own, q_heads, k_heads, v_heads, q_wide, vectors, n1)
        )
    )
    ffn_all = lax.all_gather(ffn, WIDE, axis=0, tiled=True)

    ctx_low, ctx, lse = attend(slots, own, q_heads, kv_all, heads)
    ctx_all = to_all(ctx_low).reshape(width, rows)
    q_wide, ctx_all = lax.optimization_barrier((q_wide, ctx_all))
    q_all = lax.all_gather(q_wide, BLK, axis=0, tiled=True)
    x2_own, h2, act, du, dh2, down = feed_forward(
        me[None], both, ctx_all, vectors, ffn_all, ways
    )
    dh2 = summed_at_owner(dh2)
    ctx_rows = lax.dynamic_index_in_dim(
        ctx_all.reshape(wide, ways, held, rows), me, axis=1, keepdims=False
    ).reshape(part, rows)
    w_out_u = lax.dynamic_slice(ffn_all, (me * part, width), (part, width))
    g_up_bias = jnp.sum(du.astype(F32), axis=0)
    g_down_bias = jnp.sum(df_own.astype(F32), axis=0)

    n2_own, r2_own = normalized(x2_own)
    dx2 = cotangent + norm_back(dh2, gain_two, n2_own, r2_own)
    g_gain_two = jnp.sum(dh2 * n2_own, axis=0)
    g_shift_two = jnp.sum(dh2, axis=0)
    dc_own = dx2.astype(BF16)
    g_out_bias = jnp.sum(dc_own.astype(F32), axis=0)
    owners = wide * ways
    blank = jnp.zeros((width,), F32)
    small_grads = jnp.stack(
        [
            jnp.concatenate([blank, g_gain_two]).reshape(wide, -1),
            jnp.concatenate([blank, g_shift_two]).reshape(wide, -1),
            jnp.zeros((wide, ways * pair), F32),
            jnp.concatenate(
                [g_out_bias.reshape(owners, held), g_down_bias.reshape(owners, held)], axis=1
            ).reshape(wide, -1),
        ],
        axis=1,
    )
    g_up_full = jnp.zeros((wide, 2, ways, pair), F32)
    g_up_full = lax.dynamic_update_slice(
        g_up_full, g_up_bias.reshape(wide, 2, 1, pair), (0, 0, me, 0)
    )
    small_grads = jnp.concatenate([small_grads, g_up_full.reshape(wide, 2, ways * pair)], axis=1)
    small_grads = jnp.pad(small_grads, ((0, 0), (0, 2), (0, 128 - ways * pair)))
    dc = to_all(dc_own).reshape(rows, width)
    dc, q_all, small_grads, ctx_rows = lax.optimization_barrier((dc, q_all, small_grads, ctx_rows))
    w_out_u = lax.dynamic_slice(ffn_all, (me * part, width), (part, width))

    w_out_wide = jnp.pad(w_out_u, ((EXTRA, 0), (0, 0)))
    packed = prepare(dc, w_out_wide, ctx, lse, heads)
    packed_all = lax.all_gather(packed, BLK, axis=0, tiled=True)
    core = lax.axis_index("core")
    early, early_sent = weight_grads(core[None], h2, du, act, both, ctx_rows, dc, wide)
    early = (early + other_core(early_sent).astype(F32)).astype(BF16)
    early, q_heads = lax.optimization_barrier((early, q_heads))
    d_query = query_grad(slots, own, q_heads, packed, kv_all, heads)
    early, packed_all, d_query = lax.optimization_barrier((early, packed_all, d_query))
    early = lax.all_to_all(early, CHIPS, split_axis=0, concat_axis=0, tiled=True)
    d_key, d_value = key_grad(slots, own, k_heads, v_heads, q_all, packed_all, heads)
    early, d_value = lax.optimization_barrier((early, d_value))
    early = jnp.sum(early.astype(F32), axis=0)
    terms, late, late_sent = finish(
        core[None], me[None], d_query, d_key, d_value, h1, n1, filled, small_grads
    )
    late = (late + other_core(late_sent).astype(F32)).astype(BF16)
    terms, late = lax.optimization_barrier((terms, late))
    late = lax.all_to_all(late, CHIPS, split_axis=0, concat_axis=0, tiled=True)
    late = jnp.sum(late.astype(F32), axis=0)
    pair_sums = reduced(
        jnp.concatenate([terms, down], axis=1).reshape(ways, own_rows, 2 * width), "ulysses"
    )
    dh1 = pair_sums[:, :width]
    result = pair_sums[:, width:] + x2_own + down_bias_all
    n1_own, r1_own = normalized(tokens.astype(F32))
    d_tokens = dx2 + norm_back(dh1, gains[:width], n1_own, r1_own)

    small_rows = late[ways * held : ways * held + 6, : ways * pair].reshape(6, ways, pair)
    last = jnp.concatenate(
        [
            late[: ways * held, : 3 * part].reshape(ways, held, 3 * part),
            jnp.pad(small_rows.transpose(1, 0, 2), ((0, 0), (0, 0), (0, 64 - pair))),
            early[:ff_held].reshape(ways, held, -1),
        ],
        axis=2,
    )
    last = lax.all_to_all(last, "ulysses", split_axis=0, concat_axis=0, tiled=True)
    o_w_qkv = last[:, :, : 3 * part].reshape(ways, held, 3, part).transpose(1, 2, 0, 3)
    o_small = jnp.sum(last[:, :, 3 * part : 3 * part + pair], axis=0)
    o_w_up = last[:, :, 3 * part + 64 :].reshape(ways, held, wide, ff_held).transpose(1, 2, 0, 3)
    return (
        result,
        d_tokens,
        o_small[0:1],
        o_small[1:2],
        o_w_qkv.reshape(1, held, 3 * width),
        o_small[2:3],
        early[None, 2 * ff_held : 2 * ff_held + held],
        o_small[3:4, :held],
        o_w_up.reshape(1, held, -1),
        o_small[4:6].reshape(1, ff_held),
        early[None, ff_held : 2 * ff_held],
        o_small[3:4, held:],
    )


def solution(mesh):
    chips_z = mesh.shape["blk"] // 4
    parts = Mesh(
        mesh.devices.reshape(mesh.shape["batch"], 2, chips_z, 2, mesh.shape["ulysses"]), ALL
    )
    rows = P(ALL, None)
    flat = P(None, ALL)
    deep = P(None, ALL, None)
    return jax.shard_map(
        on_device,
        mesh=parts,
        in_specs=(
            rows, P("batch", None), flat, flat, deep, flat, deep, flat, deep, flat, deep, flat, rows,
        ),
        out_specs=(rows, rows, flat, flat, deep, flat, deep, flat, deep, flat, deep, flat),
        check_vma=False,
    )
```
